128 devices in a mesh: fsdp: 4 (over z_hi, core), ctx: 8 (over x, z_lo), tp: 4 (over y).
Axes of the slice: x: 4, y: 4, z: 4 (z_hi: 2, z_lo: 2; z = z_hi * 2 + z_lo), core: 2. Of those that a mesh axis runs over, the one named last changes fastest.
Arguments:
- tokens: bfloat16 [4, 1024, 1024], P('fsdp', 'ctx'), may hold values from -6 to 6
- cotangent: bfloat16 [4, 1024, 1024], P('fsdp', 'ctx'), may hold values from -6 to 6
- w_qkv: bfloat16 [2, 3, 1024, 1024], P(None, None, ('fsdp', 'ctx'), 'tp'), may hold values from -0.1875 to 0.1875
- w_attn: bfloat16 [2, 1024, 1024], P(None, 'tp', ('fsdp', 'ctx')), may hold values from -0.75 to 0.75
- w_in: bfloat16 [2, 1024, 4096], P(None, ('fsdp', 'ctx'), 'tp'), may hold values from -0.1875 to 0.1875
- w_out: bfloat16 [2, 4096, 1024], P(None, 'tp', ('fsdp', 'ctx')), may hold values from -0.09375 to 0.09375
- ln_gain: bfloat16 [2, 2, 1024], P(None, None, ('fsdp', 'ctx')), may hold values from 0.5 to 1.5
- ln_bias: bfloat16 [2, 2, 1024], P(None, None, ('fsdp', 'ctx')), may hold values from -1 to 1
- rel_emb: bfloat16 [512, 1024], P(('fsdp', 'ctx')), may hold values from -6 to 6
- rel_gain: bfloat16 [1024], P(('fsdp', 'ctx')), may hold values from 0.5 to 1.5
- rel_bias: bfloat16 [1024], P(('fsdp', 'ctx')), may hold values from -1 to 1
- doc_ids: int32 [4, 1024], P('fsdp', 'ctx'), may hold values from 0 to 3, as said below
- rel_bucket: int32 [2047], replicated, may hold values from 0 to 511, as said below
Outputs:
- out: bfloat16 [4, 1024, 1024], P('fsdp', 'ctx')
- grad_tokens: bfloat16 [4, 1024, 1024], P('fsdp', 'ctx')
- grad_qkv: float32 [2, 3, 1024, 1024], P(None, None, ('fsdp', 'ctx'), 'tp')
- grad_attn: float32 [2, 1024, 1024], P(None, 'tp', ('fsdp', 'ctx'))
- grad_in: float32 [2, 1024, 4096], P(None, ('fsdp', 'ctx'), 'tp')
- grad_out: float32 [2, 4096, 1024], P(None, 'tp', ('fsdp', 'ctx'))
- grad_gain: float32 [2, 2, 1024], P(None, None, ('fsdp', 'ctx'))
- grad_bias: float32 [2, 2, 1024], P(None, None, ('fsdp', 'ctx'))
- grad_rel: float32 [512, 1024], P(('fsdp', 'ctx'))
- grad_rel_gain: float32 [1024], P(('fsdp', 'ctx'))
- grad_rel_bias: float32 [1024], P(('fsdp', 'ctx'))
The draws below stay inside these ranges and needn't reach their ends.
Inputs may be any that keep to these rules, and one draw needn't show every extreme that they name: `doc_ids`: nondecreasing along each sequence, 0 at its first token and 3 at its last; in every sequence, document 1 covers at least positions 127 to 896. `rel_bucket`: entry o is the bucket of the offset o - (1023) from a key's position to a query's; nondecreasing in o, equal to 256 + o - (1023) where that offset lies within 128 of zero, 0 at the first entry and 511 at the last.
All inputs are finite; a program needn't handle non-finite values.
Results may differ from the reference program's by a relative error of at most 0.03.
Values may be sent and summed in bfloat16 or wider, within the bound.
No kernel may reach another device: no remote copies, remote signals or barrier semaphores. Data moves between devices by JAX's collectives and lax.ppermute only.
A program may use at most 192 MiB of HBM per device.

```python
import math
import jax
import jax.numpy as jnp
from jax import lax

D = 1024
HEADS = 16
HEAD_DIM = 64
FF = 4096
SPAN = 256
LEN = 1024
LAYERS = 2
SEQS = 1
BATCH = 4
LOCAL = 128


def bucket_side(key, total):
    remaining = LEN - 1 - SPAN // 2
    order = jax.random.permutation(key, remaining)
    marks = (order < total - SPAN // 2).astype(jnp.int32)
    steps = jnp.concatenate([jnp.ones((SPAN // 2,), jnp.int32), marks])
    return jnp.cumsum(steps).astype(jnp.int32)


def draw_rel_bucket(key, part):
    key = jax.random.fold_in(key, 5)
    upper_key, lower_key = jax.random.split(key)
    above = SPAN + bucket_side(upper_key, SPAN - 1)
    below = SPAN - bucket_side(lower_key, SPAN)
    return jnp.concatenate([below[::-1], jnp.full((1,), SPAN, jnp.int32), above]).astype(jnp.int32)


def draw_doc_ids(key, part):
    key = jax.random.fold_in(key, 9)
    free_key, early_key, late_key, pick_key = jax.random.split(key, 4)
    spread_cuts = jax.random.randint(free_key, (BATCH, 3), 1, LEN)
    early_cut = jax.random.randint(early_key, (BATCH, 1), 1, LOCAL)
    late_cuts = jax.random.randint(late_key, (BATCH, 2), LEN - LOCAL + 1, LEN)
    edge_cuts = jnp.concatenate([early_cut, late_cuts], axis=1)
    picked = jax.random.randint(pick_key, (BATCH // SEQS,), 0, SEQS)
    chosen = jnp.arange(BATCH) % SEQS == jnp.repeat(picked, SEQS)
    cuts = jnp.where(chosen[:, None], edge_cuts, spread_cuts)
    positions = jnp.arange(LEN)
    return jnp.sum((cuts[:, :, None] <= positions[None, None, :]).astype(jnp.int32), axis=1).astype(jnp.int32)


def strengthened(values, rng, source, target, parts, factor):
    owner, partner = [(jnp.arange(values.shape[position]) // (values.shape[position] // parts)).reshape([-1 if axis == position else 1 for axis in range(values.ndim)]) for position in (source, target)]
    chosen = jax.random.permutation(rng, parts)[partner]
    strong = (owner == chosen) | (owner == (partner + parts // 2) % parts)
    return jnp.where(strong, factor * values, values)


def steps_of(own_key, extent, cuts, smallest, top_value):
    level = 1.0
    for position, shards_of in cuts:
        draws = jax.random.uniform(jax.random.fold_in(jax.random.fold_in(own_key, 6), position), (shards_of,), jnp.float32, smallest / len(cuts), top_value / len(cuts))
        level = level * jnp.repeat(jnp.exp(draws), extent[position] // shards_of).reshape((-1,) + (1,) * (len(extent) - 1 - position))
    return level


def gaussian(stream_key, dims, deviation, bound, cuts=(), kind=jnp.bfloat16):
    gain = steps_of(stream_key, dims, cuts, -0.22, 0.18) if cuts else 1.0
    values = jax.random.normal(stream_key, dims, jnp.float32) * deviation * gain
    return jnp.minimum(jnp.maximum(values, -bound), bound).astype(kind)


def heavy_noise(rng, shape, width, bound, shards, heavy, held_as=jnp.bfloat16):
    values = width * jax.random.normal(rng, shape, jnp.float32)
    if shards:
        values = values * steps_of(rng, shape, shards, -0.22, 0.18)
    return jnp.clip(strengthened(values, jax.random.fold_in(rng, 3), *heavy), -bound, bound).astype(held_as)


def setup_inputs(seed: int = 0) -> dict:
    seeds = jax.random.split(jax.random.key(seed), 14)
    tokens = gaussian(seeds[0], (BATCH, LEN, D), 1.0, 6.0, ((0, 4), (1, 8)))
    cotangent = heavy_noise(seeds[1], (BATCH, LEN, D), 1.0, 6.0, ((0, 4), (1, 8)), (1, 2, 8, 2.0))
    w_qkv = gaussian(seeds[2], (LAYERS, 3, D, D), D ** -0.5, 0.1875, ((2, 32), (3, 4)))
    w_attn = gaussian(seeds[3], (LAYERS, D, D), (D // 16) ** -0.5, 0.75, ((1, 4), (2, 32)))
    w_in = gaussian(seeds[4], (LAYERS, D, FF), D ** -0.5, 0.1875, ((1, 32), (2, 4)))
    w_out = gaussian(seeds[5], (LAYERS, FF, D), FF ** -0.5, 0.09375, ((1, 4), (2, 32)))
    ln_gain = jnp.clip(1.0 + 0.1 * jax.random.normal(seeds[6], (LAYERS, 2, D), jnp.float32), 0.5, 1.5).astype(jnp.bfloat16)
    ln_bias = gaussian(seeds[7], (LAYERS, 2, D), 0.2, 1.0, ((2, 32),))
    rel_emb = gaussian(seeds[8], (2 * SPAN, D), 1.0, 6.0, ((0, 32),))
    rel_gain = jnp.clip(1.0 + 0.1 * jax.random.normal(seeds[9], (D,), jnp.float32), 0.5, 1.5).astype(jnp.bfloat16)
    rel_bias = gaussian(seeds[10], (D,), 0.2, 1.0, ((0, 32),))
    doc_ids = draw_doc_ids(jax.random.fold_in(seeds[13], 71), 0)
    rel_bucket = draw_rel_bucket(jax.random.fold_in(seeds[13], 71), 0)
    return {"tokens": tokens, "cotangent": cotangent, "w_qkv": w_qkv, "w_attn": w_attn, "w_in": w_in, "w_out": w_out, "ln_gain": ln_gain, "ln_bias": ln_bias, "rel_emb": rel_emb, "rel_gain": rel_gain, "rel_bias": rel_bias, "doc_ids": doc_ids, "rel_bucket": rel_bucket}


@jax.custom_vjp
def low(v):
    return lax.optimization_barrier(v.astype(jnp.bfloat16)).astype(jnp.float32)

@jax.custom_vjp
def reduced_backward(v):
    return v

def low_keep(v):
    return (low(v), None)

def low_pass(kept, grad):
    return (grad,)

def back_keep(v):
    return (v, None)

def back_low(kept, grad):
    return (low(grad),)
low.defvjp(low_keep, low_pass)
reduced_backward.defvjp(back_keep, back_low)
EPS = 1e-07
NEG = -1e+30
PRECISION_TOP = lax.Precision.HIGHEST

def normalize(values, gain_vec, offset):
    average = lax.optimization_barrier(jnp.mean(values, axis=-1, keepdims=True))
    centered = values - average
    spread = lax.optimization_barrier(jnp.mean(centered * centered, axis=-1, keepdims=True))
    return centered * lax.rsqrt(spread + EPS) * gain_vec + offset

def attend(query_rows, key_vecs, values, position_key_rows, pos_queries, to_index, documents):
    content = jnp.einsum('ihd,jhd->hij', query_rows, key_vecs, precision=PRECISION_TOP)
    toward_position = reduced_backward(jnp.einsum('qnu,fnu->nqf', query_rows, position_key_rows, precision=PRECISION_TOP))
    from_pos = jnp.einsum('jhd,bhd->hjb', key_vecs, pos_queries, precision=PRECISION_TOP)
    bucket_map = jnp.broadcast_to(to_index, (HEADS, LEN, LEN))
    to_terms = jnp.take_along_axis(toward_position, bucket_map, axis=2)
    from_terms = jnp.swapaxes(jnp.take_along_axis(from_pos, bucket_map, axis=2), 1, 2)
    score_matrix = reduced_backward(content + to_terms + from_terms)
    same_doc = documents[:, None] == documents[None, :]
    masked = jnp.where(same_doc[None], score_matrix, NEG)
    attention = jax.nn.softmax(masked, axis=-1)
    mixture = jnp.einsum('hij,jhd->ihd', low(attention), values, precision=PRECISION_TOP)
    return mixture.reshape(LEN, D)

def block(stream, weights, to_index, documents, rel_low):
    w_qkv, w_attn, w_in, w_out, gain_pair, shift_pair = weights
    score_scale = 1.0 / math.sqrt(3.0 * HEAD_DIM)
    stream_low = low(stream)
    query_rows = low(score_scale * reduced_backward(jnp.dot(stream_low, w_qkv[0], precision=PRECISION_TOP)))
    key_vecs = low(reduced_backward(jnp.dot(stream_low, w_qkv[1], precision=PRECISION_TOP)))
    value_vecs = low(reduced_backward(jnp.dot(stream_low, w_qkv[2], precision=PRECISION_TOP)))
    position_key_rows = low(jnp.dot(rel_low, w_qkv[1], precision=PRECISION_TOP)).reshape(2 * SPAN, HEADS, HEAD_DIM)
    pos_queries = low(score_scale * jnp.dot(rel_low, w_qkv[0], precision=PRECISION_TOP)).reshape(2 * SPAN, HEADS, HEAD_DIM)
    shaped = (query_rows.reshape(BATCH, LEN, HEADS, HEAD_DIM), key_vecs.reshape(BATCH, LEN, HEADS, HEAD_DIM), value_vecs.reshape(BATCH, LEN, HEADS, HEAD_DIM), documents)

    def one_seq(record):
        return attend(record[0], record[1], record[2], position_key_rows, pos_queries, to_index, record[3])
    mixture = low(reduced_backward(lax.map(jax.checkpoint(one_seq), shaped)))
    attended = reduced_backward(jnp.dot(mixture, w_attn, precision=PRECISION_TOP))
    hidden = normalize(stream + attended, gain_pair[0], shift_pair[0])
    hidden_low = low(hidden)
    inner_pre = reduced_backward(jnp.dot(hidden_low, w_in, precision=PRECISION_TOP))
    active = low(jax.nn.gelu(inner_pre, approximate=False))
    branch = reduced_backward(jnp.dot(active, w_out, precision=PRECISION_TOP))
    return normalize(hidden + branch, gain_pair[1], shift_pair[1])

def reference(tokens, cotangent, w_qkv, w_attn, w_in, w_out, ln_gain, ln_bias, rel_emb, rel_gain, rel_bias, doc_ids, rel_bucket):
    places = (lax.broadcasted_iota(jnp.int32, (LEN, LEN), 0) - lax.broadcasted_iota(jnp.int32, (LEN, LEN), 1) + (LEN - 1)).astype(jnp.int32)
    to_index = jnp.take(rel_bucket, places, axis=0).astype(jnp.int32)

    def forward(stream, w_qkv, w_attn, w_in, w_out, ln_gain, ln_bias, rel_emb, rel_gain, rel_bias):
        rel_low = low(normalize(rel_emb, rel_gain, rel_bias))
        for layer_id in range(LAYERS):
            weights = (w_qkv[layer_id], w_attn[layer_id], w_in[layer_id], w_out[layer_id], ln_gain[layer_id], ln_bias[layer_id])
            stream = block(stream, weights, to_index, doc_ids, rel_low)
        return stream
    floats = tuple((argument.astype(jnp.float32) for argument in (tokens, w_qkv, w_attn, w_in, w_out, ln_gain, ln_bias, rel_emb, rel_gain, rel_bias)))
    result, pullback = jax.vjp(forward, *floats)
    gradients = pullback(cotangent.astype(jnp.float32))
    return (result.astype(jnp.bfloat16), gradients[0].astype(jnp.bfloat16), gradients[1], gradients[2], gradients[3], gradients[4], gradients[5], gradients[6], gradients[7], gradients[8], gradients[9])
```

```python
import functools
import math

import jax
import jax.numpy as jnp
from jax import lax
from jax.experimental import pallas as pl
from jax.experimental.pallas import tpu as pltpu
from jax.sharding import Mesh
from jax.sharding import PartitionSpec as P

HEAD_DIM = 64
EPS = 1e-07
NEG = -1e30
BLOCK = 128
F32 = jnp.float32
BF16 = jnp.bfloat16
VMEM_LIMIT = 56 << 20
CTX = ("x", "zl")
ZED = ("zh", "zl")
PLANE = ("zh", "x", "zl")
OWNERS = ("zh", "core", "x", "zl")


def dot(a, b, ca, cb):
    return lax.dot_general(a, b, (((ca,), (cb,)), ((), ())), preferred_element_type=F32)


def params():
    return pltpu.CompilerParams(vmem_limit_bytes=VMEM_LIMIT)


def head_mask(shape, head):
    lane = lax.broadcasted_iota(jnp.int32, shape, len(shape) - 1)
    return (lane >= head * HEAD_DIM) & (lane < (head + 1) * HEAD_DIM)


def only_head(values, head):
    return jnp.where(head_mask(values.shape, head), values.astype(F32), 0.0).astype(BF16)


def forward_kernel(place_ref, q_ref, *refs):
    count = len(refs) - 10
    blocks = refs[:count]
    pk_ref, pq_ref, doc_i_ref, doc_j_ref = refs[count : count + 4]
    mix_ref, p_ref, k_ref, v_ref, kv_ref, sems = refs[count + 4 :]
    rows, width = q_ref.shape
    keys = k_ref.shape[0]
    win = pk_ref.shape[0]
    mine = place_ref[0]
    copies = []
    for shift, block in enumerate(blocks):
        owner = lax.rem(mine - shift + count, count)
        start = pl.multiple_of(owner * rows, rows)
        copies.append(
            pltpu.make_async_copy(block, kv_ref.at[pl.ds(start, rows), :], sems.at[shift])
        )
    for copy in copies:
        copy.start()
    for copy in copies:
        copy.wait()
    k_ref[...] = kv_ref[:, :width]
    v_ref[...] = kv_ref[:, width:]
    mix = jnp.zeros((rows, width), F32)
    for head in range(width // HEAD_DIM):
        q = only_head(q_ref[...], head)
        to = dot(q, pk_ref[...], 1, 1)
        to = pltpu.roll(to, win + 1 - rows, 1, stride=1, stride_axis=0)
        parts = []
        for start in range(0, keys, BLOCK):
            key_block = k_ref[start : start + BLOCK, :]
            first = win - 2 * BLOCK - start
            pq = only_head(pq_ref[first : first + 2 * BLOCK, :], head)
            off = dot(key_block, pq, 1, 1)
            off = pltpu.roll(off, BLOCK, 1, stride=1, stride_axis=0)
            s = dot(q, key_block, 1, 1) + to[:, start : start + BLOCK] + off[:, :BLOCK].T
            same = doc_i_ref[...] == doc_j_ref[:, start : start + BLOCK]
            parts.append(jnp.where(same, s, NEG))
        s = jnp.concatenate(parts, axis=1)
        e = jnp.exp(s - jnp.max(s, axis=1, keepdims=True))
        p = (e / jnp.sum(e, axis=1, keepdims=True)).astype(BF16)
        p_ref[head] = p
        mix = jnp.where(head_mask(mix.shape, head), dot(p, v_ref[...], 1, 0), mix)
    mix_ref[...] = mix.astype(BF16)


def attention_forward(place, q, blocks, pk_rev, pq_rev, doc_i, doc_j):
    rows, width = q.shape
    keys = rows * len(blocks)
    heads = width // HEAD_DIM
    vmem = pl.BlockSpec(memory_space=pltpu.VMEM)
    return pl.pallas_call(
        forward_kernel,
        in_specs=[pl.BlockSpec(memory_space=pltpu.SMEM), vmem]
        + [pl.BlockSpec(memory_space=pl.ANY)] * len(blocks)
        + [vmem] * 4,
        out_specs=(vmem,) * 4,
        out_shape=(
            jax.ShapeDtypeStruct((rows, width), BF16),
            jax.ShapeDtypeStruct((heads, rows, keys), BF16),
            jax.ShapeDtypeStruct((keys, width), BF16),
            jax.ShapeDtypeStruct((keys, width), BF16),
        ),
        scratch_shapes=[
            pltpu.VMEM((keys, 2 * width), BF16),
            pltpu.SemaphoreType.DMA((len(blocks),)),
        ],
        compiler_params=params(),
        name="attention_forward",
    )(place, q, *blocks, pk_rev, pq_rev, doc_i, doc_j)


def backward_kernel(
    scale,
    q_ref,
    k_ref,
    v_ref,
    pk_ref,
    pq_ref,
    p_ref,
    dm_ref,
    dq_ref,
    dkv_ref,
    dpk_ref,
    dpq_ref,
    ds_all,
    to_all,
    dk_pos,
    dm_all,
    q_all,
    qr_all,
    dpq_sum,
):
    rows, width = q_ref.shape
    keys = k_ref.shape[0]
    heads = width // HEAD_DIM
    win = pk_ref.shape[0]
    row = lax.broadcasted_iota(jnp.int32, (rows, rows), 0)
    col = lax.broadcasted_iota(jnp.int32, (rows, rows), 1)
    flip = jnp.where(row + col == rows - 1, 1.0, 0.0).astype(BF16)
    q_back = dot(flip, q_ref[...], 1, 0)
    content = jnp.zeros((rows, width), F32)
    position = jnp.zeros((rows, width), F32)
    dpq_sum[...] = jnp.zeros_like(dpq_sum)
    for head in range(heads):
        here = slice(head * rows, (head + 1) * rows)
        mask = head_mask((rows, width), head)
        dm = only_head(dm_ref[...], head)
        dm_all[here, :] = dm
        q_all[here, :] = only_head(q_ref[...], head)
        qr_all[here, :] = only_head(q_back, head)
        p = p_ref[head].astype(F32)
        da = dot(dm, v_ref[...], 1, 1)
        ds = (p * (da - jnp.sum(p * da, axis=1, keepdims=True))).astype(BF16)
        ds_all[here, :] = ds
        content = jnp.where(mask, dot(ds, k_ref[...], 1, 0), content)
        ds_back = dot(flip, ds, 1, 0)
        to = jnp.concatenate([ds_back, jnp.zeros((rows, win - keys), F32)], axis=1)
        to = pltpu.roll(to, 0, 1, stride=1, stride_axis=0).astype(BF16)
        to_all[here, :] = to
        position = jnp.where(mask, dot(to, pk_ref[...], 1, 0), position)
        for start in range(0, keys, BLOCK):
            off = ds_back[:, start : start + BLOCK].T
            off = jnp.concatenate([off, jnp.zeros((BLOCK, BLOCK), F32)], axis=1)
            off = pltpu.roll(off, 0, 1, stride=1, stride_axis=0).astype(BF16)
            key_block = only_head(k_ref[start : start + BLOCK, :], head)
            dpq_sum[start : start + 2 * BLOCK, :] += dot(off, key_block, 0, 0)
            more = dot(off, pq_ref[start : start + 2 * BLOCK, :], 1, 0)
            if head:
                more = jnp.where(
                    head_mask(more.shape, head), more, dk_pos[start : start + BLOCK, :]
                )
            dk_pos[start : start + BLOCK, :] = more
    high = position.astype(BF16)
    low = (position - high.astype(F32)).astype(BF16)
    dq = content + dot(flip, high, 1, 0) + dot(flip, low, 1, 0)
    dq_ref[...] = (scale * dq).astype(BF16)
    dkv_ref[:, :width] = (dot(ds_all[...], q_all[...], 0, 0) + dk_pos[...]).astype(BF16)
    p_all = p_ref[...].reshape(heads * rows, keys)
    dkv_ref[:, width:] = dot(p_all, dm_all[...], 0, 0).astype(BF16)
    dpk_ref[...] = dot(to_all[...], qr_all[...], 0, 0).astype(BF16)
    dpq_ref[...] = (scale * dpq_sum[...]).astype(BF16)


def attention_backward(q, k, v, pk_rev, pq_win, p, dm, scale):
    rows, width = q.shape
    keys = k.shape[0]
    heads = width // HEAD_DIM
    win = pk_rev.shape[0]
    return pl.pallas_call(
        functools.partial(backward_kernel, scale),
        out_shape=(
            jax.ShapeDtypeStruct((rows, width), BF16),
            jax.ShapeDtypeStruct((keys, 2 * width), BF16),
            jax.ShapeDtypeStruct((win, width), BF16),
            jax.ShapeDtypeStruct((win, width), BF16),
        ),
        scratch_shapes=[
            pltpu.VMEM((heads * rows, keys), BF16),
            pltpu.VMEM((heads * rows, win), BF16),
            pltpu.VMEM((keys, width), F32),
            pltpu.VMEM((heads * rows, width), BF16),
            pltpu.VMEM((heads * rows, width), BF16),
            pltpu.VMEM((heads * rows, width), BF16),
            pltpu.VMEM((win, width), F32),
        ],
        compiler_params=params(),
        name="attention_backward",
    )(q, k, v, pk_rev, pq_win, p, dm)


def shifted(values, axes, count, shift):
    return lax.ppermute(values, axes, [(i, (i + shift) % count) for i in range(count)])


def assemble_kernel(dims, place_ref, *refs):
    pieces, out_ref, sems = refs[:-2], refs[-2], refs[-1]
    core_count, z_count, x_count, zl_count = dims
    core, z, x = place_ref[0], place_ref[1], place_ref[2]
    rows = out_ref.shape[0] // (core_count * z_count * x_count)
    copies = []
    for c_shift in range(core_count):
        for z_shift in range(z_count):
            piece = pieces[c_shift * z_count + z_shift]
            for x_shift in range(x_count):
                from_c = lax.rem(core - c_shift + core_count, core_count)
                from_z = lax.rem(z - z_shift + z_count, z_count)
                from_x = lax.rem(x - x_shift + x_count, x_count)
                zh, zl = from_z // zl_count, lax.rem(from_z, zl_count)
                owner = ((zh * core_count + from_c) * x_count + from_x) * zl_count + zl
                start = pl.multiple_of(owner * rows, rows)
                copies.append(
                    pltpu.make_async_copy(
                        piece.at[pl.ds(x_shift * rows, rows), :],
                        out_ref.at[pl.ds(start, rows), :],
                        sems.at[len(copies)],
                    )
                )
    for copy in copies:
        copy.start()
    for copy in copies:
        copy.wait()


def gather_rows(values):
    core_count, x_count, zl_count = (lax.axis_size(a) for a in ("core", "x", "zl"))
    z_count = lax.axis_size("zh") * zl_count
    along_x = [values] + [shifted(values, "x", x_count, s) for s in range(1, x_count)]
    along_x = jnp.concatenate(along_x, axis=0)
    along_z = [along_x] + [shifted(along_x, ZED, z_count, s) for s in range(1, z_count)]
    other = [shifted(piece, "core", core_count, 1) for piece in along_z]
    place = jnp.stack([lax.axis_index("core"), lax.axis_index(ZED), lax.axis_index("x")])
    owners = core_count * z_count * x_count
    return pl.pallas_call(
        functools.partial(assemble_kernel, (core_count, z_count, x_count, zl_count)),
        in_specs=[pl.BlockSpec(memory_space=pltpu.SMEM)]
        + [pl.BlockSpec(memory_space=pl.ANY)] * (2 * z_count),
        out_specs=pl.BlockSpec(memory_space=pl.ANY),
        out_shape=jax.ShapeDtypeStruct((owners * values.shape[0], values.shape[1]), BF16),
        scratch_shapes=[pltpu.SemaphoreType.DMA((owners,))],
        compiler_params=params(),
        name="assemble",
    )(place.astype(jnp.int32), *along_z, *other)


def tp_sum(values):
    low = values.astype(BF16)
    count = lax.axis_size("tp")
    parts = [low] + [shifted(low, "tp", count, s) for s in range(1, count)]
    parts = [part.astype(F32) for part in parts]
    return (parts[0] + parts[2]) + (parts[1] + parts[3])


def core_columns(values, core):
    zh = lax.axis_size("zh")
    run = values.shape[1] // (zh * lax.axis_size("core"))
    picked = [
        lax.dynamic_slice_in_dim(values, (2 * part + core) * run, run, 1) for part in range(zh)
    ]
    return jnp.concatenate(picked, axis=1)


def core_rows(values, core):
    zh = lax.axis_size("zh")
    run = values.shape[0] // (zh * lax.axis_size("core"))
    picked = [
        lax.dynamic_slice_in_dim(values, (2 * part + core) * run, run, 0) for part in range(zh)
    ]
    return jnp.concatenate(picked, axis=0)


def scatter_rows(make):
    core = lax.axis_index("core")
    other = make(1 - core).astype(BF16)
    arrived = shifted(other, "core", 2, 1)
    total = (make(core) + arrived.astype(F32)).astype(BF16)
    owners = lax.axis_size(PLANE)
    rows = total.shape[0] // owners
    moved = lax.all_to_all(total.reshape(owners, rows, total.shape[1]), PLANE, 0, 0)
    return jnp.sum(moved.astype(F32), axis=0)


def normalize(values, gain_vec, offset):
    average = jnp.mean(values, axis=-1, keepdims=True)
    centered = values - average
    spread = jnp.mean(centered * centered, axis=-1, keepdims=True)
    return centered * lax.rsqrt(spread + EPS) * gain_vec + offset


def normalize_back(values, gain_vec, grad):
    average = jnp.mean(values, axis=-1, keepdims=True)
    centered = values - average
    spread = jnp.mean(centered * centered, axis=-1, keepdims=True)
    inverse = lax.rsqrt(spread + EPS)
    unit = centered * inverse
    scaled = grad * gain_vec
    back = (
        scaled
        - jnp.mean(scaled, axis=-1, keepdims=True)
        - unit * jnp.mean(scaled * unit, axis=-1, keepdims=True)
    ) * inverse
    return back, grad * unit


def gelu(values):
    return jax.nn.gelu(values, approximate=False)


def local(
    tokens,
    cotangent,
    w_qkv,
    w_attn,
    w_in,
    w_out,
    ln_gain,
    ln_bias,
    rel_emb,
    rel_gain,
    rel_bias,
    doc_ids,
    rel_bucket,
):
    _, rows, model = tokens.shape
    layers = w_qkv.shape[0]
    own = w_qkv.shape[2]
    width = w_qkv.shape[3]
    hidden_units = w_in.shape[2]
    ctx_count = lax.axis_size(CTX)
    length = rows * ctx_count
    ctx = lax.axis_index(CTX)
    row_start = ctx * rows
    scale = 1.0 / math.sqrt(3.0 * HEAD_DIM)
    win = length + rows

    first_qkv = jnp.concatenate([w_qkv[0, i] for i in range(3)], axis=1)
    small = jnp.concatenate(
        [
            ln_gain.reshape(2 * layers, own),
            ln_bias.reshape(2 * layers, own),
            rel_gain[None],
            rel_bias[None],
            doc_ids.astype(BF16).reshape(rows // own, own),
        ],
        axis=0,
    )
    small_rows = small.shape[0]
    small = jnp.pad(small, ((0, 128 - small_rows), (0, 0))).T
    rel_own = rel_emb.shape[0]
    rel_flat = rel_emb.reshape(own, rel_own * model // own)
    rest = [
        jnp.concatenate([w_attn[layer].T, w_in[layer], w_out[layer].T], axis=1)
        for layer in range(layers)
    ]
    start_pack = gather_rows(jnp.concatenate([first_qkv, rel_flat, small], axis=1))
    rest_full = [gather_rows(rest[0])]
    qkv_full = [start_pack[:, : 3 * width]]
    for layer in range(1, layers):
        pack = jnp.concatenate([w_qkv[layer, i] for i in range(3)] + [rest[layer]], axis=1)
        full = gather_rows(pack)
        qkv_full.append(full[:, : 3 * width])
        rest_full.append(full[:, 3 * width :])
    rel_cols = rel_flat.shape[1]
    rel_whole = start_pack[:, 3 * width : 3 * width + rel_cols].reshape(-1, model).astype(F32)
    bucket_count = rel_whole.shape[0]
    small_all = start_pack[:, 3 * width + rel_cols :].T
    gains = small_all[: 2 * layers].astype(F32).reshape(layers, 2, model)
    shifts = small_all[2 * layers : 4 * layers].astype(F32).reshape(layers, 2, model)
    rel_gain_all = small_all[4 * layers].astype(F32)
    rel_bias_all = small_all[4 * layers + 1].astype(F32)
    fsdp = lax.axis_index(("zh", "core"))
    docs = small_all[4 * layers + 2 : small_rows]
    docs = lax.dynamic_slice_in_dim(docs, fsdp * (ctx_count * own), ctx_count * own, 1)
    docs = docs.reshape(rows // own, ctx_count, own).swapaxes(0, 1).reshape(1, length)
    doc_j = docs.astype(jnp.int32)
    doc_i = doc_ids.reshape(rows, 1)

    rel_low = normalize(rel_whole, rel_gain_all, rel_bias_all).astype(BF16)

    padded = jnp.pad(rel_bucket, (1, 1), mode="edge")
    to_index = lax.dynamic_slice_in_dim(padded, row_start, win, 0)[::-1]
    from_index = lax.dynamic_slice_in_dim(padded, length - rows - row_start + 1, win, 0)
    ids = lax.broadcasted_iota(jnp.int32, (win, bucket_count), 1)
    to_table = (to_index[:, None] == ids).astype(BF16)
    from_table = (from_index[:, None] == ids).astype(BF16)
    from_back = (from_index[::-1][:, None] == ids).astype(BF16)
    place = jnp.stack([ctx]).astype(jnp.int32)

    stream = tokens[0].astype(F32)
    kept = []
    for layer in range(layers):
        qkv = qkv_full[layer]
        attn_t = rest_full[layer][:, :width]
        w_in_full = rest_full[layer][:, width : width + hidden_units]
        w_out_t = rest_full[layer][:, width + hidden_units :]
        stream_low = stream.astype(BF16)
        key_value = dot(stream_low, qkv[:, width:], 1, 0).astype(BF16)
        blocks = [key_value] + [shifted(key_value, CTX, ctx_count, s) for s in range(1, ctx_count)]
        q = (scale * dot(stream_low, qkv[:, :width], 1, 0)).astype(BF16)
        pos_q = (scale * dot(rel_low, qkv[:, :width], 1, 0)).astype(BF16)
        pos_k = dot(rel_low, qkv[:, width : 2 * width], 1, 0).astype(BF16)
        pk_rev = dot(to_table, pos_k, 1, 0).astype(BF16)
        pq_rev = dot(from_back, pos_q, 1, 0).astype(BF16)
        pq_win = dot(from_table, pos_q, 1, 0).astype(BF16)
        mixture, p, k_all, v_all = attention_forward(
            place, q, blocks, pk_rev, pq_rev, doc_i, doc_j
        )
        pre_hidden = stream + tp_sum(dot(mixture, attn_t, 1, 1))
        hidden = normalize(pre_hidden, gains[layer, 0], shifts[layer, 0])
        hidden_low = hidden.astype(BF16)
        inner_pre = dot(hidden_low, w_in_full, 1, 0)
        active = gelu(inner_pre).astype(BF16)
        pre_out = hidden + tp_sum(dot(active, w_out_t, 1, 1))
        stream = normalize(pre_out, gains[layer, 1], shifts[layer, 1])
        kept.append(
            (stream_low, q, k_all, v_all, pk_rev, pq_win, p, mixture, pre_hidden, hidden_low)
            + (inner_pre, active, pre_out, qkv, attn_t, w_in_full, w_out_t)
        )
    out_local = stream.astype(BF16)

    gradient = cotangent[0].astype(F32)
    results = [None] * layers
    rel_partial = None
    owner_rows = bucket_count // lax.axis_size(OWNERS)
    for layer in reversed(range(layers)):
        (stream_low, q, k_all, v_all, pk_rev, pq_win, p, mixture, pre_hidden, hidden_low) = kept[
            layer
        ][:10]
        (inner_pre, active, pre_out, qkv, attn_t, w_in_full, w_out_t) = kept[layer][10:]
        d_pre_out, gain_rows_out = normalize_back(pre_out, gains[layer, 1], gradient)
        d_out_low = d_pre_out.astype(BF16)
        d_active = dot(d_out_low, w_out_t, 1, 0)
        d_inner = jax.vjp(gelu, inner_pre)[1](d_active)[0].astype(BF16)
        d_hidden = d_pre_out + tp_sum(dot(d_inner, w_in_full, 1, 1))
        d_pre_hidden, gain_rows_hidden = normalize_back(pre_hidden, gains[layer, 0], d_hidden)
        d_attended = d_pre_hidden.astype(BF16)
        d_mixture = dot(d_attended, attn_t, 1, 0).astype(BF16)
        norm_grads = jnp.stack(
            [
                jnp.sum(gain_rows_hidden, axis=0),
                jnp.sum(gain_rows_out, axis=0),
                jnp.sum(d_hidden, axis=0),
                jnp.sum(gradient, axis=0),
            ]
        )
        norm_grads = jnp.pad(norm_grads, ((0, 124), (0, 0)))

        def early(core):
            return jnp.concatenate(
                [
                    dot(core_columns(d_attended, core), mixture, 0, 0),
                    dot(core_columns(hidden_low, core), d_inner, 0, 0),
                    dot(core_columns(d_out_low, core), active, 0, 0),
                    core_columns(norm_grads, core).T,
                ],
                axis=1,
            )

        early_sum = scatter_rows(early)
        dq, dkv, dpk, dpq = attention_backward(q, k_all, v_all, pk_rev, pq_win, p, d_mixture, scale)
        moved = lax.all_to_all(dkv.reshape(ctx_count, rows, 2 * width), CTX, 0, 0)
        dkv_low = jnp.sum(moved.astype(F32), axis=0).astype(BF16)
        d_pos_k = dot(to_table, dpk, 0, 0)
        d_pos_q = dot(from_table, dpq, 0, 0)
        pos_low = jnp.concatenate([d_pos_q, d_pos_k], axis=1).astype(BF16)
        pos_rows = jnp.concatenate(
            [
                d_pos_q.reshape(-1, owner_rows, width),
                d_pos_k.reshape(-1, owner_rows, width),
            ],
            axis=1,
        ).reshape(-1, width)
        dqkv = jnp.concatenate([dq, dkv_low], axis=1)

        def late(core):
            token_part = dot(core_columns(stream_low, core), dqkv, 0, 0)
            rel_part = dot(core_columns(rel_low, core), pos_low, 0, 0)
            token_part = token_part + jnp.pad(rel_part, ((0, 0), (0, width)))
            return jnp.concatenate([token_part, core_rows(pos_rows, core)], axis=1)

        gradient = d_pre_hidden + tp_sum(dot(dqkv, qkv, 1, 1))
        late_sum = scatter_rows(late)
        pos_sum = late_sum[:, 3 * width :].astype(BF16)
        term = dot(pos_sum[:owner_rows], qkv[:, :width], 1, 1) + dot(
            pos_sum[owner_rows:], qkv[:, width : 2 * width], 1, 1
        )
        rel_partial = term if rel_partial is None else rel_partial + term
        results[layer] = (early_sum, late_sum)

    grad_qkv = jnp.stack(
        [
            jnp.stack([late[:, i * width : (i + 1) * width] for i in range(3)])
            for _, late in results
        ]
    )
    grad_attn = jnp.stack([early[:, :width].T for early, _ in results])
    grad_in = jnp.stack([early[:, width : width + hidden_units] for early, _ in results])
    grad_out = jnp.stack(
        [early[:, width + hidden_units : width + 2 * hidden_units].T for early, _ in results]
    )
    norms = [early[:, width + 2 * hidden_units :].T for early, _ in results]
    grad_gain = jnp.stack([n[:2] for n in norms])
    grad_bias = jnp.stack([n[2:4] for n in norms])

    count = lax.axis_size("tp")
    parts = [rel_partial] + [shifted(rel_partial, "tp", count, s) for s in range(1, count)]
    d_rel = (parts[0] + parts[2]) + (parts[1] + parts[3])
    owner = lax.axis_index(OWNERS)
    grad_rel, gain_rows = normalize_back(rel_emb.astype(F32), rel_gain_all, d_rel)
    ends = jnp.stack([jnp.sum(gain_rows, axis=0), jnp.sum(d_rel, axis=0)])
    ends = ends.reshape(2, -1, own).swapaxes(0, 1)
    ends = lax.all_to_all(ends, OWNERS, 0, 0)
    ends = jnp.sum(ends, axis=0)
    return (
        out_local[None],
        gradient.astype(BF16)[None],
        grad_qkv,
        grad_attn,
        grad_in,
        grad_out,
        grad_gain,
        grad_bias,
        grad_rel,
        ends[0],
        ends[1],
    )


def solution(mesh):
    sizes = mesh.shape
    zh, zl, core = 2, 2, 2
    finer = Mesh(
        mesh.devices.reshape(zh, sizes["fsdp"] // zh, sizes["ctx"] // zl, zl, sizes["tp"]),
        ("zh", "core", "x", "zl", "tp"),
    )
    own = OWNERS
    fsdp = ("zh", "core")
    return jax.shard_map(
        local,
        mesh=finer,
        in_specs=(
            P(fsdp, CTX, None),
            P(fsdp, CTX, None),
            P(None, None, own, "tp"),
            P(None, "tp", own),
            P(None, own, "tp"),
            P(None, "tp", own),
            P(None, None, own),
            P(None, None, own),
            P(own, None),
            P(own),
            P(own),
            P(fsdp, CTX),
            P(),
        ),
        out_specs=(
            P(fsdp, CTX, None),
            P(fsdp, CTX, None),
            P(None, None, own, "tp"),
            P(None, "tp", own),
            P(None, own, "tp"),
            P(None, "tp", own),
            P(None, None, own),
            P(None, None, own),
            P(own, None),
            P(own),
            P(own),
        ),
        check_vma=False,
    )
```

```python
import functools
import math

import jax
import jax.numpy as jnp
from jax import lax
from jax.experimental import pallas as pl
from jax.experimental.pallas import tpu as pltpu
from jax.sharding import Mesh
from jax.sharding import PartitionSpec as P

HEAD_DIM = 64
EPS = 1e-07
NEG = -1e30
BLOCK = 128
LANES = 128
F32 = jnp.float32
BF16 = jnp.bfloat16
CTX = ("x", "zl")
ZED = ("zh", "zl")
PLANE = ("zh", "x", "zl")
OWNERS = ("zh", "core", "x", "zl")


def dot(a, b, ca, cb):
    return lax.dot_general(a, b, (((ca,), (cb,)), ((), ())), preferred_element_type=F32)


def call(body, outs, ins, *, anys=(), smem=(), scratch=(), limit=32, name=None):
    specs = []
    for i in range(len(ins)):
        space = pl.ANY if i in anys else pltpu.SMEM if i in smem else pltpu.VMEM
        specs.append(pl.BlockSpec(memory_space=space))
    return pl.pallas_call(
        body,
        in_specs=specs,
        out_specs=tuple(pl.BlockSpec(memory_space=pltpu.VMEM) for _ in outs),
        out_shape=tuple(jax.ShapeDtypeStruct(shape, dtype) for shape, dtype in outs),
        scratch_shapes=list(scratch),
        compiler_params=pltpu.CompilerParams(vmem_limit_bytes=limit << 20),
        name=name,
    )(*ins)


def head_mask(shape, head, axis=1):
    index = lax.broadcasted_iota(jnp.int32, shape, axis)
    return (index >= head * HEAD_DIM) & (index < (head + 1) * HEAD_DIM)


def only_head(values, head, axis=1):
    mask = head_mask(values.shape, head, axis)
    return jnp.where(mask, values.astype(F32), 0.0).astype(BF16)


def unit_of(values):
    average = jnp.mean(values, axis=-1, keepdims=True)
    centered = values - average
    spread = jnp.mean(centered * centered, axis=-1, keepdims=True)
    inverse = lax.rsqrt(spread + EPS)
    return centered * inverse, inverse


def normalize_back(values, gain_vec, grad):
    unit, inverse = unit_of(values)
    scaled = grad * gain_vec
    back = (
        scaled
        - jnp.mean(scaled, axis=-1, keepdims=True)
        - unit * jnp.mean(scaled * unit, axis=-1, keepdims=True)
    ) * inverse
    return back, grad * unit


def sum_pieces(pieces):
    parts = [piece[...].astype(F32) for piece in pieces]
    return (parts[0] + parts[2]) + (parts[1] + parts[3])


def pack_start_kernel(qkv_ref, rel_ref, gain_ref, bias_ref, rgain_ref, rbias_ref, doc_ref, out_ref, scr):
    own, width = qkv_ref.shape[2], qkv_ref.shape[3]
    layers = qkv_ref.shape[0]
    for i in range(3):
        out_ref[:, i * width : (i + 1) * width] = qkv_ref[0, i]
    at = 3 * width
    half = rel_ref.shape[1] // 2
    rel_rows = rel_ref.shape[0]
    out_ref[:rel_rows, at : at + half] = rel_ref[:, :half]
    out_ref[rel_rows:, at : at + half] = rel_ref[:, half:]
    at += half
    scr[...] = jnp.zeros_like(scr)
    for layer in range(layers):
        scr[2 * layer : 2 * layer + 2, :own] = gain_ref[layer].astype(F32)
        base = 2 * layers + 2 * layer
        scr[base : base + 2, :own] = bias_ref[layer].astype(F32)
    scr[4 * layers : 4 * layers + 1, :own] = rgain_ref[...].astype(F32)
    scr[4 * layers + 1 : 4 * layers + 2, :own] = rbias_ref[...].astype(F32)
    small = scr[...].T[:own, :]
    row = lax.broadcasted_iota(jnp.int32, small.shape, 0)
    upper = lax.broadcasted_iota(jnp.int32, small.shape, 1) >= LANES // 2
    doc = doc_ref[...].astype(F32)
    turned = pltpu.roll(doc, LANES // 2, 1)
    small = jnp.where(upper & (row == 0), turned, small)
    small = jnp.where(upper & (row == 1), doc, small)
    out_ref[:, at : at + LANES] = small.astype(BF16)


def pack_rest_kernel(layer, with_qkv, qkv_ref, attn_ref, in_ref, out_w_ref, pack_ref):
    width = qkv_ref.shape[3]
    hidden = in_ref.shape[2]
    at = 0
    if with_qkv:
        for i in range(3):
            pack_ref[:, i * width : (i + 1) * width] = qkv_ref[layer, i]
        at = 3 * width
    pack_ref[:, at : at + width] = attn_ref[layer].astype(F32).T.astype(BF16)
    at += width
    pack_ref[:, at : at + hidden] = in_ref[layer]
    at += hidden
    pack_ref[:, at : at + hidden] = out_w_ref[layer].astype(F32).T.astype(BF16)


def assemble(dims, place_ref, pieces, moves, sems):
    core_count, z_count, x_count, zl_count, own = dims
    core, z, x = place_ref[0], place_ref[1], place_ref[2]
    copies = []
    for c_shift in range(core_count):
        for z_shift in range(z_count):
            piece = pieces[c_shift * z_count + z_shift]
            for x_shift in range(x_count):
                from_c = lax.rem(core - c_shift + core_count, core_count)
                from_z = lax.rem(z - z_shift + z_count, z_count)
                from_x = lax.rem(x - x_shift + x_count, x_count)
                zh, zl = lax.div(from_z, zl_count), lax.rem(from_z, zl_count)
                owner = ((zh * core_count + from_c) * x_count + from_x) * zl_count + zl
                for row, rows, col, cols, target, step, to_col in moves:
                    start = pl.multiple_of(owner * step, step)
                    copies.append(
                        pltpu.make_async_copy(
                            piece.at[pl.ds(x_shift * own + row, rows), pl.ds(col, cols)],
                            target.at[pl.ds(start, rows), pl.ds(to_col, cols)],
                            sems.at[len(copies)],
                        )
                    )
    for copy in copies:
        copy.start()
    for copy in copies:
        copy.wait()


def start_kernel(dims, scale, place_ref, *refs):
    pieces, (tokens_ref, qkv_ref, rel_ref, small_ref, q_ref, kv_ref, sems) = refs[:-7], refs[-7:]
    own = dims[-1]
    wide = qkv_ref.shape[1]
    width = wide // 3
    half = rel_ref.shape[1] // 2
    part = own // 2
    moves = (
        (0, own, 0, wide, qkv_ref, own, 0),
        (0, part, wide, half, rel_ref, part, 0),
        (part, part, wide, half, rel_ref, part, half),
        (0, own, wide + half, LANES, small_ref, own, 0),
    )
    assemble(dims, place_ref, pieces, moves, sems)
    low = tokens_ref[...]
    kv_ref[...] = dot(low, qkv_ref[:, width:], 1, 0).astype(BF16)
    q_ref[...] = (scale * dot(low, qkv_ref[:, :width], 1, 0)).astype(BF16)


def rest_kernel(dims, outs, place_ref, *refs):
    pieces, targets, sems = refs[: -outs - 1], refs[-outs - 1 : -1], refs[-1]
    own = dims[-1]
    moves, at = [], 0
    for target in targets:
        cols = target.shape[1]
        moves.append((0, own, at, cols, target, own, 0))
        at += cols
    assemble(dims, place_ref, pieces, moves, sems)


def relative_kernel(layers, owners, place_ref, rel_ref, small_ref, low_ref, vec_ref, doc_ref):
    turned = small_ref[...].astype(F32).T[: vec_ref.shape[0], :]
    vec_ref[...] = turned
    unit, _ = unit_of(rel_ref[...].astype(F32))
    gain, bias = turned[4 * layers : 4 * layers + 1], turned[4 * layers + 1 : 4 * layers + 2]
    low_ref[...] = (unit * gain + bias).astype(BF16)
    length = doc_ref.shape[1]
    blocks = length // LANES
    fsdp = place_ref[0]
    own = small_ref.shape[0] // owners
    span = blocks * own
    mine = small_ref[pl.ds(pl.multiple_of(fsdp * span, span), span), :].astype(F32)
    upper = lax.broadcasted_iota(jnp.int32, (1, LANES), 1) >= LANES // 2
    for block in range(blocks):
        first = pltpu.roll(mine[block * own : block * own + 1, :], LANES // 2, 1)
        second = mine[block * own + 1 : block * own + 2, :]
        doc_ref[:, block * LANES : (block + 1) * LANES] = jnp.where(upper, second, first)


def table_kernel(index_ref, table_ref):
    count, buckets, win = table_ref.shape
    bucket = lax.broadcasted_iota(jnp.int32, (buckets, win), 0)
    for i in range(count):
        same = bucket == index_ref[i : i + 1, :]
        table_ref[i] = jnp.where(same, 1.0, 0.0).astype(BF16)


def position_kernel(scale, rel_ref, qkv_ref, table_ref, pk_ref, pq_rev_ref, pq_ref):
    width = qkv_ref.shape[1] // 3
    pos_q = (scale * dot(rel_ref[...], qkv_ref[:, :width], 1, 0)).astype(BF16)
    pos_k = dot(rel_ref[...], qkv_ref[:, width : 2 * width], 1, 0).astype(BF16)
    pk_ref[...] = dot(pos_k, table_ref[0], 0, 0).astype(BF16)
    pq_rev_ref[...] = dot(pos_q, table_ref[1], 0, 0).astype(BF16)
    pq_ref[...] = dot(pos_q, table_ref[2], 0, 0).astype(BF16)


def project_kernel(scale, rows_of, hidden_ref, *refs):
    pieces, rest = refs[:4], refs[4:]
    vec_ref, qkv_ref, pre_ref, stream_ref, low_ref, q_ref, kv_ref = rest
    width = qkv_ref.shape[1] // 3
    gain, bias = rows_of
    pre = hidden_ref[...] + sum_pieces(pieces)
    pre_ref[...] = pre
    unit, _ = unit_of(pre)
    stream = unit * vec_ref[gain : gain + 1, :] + vec_ref[bias : bias + 1, :]
    stream_ref[...] = stream
    low = stream.astype(BF16)
    low_ref[...] = low
    kv_ref[...] = dot(low, qkv_ref[:, width:], 1, 0).astype(BF16)
    q_ref[...] = (scale * dot(low, qkv_ref[:, :width], 1, 0)).astype(BF16)


def attention_kernel(place_ref, q_ref, *refs):
    blocks, rest = refs[:-12], refs[-12:]
    pk_ref, pq_ref, doc_i_ref, doc_j_ref, attn_ref = rest[:5]
    part_ref, mix_ref, p_ref, kv_ref, to_ref, q_all, sems = rest[5:]
    count = len(blocks)
    rows, width = q_ref.shape
    keys = kv_ref.shape[0]
    win = pk_ref.shape[1]
    heads = width // HEAD_DIM
    mine = place_ref[1]
    copies = []
    for shift, block in enumerate(blocks):
        owner = lax.rem(mine - shift + count, count)
        start = pl.multiple_of(owner * rows, rows)
        copies.append(
            pltpu.make_async_copy(block, kv_ref.at[pl.ds(start, rows), :], sems.at[shift])
        )
    for copy in copies:
        copy.start()
    for head in range(heads):
        q = only_head(q_ref[...], head)
        q_all[head] = q
        to = dot(q, pk_ref[...], 1, 0)
        to = pltpu.roll(to, win + 1 - rows, 1, stride=1, stride_axis=0)
        to_ref[head] = to[:, :keys]
    doc_i = jnp.broadcast_to(doc_i_ref[...].astype(F32), (rows, rows)).T
    for copy in copies:
        copy.wait()
    mix = jnp.zeros((rows, width), F32)
    for head in range(heads):
        q = q_all[head]
        parts = []
        for start in range(0, keys, BLOCK):
            key_block = kv_ref[start : start + BLOCK, :width]
            first = win - 2 * BLOCK - start
            pq = only_head(pq_ref[:, first : first + 2 * BLOCK], head, 0)
            off = dot(key_block, pq, 1, 0)
            off = pltpu.roll(off, BLOCK, 1, stride=1, stride_axis=0)
            s = dot(q, key_block, 1, 1) + to_ref[head, :, start : start + BLOCK]
            s = s + off[:, :BLOCK].T
            same = doc_i == doc_j_ref[:, start : start + BLOCK]
            parts.append(jnp.where(same, s, NEG))
        s = jnp.concatenate(parts, axis=1)
        e = jnp.exp(s - jnp.max(s, axis=1, keepdims=True))
        p = (e / jnp.sum(e, axis=1, keepdims=True)).astype(BF16)
        p_ref[head] = p
        mix = jnp.where(head_mask(mix.shape, head), dot(p, kv_ref[:, width:], 1, 0), mix)
    mix = mix.astype(BF16)
    mix_ref[...] = mix
    part_ref[...] = dot(mix, attn_ref[...], 1, 1).astype(BF16)


def feed_kernel(rows_of, stream_ref, *refs):
    pieces, rest = refs[:4], refs[4:]
    vec_ref, in_ref, out_ref = rest[:3]
    pre_ref, hidden_ref, low_ref, slope_ref, active_ref, part_ref = rest[3:]
    gain, bias = rows_of
    pre = stream_ref[...].astype(F32) + sum_pieces(pieces)
    pre_ref[...] = pre
    unit, _ = unit_of(pre)
    hidden = unit * vec_ref[gain : gain + 1, :] + vec_ref[bias : bias + 1, :]
    hidden_ref[...] = hidden
    low = hidden.astype(BF16)
    low_ref[...] = low
    inner = dot(low, in_ref[...], 1, 0)
    below = 0.5 * (1.0 + lax.erf(inner * math.sqrt(0.5)))
    bell = jnp.exp(-0.5 * inner * inner) * (1.0 / math.sqrt(2.0 * math.pi))
    slope_ref[...] = below + inner * bell
    active = (inner * below).astype(BF16)
    active_ref[...] = active
    part_ref[...] = dot(active, out_ref[...], 1, 1).astype(BF16)


def end_kernel(rows_of, hidden_ref, *refs):
    pieces, (vec_ref, pre_ref, out_ref) = refs[:4], refs[4:]
    gain, bias = rows_of
    pre = hidden_ref[...] + sum_pieces(pieces)
    pre_ref[...] = pre
    unit, _ = unit_of(pre)
    stream = unit * vec_ref[gain : gain + 1, :] + vec_ref[bias : bias + 1, :]
    out_ref[...] = stream.astype(BF16)


def column_sums(ref, first, second):
    ref[...] = jnp.zeros_like(ref)
    ref[0:1, :] = jnp.sum(first, axis=0, keepdims=True)
    ref[1:2, :] = jnp.sum(second, axis=0, keepdims=True)


def feed_back_kernel(gain, has_pieces, grad_ref, *refs):
    pieces, rest = (refs[:4], refs[4:]) if has_pieces else ((), refs)
    pre_ref, vec_ref, slope_ref, in_ref, out_ref = rest[:5]
    d_pre_ref, d_low_ref, d_inner_ref, part_ref, norm_ref = rest[5:]
    grad = grad_ref[...].astype(F32)
    if has_pieces:
        grad = grad + sum_pieces(pieces)
    back, gain_terms = normalize_back(pre_ref[...], vec_ref[gain : gain + 1, :], grad)
    column_sums(norm_ref, gain_terms, grad)
    d_pre_ref[...] = back
    low = back.astype(BF16)
    d_low_ref[...] = low
    inner = (dot(low, out_ref[...], 1, 0) * slope_ref[...]).astype(BF16)
    d_inner_ref[...] = inner
    part_ref[...] = dot(inner, in_ref[...], 1, 1).astype(BF16)


def attention_back_kernel(gain, scale, place_ref, *refs):
    pieces, rest = refs[:4], refs[4:]
    d_out_ref, pre_ref, vec_ref, attn_ref, q_ref, kv_ref, pk_ref, pq_ref, p_ref = rest[:9]
    d_pre_ref, d_low_ref, dq_ref, dpk_ref, dpq_ref, norm_ref = rest[9:15]
    ds_all, to_all, dk_pos, dm_all, q_all, qr_all, dpq_sum, dkv = rest[-8:]
    dkv_refs = rest[15:-8]
    rows, width = q_ref.shape
    keys = kv_ref.shape[0]
    heads = width // HEAD_DIM
    win = pk_ref.shape[1]

    grad = d_out_ref[...] + sum_pieces(pieces)
    back, gain_terms = normalize_back(pre_ref[...], vec_ref[gain : gain + 1, :], grad)
    column_sums(norm_ref, gain_terms, grad)
    d_pre_ref[...] = back
    d_low = back.astype(BF16)
    d_low_ref[...] = d_low
    d_mixture = dot(d_low, attn_ref[...], 1, 0)

    row = lax.broadcasted_iota(jnp.int32, (rows, rows), 0)
    col = lax.broadcasted_iota(jnp.int32, (rows, rows), 1)
    flip = jnp.where(row + col == rows - 1, 1.0, 0.0).astype(BF16)
    q_back = dot(flip, q_ref[...], 1, 0)
    content = jnp.zeros((rows, width), F32)
    position = jnp.zeros((rows, width), F32)
    dpq_sum[...] = jnp.zeros_like(dpq_sum)
    for head in range(heads):
        here = slice(head * rows, (head + 1) * rows)
        mask = head_mask((rows, width), head)
        dm = only_head(d_mixture, head)
        dm_all[here, :] = dm
        q_all[here, :] = only_head(q_ref[...], head)
        qr_all[here, :] = only_head(q_back, head)
        p = p_ref[head].astype(F32)
        da = dot(dm, kv_ref[:, width:], 1, 1)
        ds = (p * (da - jnp.sum(p * da, axis=1, keepdims=True))).astype(BF16)
        ds_all[here, :] = ds
        content = jnp.where(mask, dot(ds, kv_ref[:, :width], 1, 0), content)
        ds_back = dot(flip, ds, 1, 0)
        to = jnp.concatenate([ds_back, jnp.zeros((rows, win - keys), F32)], axis=1)
        to = pltpu.roll(to, 0, 1, stride=1, stride_axis=0).astype(BF16)
        to_all[here, :] = to
        position = jnp.where(mask, dot(to, pk_ref[...], 1, 1), position)
        for start in range(0, keys, BLOCK):
            off = ds_back[:, start : start + BLOCK].T
            off = jnp.concatenate([off, jnp.zeros((BLOCK, BLOCK), F32)], axis=1)
            off = pltpu.roll(off, 0, 1, stride=1, stride_axis=0).astype(BF16)
            key_block = only_head(kv_ref[start : start + BLOCK, :width], head)
            dpq_sum[start : start + 2 * BLOCK, :] += dot(off, key_block, 0, 0)
            more = dot(off, pq_ref[:, start : start + 2 * BLOCK], 1, 1)
            if head:
                more = jnp.where(
                    head_mask(more.shape, head), more, dk_pos[start : start + BLOCK, :]
                )
            dk_pos[start : start + BLOCK, :] = more
    high = position.astype(BF16)
    low = (position - high.astype(F32)).astype(BF16)
    dq = content + dot(flip, high, 1, 0) + dot(flip, low, 1, 0)
    dq_ref[...] = (scale * dq).astype(BF16)
    dkv[:, :width] = (dot(ds_all[...], q_all[...], 0, 0) + dk_pos[...]).astype(BF16)
    p_all = p_ref[...].reshape(heads * rows, keys)
    dkv[:, width:] = dot(p_all, dm_all[...], 0, 0).astype(BF16)
    count = len(dkv_refs)
    for shift, target in enumerate(dkv_refs):
        owner = lax.rem(place_ref[1] + shift, count)
        target[...] = dkv[pl.ds(pl.multiple_of(owner * rows, rows), rows), :]
    dpk_ref[...] = dot(to_all[...], qr_all[...], 0, 0).astype(BF16)
    dpq_ref[...] = (scale * dpq_sum[...]).astype(BF16)


def position_back_kernel(table_ref, dpk_ref, dpq_ref, low_ref, rows_ref):
    width = dpk_ref.shape[1]
    d_k = dot(table_ref[0], dpk_ref[...], 1, 0).astype(BF16)
    d_q = dot(table_ref[2], dpq_ref[...], 1, 0).astype(BF16)
    low_ref[:, :width] = d_q
    low_ref[:, width:] = d_k
    owners, step = rows_ref.shape[0], rows_ref.shape[1] // 2
    for owner in range(owners):
        rows_ref[owner, :step, :] = d_q[owner * step : (owner + 1) * step, :]
        rows_ref[owner, step:, :] = d_k[owner * step : (owner + 1) * step, :]


def picked_columns(ref, core, parts=2):
    run = ref.shape[1] // (2 * parts)
    picked = [ref[:, pl.ds(pl.multiple_of((2 * i + core) * run, run), run)] for i in range(parts)]
    return jnp.concatenate(picked, axis=1)


def early_kernel(own_core, place_ref, *refs):
    d_att_ref, mix_ref, hid_ref, d_inner_ref, d_out_ref, act_ref, norm_h_ref, norm_o_ref = refs[:8]
    out_ref, scr = refs[-2:]
    core = place_ref[2] if own_core else 1 - place_ref[2]
    at = 0
    for left, right in ((d_att_ref, mix_ref), (hid_ref, d_inner_ref), (d_out_ref, act_ref)):
        cols = right.shape[1]
        value = dot(picked_columns(left, core), right[...], 0, 0)
        if own_core:
            value = value + refs[8][:, at : at + cols].astype(F32)
        out_ref[:, at : at + cols] = value.astype(BF16)
        at += cols
    hid = picked_columns(norm_h_ref, core)
    out = picked_columns(norm_o_ref, core)
    scr[...] = jnp.zeros_like(scr)
    scr[0:1, :] = hid[0:1]
    scr[1:2, :] = out[0:1]
    scr[2:3, :] = hid[1:2]
    scr[3:4, :] = out[1:2]
    value = scr[...].T
    if own_core:
        value = value + refs[8][:, at : at + LANES].astype(F32)
    out_ref[:, at : at + LANES] = value.astype(BF16)


def stream_back_kernel(dq_ref, *refs):
    pieces, (qkv_ref, all_ref, part_ref) = refs[:-3], refs[-3:]
    total = pieces[0][...].astype(F32)
    for piece in pieces[1:]:
        total = total + piece[...].astype(F32)
    both = jnp.concatenate([dq_ref[...], total.astype(BF16)], axis=1)
    all_ref[...] = both
    part_ref[...] = dot(both, qkv_ref[...], 1, 1).astype(BF16)


def late_kernel(own_core, place_ref, low_ref, all_ref, rel_ref, pos_ref, *refs):
    out_ref = refs[-1]
    core = place_ref[2] if own_core else 1 - place_ref[2]
    wide = pos_ref.shape[1]
    value = dot(picked_columns(low_ref, core), all_ref[...], 0, 0)
    terms = dot(picked_columns(rel_ref, core), pos_ref[...], 0, 0)
    first = value[:, :wide] + terms
    second = value[:, wide:]
    if own_core:
        first = first + refs[0][:, :wide].astype(F32)
        second = second + refs[0][:, wide:].astype(F32)
    out_ref[:, :wide] = first.astype(BF16)
    out_ref[:, wide:] = second.astype(BF16)


def total_of(ref):
    total = ref[0].astype(F32)
    for i in range(1, ref.shape[0]):
        total = total + ref[i].astype(F32)
    return total


def early_end_kernel(*refs):
    layers = len(refs) - 5
    attn_ref, in_ref, out_ref, gain_ref, bias_ref = refs[layers:]
    width, hidden = attn_ref.shape[1], in_ref.shape[2]
    for layer in range(layers):
        total = total_of(refs[layer])
        attn_ref[layer] = total[:, :width].T
        in_ref[layer] = total[:, width : width + hidden]
        out_ref[layer] = total[:, width + hidden : width + 2 * hidden].T
        norms = total[:, width + 2 * hidden :].T
        gain_ref[layer] = norms[0:2, :]
        bias_ref[layer] = norms[2:4, :]


def late_end_kernel(*refs):
    layers = len(refs) - 1
    out_ref = refs[-1]
    width = out_ref.shape[3]
    for layer in range(layers):
        total = total_of(refs[layer])
        for i in range(3):
            out_ref[layer, i] = total[:, i * width : (i + 1) * width]


def relative_term_kernel(*refs):
    layers = (len(refs) - 1) // 2
    out_ref = refs[-1]
    width = refs[0].shape[2]
    step = refs[0].shape[1] // 2
    total = None
    for layer in range(layers):
        moved = total_of(refs[2 * layer]).astype(BF16)
        qkv_ref = refs[2 * layer + 1]
        term = dot(moved[:step], qkv_ref[:, :width], 1, 1)
        term = term + dot(moved[step:], qkv_ref[:, width : 2 * width], 1, 1)
        total = term if total is None else total + term
    out_ref[...] = total


def relative_end_kernel(gain, *refs):
    pieces, (rel_ref, vec_ref, grad_ref, ends_ref) = refs[:4], refs[4:]
    d_rel = sum_pieces(pieces)
    back, gain_terms = normalize_back(
        rel_ref[...].astype(F32), vec_ref[gain : gain + 1, :], d_rel
    )
    grad_ref[...] = back
    owners, _, own = ends_ref.shape
    for k, terms in enumerate((gain_terms, d_rel)):
        sums = jnp.sum(terms, axis=0, keepdims=True)
        for owner in range(owners):
            first = owner * own // LANES * LANES
            chunk = sums[:, first : first + LANES]
            offset = owner * own - first
            if offset:
                chunk = pltpu.roll(chunk, LANES - offset, 1)
            ends_ref[owner, k : k + 1, :] = chunk[:, :own]


def shifted(values, axes, shift):
    count = lax.axis_size(axes)
    return lax.ppermute(values, axes, [(i, (i + shift) % count) for i in range(count)])


def gather_pieces(values):
    x_count, z_count = lax.axis_size("x"), lax.axis_size(ZED)
    along_x = [values] + [shifted(values, "x", s) for s in range(1, x_count)]
    along_x = jnp.concatenate(along_x, axis=0)
    along_z = [along_x] + [shifted(along_x, ZED, s) for s in range(1, z_count)]
    return along_z + [shifted(piece, "core", 1) for piece in along_z]


def tp_pieces(low):
    return [low] + [shifted(low, "tp", s) for s in range(1, lax.axis_size("tp"))]


def plane_blocks(values):
    owners = lax.axis_size(PLANE)
    blocks = values.reshape(owners, values.shape[0] // owners, values.shape[1])
    return lax.all_to_all(blocks, PLANE, 0, 0)


def local(
    tokens,
    cotangent,
    w_qkv,
    w_attn,
    w_in,
    w_out,
    ln_gain,
    ln_bias,
    rel_emb,
    rel_gain,
    rel_bias,
    doc_ids,
    rel_bucket,
):
    _, rows, model = tokens.shape
    layers, _, own, width = w_qkv.shape
    hidden_units = w_in.shape[2]
    heads = width // HEAD_DIM
    ctx_count = lax.axis_size(CTX)
    owners = lax.axis_size(OWNERS)
    length = rows * ctx_count
    row_start = lax.axis_index(CTX) * rows
    scale = 1.0 / math.sqrt(3.0 * HEAD_DIM)
    win = length + rows
    rel_own = rel_emb.shape[0]
    buckets = rel_own * owners
    wide = 3 * width

    dims = (
        lax.axis_size("core"),
        lax.axis_size(ZED),
        lax.axis_size("x"),
        lax.axis_size("zl"),
        own,
    )
    whence = jnp.stack([lax.axis_index("core"), lax.axis_index(ZED), lax.axis_index("x")])
    whence = whence.astype(jnp.int32)
    place = jnp.stack(
        [lax.axis_index(("zh", "core")), lax.axis_index(CTX), lax.axis_index("core")]
    ).astype(jnp.int32)

    start_cols = wide + model // 2 + LANES
    (start_pack,) = call(
        pack_start_kernel,
        [((own, start_cols), BF16)],
        [w_qkv, rel_emb, ln_gain, ln_bias, rel_gain[None], rel_bias[None], doc_ids],
        scratch=[pltpu.VMEM((LANES, LANES), F32)],
        limit=8,
        name="pack_start",
    )
    rest_packs = []
    for layer in range(layers):
        cols = width + 2 * hidden_units + (wide if layer else 0)
        rest_packs.extend(
            call(
                functools.partial(pack_rest_kernel, layer, layer > 0),
                [((own, cols), BF16)],
                [w_qkv, w_attn, w_in, w_out],
                limit=16,
                name="pack_rest",
            )
        )
    start_pieces = gather_pieces(start_pack)
    rest_pieces = [gather_pieces(pack) for pack in rest_packs]

    padded = jnp.pad(rel_bucket, (1, 1), mode="edge")
    to_index = lax.dynamic_slice_in_dim(padded, row_start, win, 0)
    from_index = lax.dynamic_slice_in_dim(padded, length - rows - row_start + 1, win, 0)
    index = jnp.stack([to_index[::-1], from_index[::-1], from_index])
    (tables,) = call(
        table_kernel, [((3, buckets, win), BF16)], [index], limit=16, name="tables"
    )

    copies = 4 * owners
    qkv, rel_raw, small, q, key_value = call(
        functools.partial(start_kernel, dims, scale),
        [
            ((model, wide), BF16),
            ((buckets, model), BF16),
            ((model, LANES), BF16),
            ((rows, width), BF16),
            ((rows, 2 * width), BF16),
        ],
        [whence, *start_pieces, tokens[0]],
        smem=(0,),
        anys=range(1, 1 + len(start_pieces)),
        scratch=[pltpu.SemaphoreType.DMA((copies,))],
        limit=24,
        name="start",
    )
    rel_low, vecs, doc_j = call(
        functools.partial(relative_kernel, layers, owners),
        [((buckets, model), BF16), ((16, model), F32), ((1, length), F32)],
        [place, rel_raw, small],
        smem=(0,),
        limit=24,
        name="relative",
    )
    qkvs, rests = [qkv], []
    for layer in range(layers):
        shapes = [((model, c), BF16) for c in (width, hidden_units, hidden_units)]
        if layer:
            shapes = [((model, wide), BF16)] + shapes
        outs = call(
            functools.partial(rest_kernel, dims, len(shapes)),
            shapes,
            [whence, *rest_pieces[layer]],
            smem=(0,),
            anys=range(1, 1 + len(rest_pieces[layer])),
            scratch=[pltpu.SemaphoreType.DMA((len(shapes) * owners,))],
            limit=24,
            name="rest",
        )
        if layer:
            qkvs.append(outs[0])
        rests.append(outs[-3:])

    token_low = tokens[0]
    stream = token_low
    kept = []
    hidden, pieces = None, None
    tile = (rows, model)
    for layer in range(layers):
        qkv = qkvs[layer]
        attn_t, in_full, out_t = rests[layer]
        if layer:
            pre_out, stream, stream_low, q, key_value = call(
                functools.partial(
                    project_kernel, scale, (2 * layer - 1, 2 * layers + 2 * layer - 1)
                ),
                [
                    (tile, F32),
                    (tile, F32),
                    (tile, BF16),
                    ((rows, width), BF16),
                    ((rows, 2 * width), BF16),
                ],
                [hidden, *pieces, vecs, qkv],
                name="project",
            )
            kept[-1]["pre_out"] = pre_out
        else:
            stream_low = token_low
        blocks = [key_value] + [shifted(key_value, CTX, s) for s in range(1, ctx_count)]
        pk, pq_rev, pq = call(
            functools.partial(position_kernel, scale),
            [((width, win), BF16)] * 3,
            [rel_low, qkv, tables],
            name="position",
        )
        part, mixture, p, kv = call(
            attention_kernel,
            [
                (tile, BF16),
                ((rows, width), BF16),
                ((heads, rows, length), BF16),
                ((length, 2 * width), BF16),
            ],
            [place, q, *blocks, pk, pq_rev, doc_ids, doc_j, attn_t],
            smem=(0,),
            anys=range(2, 2 + ctx_count),
            scratch=[
                pltpu.VMEM((heads, rows, length), F32),
                pltpu.VMEM((heads, rows, width), BF16),
                pltpu.SemaphoreType.DMA((ctx_count,)),
            ],
            name="attention",
        )
        pre_hidden, hidden, hidden_low, slope, active, part = call(
            functools.partial(feed_kernel, (2 * layer, 2 * layers + 2 * layer)),
            [
                (tile, F32),
                (tile, F32),
                (tile, BF16),
                ((rows, hidden_units), F32),
                ((rows, hidden_units), BF16),
                (tile, BF16),
            ],
            [stream, *tp_pieces(part), vecs, in_full, out_t],
            name="feed",
        )
        pieces = tp_pieces(part)
        kept.append(
            dict(
                stream_low=stream_low,
                q=q,
                kv=kv,
                pk=pk,
                pq=pq,
                p=p,
                mixture=mixture,
                pre_hidden=pre_hidden,
                hidden_low=hidden_low,
                slope=slope,
                active=active,
            )
        )
    last = layers - 1
    pre_out, out_local = call(
        functools.partial(end_kernel, (2 * last + 1, 2 * layers + 2 * last + 1)),
        [(tile, F32), (tile, BF16)],
        [hidden, *pieces, vecs],
        name="end",
    )
    kept[-1]["pre_out"] = pre_out

    grad_parts = [cotangent[0]]
    early_blocks, late_blocks, pos_blocks = [None] * layers, [None] * layers, [None] * layers
    for layer in reversed(range(layers)):
        k = kept[layer]
        qkv = qkvs[layer]
        attn_t, in_full, out_t = rests[layer]
        d_pre_out, d_out_low, d_inner, part, norm_out = call(
            functools.partial(feed_back_kernel, 2 * layer + 1, len(grad_parts) > 1),
            [
                (tile, F32),
                (tile, BF16),
                ((rows, hidden_units), BF16),
                (tile, BF16),
                ((8, model), F32),
            ],
            [*grad_parts, k["pre_out"], vecs, k["slope"], in_full, out_t],
            name="feed_back",
        )
        backs = call(
            functools.partial(attention_back_kernel, 2 * layer, scale),
            [
                (tile, F32),
                (tile, BF16),
                ((rows, width), BF16),
                ((win, width), BF16),
                ((win, width), BF16),
                ((8, model), F32),
            ]
            + [((rows, 2 * width), BF16)] * ctx_count,
            [place, *tp_pieces(part), d_pre_out, k["pre_hidden"], vecs, attn_t]
            + [k["q"], k["kv"], k["pk"], k["pq"], k["p"]],
            smem=(0,),
            scratch=[
                pltpu.VMEM((heads * rows, length), BF16),
                pltpu.VMEM((heads * rows, win), BF16),
                pltpu.VMEM((length, width), F32),
                pltpu.VMEM((heads * rows, width), BF16),
                pltpu.VMEM((heads * rows, width), BF16),
                pltpu.VMEM((heads * rows, width), BF16),
                pltpu.VMEM((win, width), F32),
                pltpu.VMEM((length, 2 * width), BF16),
            ],
            name="attention_back",
        )
        d_pre_hidden, d_attended, dq, dpk, dpq, norm_hidden = backs[:6]
        dkv = [backs[6]] + [shifted(backs[6 + s], CTX, s) for s in range(1, ctx_count)]

        early_in = [place, d_attended, k["mixture"], k["hidden_low"], d_inner]
        early_in += [d_out_low, k["active"], norm_hidden, norm_out]
        early_cols = width + 2 * hidden_units + LANES
        early = [((model // 2, early_cols), BF16)]
        early_scratch = [pltpu.VMEM((LANES, model // 2), F32)]
        (other,) = call(
            functools.partial(early_kernel, False),
            early,
            early_in,
            smem=(0,),
            scratch=early_scratch,
            name="early_other",
        )
        (mine,) = call(
            functools.partial(early_kernel, True),
            early,
            [*early_in, shifted(other, "core", 1)],
            smem=(0,),
            scratch=early_scratch,
            name="early_own",
        )
        early_blocks[layer] = plane_blocks(mine)

        pos_low, pos_rows = call(
            position_back_kernel,
            [((buckets, 2 * width), BF16), ((owners, 2 * rel_own, width), BF16)],
            [tables, dpk, dpq],
            name="position_back",
        )
        pos_blocks[layer] = lax.all_to_all(pos_rows, OWNERS, 0, 0)

        dqkv, part = call(
            stream_back_kernel,
            [((rows, wide), BF16), (tile, BF16)],
            [dq, *dkv, qkv],
            name="stream_back",
        )
        grad_parts = [d_pre_hidden] + tp_pieces(part)
        late_in = [place, k["stream_low"], dqkv, rel_low, pos_low]
        late = [((model // 2, wide), BF16)]
        (other,) = call(
            functools.partial(late_kernel, False), late, late_in, smem=(0,), name="late_other"
        )
        (mine,) = call(
            functools.partial(late_kernel, True),
            late,
            [*late_in, shifted(other, "core", 1)],
            smem=(0,),
            name="late_own",
        )
        late_blocks[layer] = plane_blocks(mine)

    total = (grad_parts[1].astype(F32) + grad_parts[3].astype(F32)) + (
        grad_parts[2].astype(F32) + grad_parts[4].astype(F32)
    )
    grad_tokens = (grad_parts[0] + total).astype(BF16)

    grad_attn, grad_in, grad_out, grad_gain, grad_bias = call(
        early_end_kernel,
        [
            ((layers, width, own), F32),
            ((layers, own, hidden_units), F32),
            ((layers, hidden_units, own), F32),
            ((layers, 2, own), F32),
            ((layers, 2, own), F32),
        ],
        early_blocks,
        name="early_end",
    )
    (grad_qkv,) = call(
        late_end_kernel, [((layers, 3, own, width), F32)], late_blocks, name="late_end"
    )

    term_in = []
    for layer in range(layers):
        term_in += [pos_blocks[layer], qkvs[layer]]
    (term,) = call(relative_term_kernel, [((rel_own, model), F32)], term_in, name="relative_term")
    grad_rel, ends = call(
        functools.partial(relative_end_kernel, 4 * layers),
        [((rel_own, model), F32), ((owners, 2, own), F32)],
        [*tp_pieces(term), rel_emb, vecs],
        name="relative_end",
    )
    ends = jnp.sum(lax.all_to_all(ends, OWNERS, 0, 0), axis=0)
    return (
        out_local[None],
        grad_tokens[None],
        grad_qkv,
        grad_attn,
        grad_in,
        grad_out,
        grad_gain,
        grad_bias,
        grad_rel,
        ends[0],
        ends[1],
    )


def solution(mesh):
    sizes = mesh.shape
    zh, zl = 2, 2
    finer = Mesh(
        mesh.devices.reshape(zh, sizes["fsdp"] // zh, sizes["ctx"] // zl, zl, sizes["tp"]),
        ("zh", "core", "x", "zl", "tp"),
    )
    own = OWNERS
    fsdp = ("zh", "core")
    return jax.shard_map(
        local,
        mesh=finer,
        in_specs=(
            P(fsdp, CTX, None),
            P(fsdp, CTX, None),
            P(None, None, own, "tp"),
            P(None, "tp", own),
            P(None, own, "tp"),
            P(None, "tp", own),
            P(None, None, own),
            P(None, None, own),
            P(own, None),
            P(own),
            P(own),
            P(fsdp, CTX),
            P(),
        ),
        out_specs=(
            P(fsdp, CTX, None),
            P(fsdp, CTX, None),
            P(None, None, own, "tp"),
            P(None, "tp", own),
            P(None, own, "tp"),
            P(None, "tp", own),
            P(None, None, own),
            P(None, None, own),
            P(own, None),
            P(own),
            P(own),
        ),
        check_vma=False,
    )
```

```python
import functools
import math

import jax
import jax.numpy as jnp
from jax import lax
from jax.experimental import pallas as pl
from jax.experimental.pallas import tpu as pltpu
from jax.sharding import Mesh
from jax.sharding import PartitionSpec as P

HEAD_DIM = 64
EPS = 1e-07
NEG = -1e30
BLOCK = 128
LANES = 128
F32 = jnp.float32
BF16 = jnp.bfloat16
CTX = ("x", "zl")
ZED = ("zh", "zl")
PLANE = ("zh", "x", "zl")
OWNERS = ("zh", "core", "x", "zl")


def dot(a, b, ca, cb):
    return lax.dot_general(a, b, (((ca,), (cb,)), ((), ())), preferred_element_type=F32)


def call(body, outs, ins, *, anys=(), hbm=(), smem=(), scratch=(), after=(), limit=8, name=None):
    specs = []
    for i in range(len(ins)):
        space = pltpu.VMEM
        if i in anys:
            space = pl.ANY
        if i in hbm:
            space = pltpu.HBM
        if i in smem:
            space = pltpu.SMEM
        specs.append(pl.BlockSpec(memory_space=space))
    count, late = len(ins), len(after)
    specs += [pl.BlockSpec(memory_space=pl.ANY)] * late
    ins = [
        pltpu.with_memory_space_constraint(value, pltpu.HBM) if i in hbm else value
        for i, value in enumerate(ins)
    ]

    def without(*refs):
        body(*refs[:count], *refs[count + late :])

    return pl.pallas_call(
        without,
        in_specs=specs,
        out_specs=tuple(pl.BlockSpec(memory_space=pltpu.VMEM) for _ in outs),
        out_shape=tuple(jax.ShapeDtypeStruct(shape, dtype) for shape, dtype in outs),
        scratch_shapes=list(scratch),
        compiler_params=pltpu.CompilerParams(vmem_limit_bytes=limit << 20),
        name=name,
    )(*ins, *after)


def ctx_shifts(x_count, zl_count):
    pairs = [(dx, dz) for dx in range(x_count) for dz in range(zl_count)]
    return sorted(pairs, key=lambda p: (min(p[0], x_count - p[0]) + p[1], p[1], p[0]))


def ctx_owner(place_ref, shift, sign, x_count, zl_count):
    x = lax.rem(place_ref[1] + (sign * shift[0]) % x_count, x_count)
    zl = lax.rem(place_ref[2] + (sign * shift[1]) % zl_count, zl_count)
    return x * zl_count + zl


def head_mask(shape, head, axis=1):
    index = lax.broadcasted_iota(jnp.int32, shape, axis)
    return (index >= head * HEAD_DIM) & (index < (head + 1) * HEAD_DIM)


def only_head(values, head, axis=1):
    mask = head_mask(values.shape, head, axis)
    return jnp.where(mask, values.astype(F32), 0.0).astype(BF16)


def unit_of(values):
    average = jnp.mean(values, axis=-1, keepdims=True)
    centered = values - average
    spread = jnp.mean(centered * centered, axis=-1, keepdims=True)
    inverse = lax.rsqrt(spread + EPS)
    return centered * inverse, inverse


def normalize_back(values, gain_vec, grad):
    unit, inverse = unit_of(values)
    scaled = grad * gain_vec
    back = (
        scaled
        - jnp.mean(scaled, axis=-1, keepdims=True)
        - unit * jnp.mean(scaled * unit, axis=-1, keepdims=True)
    ) * inverse
    return back, grad * unit


def sum_pieces(pieces):
    parts = [piece[...].astype(F32) for piece in pieces]
    return (parts[0] + parts[2]) + (parts[1] + parts[3])


def run_copies(pairs, sems):
    copies = [
        pltpu.make_async_copy(source, target, sems.at[i])
        for i, (source, target) in enumerate(pairs)
    ]
    for copy in copies:
        copy.start()
    for copy in copies:
        copy.wait()


def pack_start_kernel(qkv_ref, attn_ref, rel_ref, gain_ref, bias_ref, rgain_ref, rbias_ref, doc_ref, *refs):
    out_ref, scr, gain, bias, rgain, rbias, doc, sems = refs
    own, width = qkv_ref.shape[2], qkv_ref.shape[3]
    layers = qkv_ref.shape[0]
    at = 4 * width
    half = rel_ref.shape[1] // 2
    part = rel_ref.shape[0]
    pairs = [(gain_ref, gain), (bias_ref, bias), (rgain_ref, rgain), (rbias_ref, rbias)]
    pairs += [(doc_ref, doc), (attn_ref.at[0], out_ref.at[:, pl.ds(3 * width, width)])]
    pairs += [(qkv_ref.at[0, i], out_ref.at[:, pl.ds(i * width, width)]) for i in range(3)]
    pairs += [
        (rel_ref.at[:, pl.ds(i * half, half)], out_ref.at[pl.ds(i * part, part), pl.ds(at, half)])
        for i in range(2)
    ]
    run_copies(pairs, sems)
    at += half
    scr[...] = jnp.zeros_like(scr)
    for layer in range(layers):
        scr[2 * layer : 2 * layer + 2, :own] = gain[layer].astype(F32)
        base = 2 * layers + 2 * layer
        scr[base : base + 2, :own] = bias[layer].astype(F32)
    scr[4 * layers : 4 * layers + 1, :own] = rgain[...].astype(F32)
    scr[4 * layers + 1 : 4 * layers + 2, :own] = rbias[...].astype(F32)
    small = scr[...].T[:own, :]
    row = lax.broadcasted_iota(jnp.int32, small.shape, 0)
    upper = lax.broadcasted_iota(jnp.int32, small.shape, 1) >= LANES // 2
    doc_row = doc[...].astype(F32)
    turned = pltpu.roll(doc_row, LANES // 2, 1)
    small = jnp.where(upper & (row == 0), turned, small)
    small = jnp.where(upper & (row == 1), doc_row, small)
    out_ref[:, at : at + LANES] = small.astype(BF16)


def pack_kernel(index, *refs):
    ins, (out_ref, sems) = refs[: len(index)], refs[-2:]
    pairs, at = [], 0
    for ref, lead in zip(ins, index):
        cols = ref.shape[-1]
        pairs.append((ref.at[lead], out_ref.at[:, pl.ds(at, cols)]))
        at += cols
    run_copies(pairs, sems)


def stack_kernel(count, *refs):
    out_ref = refs[-1]
    rows = refs[0].shape[0]
    for i in range(count):
        out_ref[i * rows : (i + 1) * rows, :] = refs[i][...]


def assemble(dims, x_inner, place_ref, pieces, moves, sems):
    core_count, z_count, x_count, zl_count, own = dims
    x, core, z = place_ref[1], place_ref[3], place_ref[4]
    pairs = []
    for c_shift in range(core_count):
        for z_shift in range(z_count):
            for x_shift in range(x_count):
                place = z_shift * x_count + x_shift if x_inner else x_shift * z_count + z_shift
                from_c = lax.rem(core - c_shift + core_count, core_count)
                from_z = lax.rem(z - z_shift + z_count, z_count)
                from_x = lax.rem(x - x_shift + x_count, x_count)
                zh, zl = lax.div(from_z, zl_count), lax.rem(from_z, zl_count)
                owner = ((zh * core_count + from_c) * x_count + from_x) * zl_count + zl
                for row, rows, col, cols, target, step, to_col in moves:
                    start = pl.multiple_of(owner * step, step)
                    pairs.append(
                        (
                            pieces[c_shift].at[pl.ds(place * own + row, rows), pl.ds(col, cols)],
                            target.at[pl.ds(start, rows), pl.ds(to_col, cols)],
                        )
                    )
    run_copies(pairs, sems)


def start_kernel(dims, scale, place_ref, one_ref, two_ref, tokens_ref, *refs):
    qkv_ref, attn_ref, small_ref, q_ref, kv_ref, sems = refs
    own = dims[-1]
    wide = qkv_ref.shape[1]
    width = wide // 3
    moves = (
        (0, own, 0, wide, qkv_ref, own, 0),
        (0, own, wide, width, attn_ref, own, 0),
        (0, own, one_ref.shape[1] - LANES, LANES, small_ref, own, 0),
    )
    assemble(dims, True, place_ref, (one_ref, two_ref), moves, sems)
    low = tokens_ref[...]
    kv_ref[...] = dot(low, qkv_ref[:, width:], 1, 0).astype(BF16)
    q_ref[...] = (scale * dot(low, qkv_ref[:, :width], 1, 0)).astype(BF16)


def rest_kernel(dims, x_inner, outs, place_ref, one_ref, two_ref, *refs):
    targets, sems = refs[-outs - 1 : -1], refs[-1]
    own = dims[-1]
    moves, at = [], 0
    for target in targets:
        cols = target.shape[1]
        moves.append((0, own, at, cols, target, own, 0))
        at += cols
    assemble(dims, x_inner, place_ref, (one_ref, two_ref), moves, sems)


def relative_kernel(dims, layers, place_ref, one_ref, two_ref, small_ref, *refs):
    low_ref, vec_ref, doc_ref, rel_ref, sems = refs
    own = dims[-1]
    part = own // 2
    half = rel_ref.shape[1] // 2
    at = one_ref.shape[1] - LANES - half
    moves = (
        (0, part, at, half, rel_ref, part, 0),
        (part, part, at, half, rel_ref, part, half),
    )
    assemble(dims, True, place_ref, (one_ref, two_ref), moves, sems)
    turned = small_ref[...].astype(F32).T[: vec_ref.shape[0], :]
    vec_ref[...] = turned
    unit, _ = unit_of(rel_ref[...].astype(F32))
    gain, bias = turned[4 * layers : 4 * layers + 1], turned[4 * layers + 1 : 4 * layers + 2]
    low_ref[...] = (unit * gain + bias).astype(BF16)
    blocks = doc_ref.shape[1] // LANES
    span = blocks * own
    start = pl.multiple_of(place_ref[0] * span, span)
    mine = small_ref[pl.ds(start, span), :].astype(F32)
    upper = lax.broadcasted_iota(jnp.int32, (1, LANES), 1) >= LANES // 2
    for block in range(blocks):
        first = pltpu.roll(mine[block * own : block * own + 1, :], LANES // 2, 1)
        second = mine[block * own + 1 : block * own + 2, :]
        doc_ref[:, block * LANES : (block + 1) * LANES] = jnp.where(upper, second, first)


def table_kernel(index_ref, table_ref):
    count, buckets, win = table_ref.shape
    bucket = lax.broadcasted_iota(jnp.int32, (buckets, win), 0)
    for i in range(count):
        same = bucket == index_ref[i : i + 1, :]
        table_ref[i] = jnp.where(same, 1.0, 0.0).astype(BF16)


def position_kernel(scale, skip, rel_ref, qkv_ref, table_ref, pk_ref, pq_rev_ref, pq_ref):
    width = pk_ref.shape[0]
    pos_q = (scale * dot(rel_ref[...], qkv_ref[:, skip : skip + width], 1, 0)).astype(BF16)
    pos_k = dot(rel_ref[...], qkv_ref[:, skip + width : skip + 2 * width], 1, 0).astype(BF16)
    pk_ref[...] = dot(pos_k, table_ref[0], 0, 0).astype(BF16)
    pq_rev_ref[...] = dot(pos_q, table_ref[1], 0, 0).astype(BF16)
    pq_ref[...] = dot(pos_q, table_ref[2], 0, 0).astype(BF16)


def project_kernel(scale, rows_of, skip, hidden_ref, *refs):
    pieces, rest = refs[:4], refs[4:]
    vec_ref, qkv_ref, pre_ref, stream_ref, low_ref, q_ref, kv_ref = rest
    width = q_ref.shape[1]
    gain, bias = rows_of
    pre = hidden_ref[...] + sum_pieces(pieces)
    pre_ref[...] = pre
    unit, _ = unit_of(pre)
    stream = unit * vec_ref[gain : gain + 1, :] + vec_ref[bias : bias + 1, :]
    stream_ref[...] = stream
    low = stream.astype(BF16)
    low_ref[...] = low
    kv_ref[...] = dot(low, qkv_ref[:, skip + width : skip + 3 * width], 1, 0).astype(BF16)
    q_ref[...] = (scale * dot(low, qkv_ref[:, skip : skip + width], 1, 0)).astype(BF16)


def gather_kernel(shape, place_ref, *refs):
    blocks, kv_ref, sems = refs[:-2], refs[-2], refs[-1]
    rows = blocks[0].shape[0]
    pairs = []
    for block, shift in zip(blocks, ctx_shifts(*shape)):
        owner = ctx_owner(place_ref, shift, -1, *shape)
        start = pl.multiple_of(owner * rows, rows)
        pairs.append((block, kv_ref.at[pl.ds(start, rows), :]))
    run_copies(pairs, sems)


def attention_kernel(q_ref, kv_ref, *refs):
    pk_ref, pq_ref, doc_i_ref, doc_j_ref = refs[:4]
    mix_ref, p_ref, to_ref, q_all = refs[4:]
    rows, width = q_ref.shape
    keys = kv_ref.shape[0]
    win = pk_ref.shape[1]
    heads = width // HEAD_DIM
    for head in range(heads):
        q = only_head(q_ref[...], head)
        q_all[head] = q
        to = dot(q, pk_ref[...], 1, 0)
        to = pltpu.roll(to, win + 1 - rows, 1, stride=1, stride_axis=0)
        to_ref[head] = to[:, :keys]
    doc_i = jnp.broadcast_to(doc_i_ref[...].astype(F32), (rows, rows)).T
    mix = jnp.zeros((rows, width), F32)
    for head in range(heads):
        q = q_all[head]
        parts = []
        for start in range(0, keys, BLOCK):
            key_block = kv_ref[start : start + BLOCK, :width]
            first = win - 2 * BLOCK - start
            pq = only_head(pq_ref[:, first : first + 2 * BLOCK], head, 0)
            off = dot(key_block, pq, 1, 0)
            off = pltpu.roll(off, BLOCK, 1, stride=1, stride_axis=0)
            s = dot(q, key_block, 1, 1) + to_ref[head, :, start : start + BLOCK]
            s = s + off[:, :BLOCK].T
            same = doc_i == doc_j_ref[:, start : start + BLOCK]
            parts.append(jnp.where(same, s, NEG))
        s = jnp.concatenate(parts, axis=1)
        e = jnp.exp(s - jnp.max(s, axis=1, keepdims=True))
        p = (e / jnp.sum(e, axis=1, keepdims=True)).astype(BF16)
        p_ref[head] = p
        mix = jnp.where(head_mask(mix.shape, head), dot(p, kv_ref[:, width:], 1, 0), mix)
    mix_ref[...] = mix.astype(BF16)


def attended_kernel(skip, mix_ref, full_ref, part_ref):
    attn = full_ref[:, skip : skip + mix_ref.shape[1]]
    part_ref[...] = dot(mix_ref[...], attn, 1, 1).astype(BF16)


def feed_kernel(rows_of, skip, stream_ref, *refs):
    pieces, rest = refs[:4], refs[4:]
    vec_ref, full_ref = rest[:2]
    pre_ref, hidden_ref, low_ref, slope_ref, active_ref, part_ref = rest[2:]
    units = active_ref.shape[1]
    gain, bias = rows_of
    pre = stream_ref[...].astype(F32) + sum_pieces(pieces)
    pre_ref[...] = pre
    unit, _ = unit_of(pre)
    hidden = unit * vec_ref[gain : gain + 1, :] + vec_ref[bias : bias + 1, :]
    hidden_ref[...] = hidden
    low = hidden.astype(BF16)
    low_ref[...] = low
    inner = dot(low, full_ref[:, skip : skip + units], 1, 0)
    below = 0.5 * (1.0 + lax.erf(inner * math.sqrt(0.5)))
    bell = jnp.exp(-0.5 * inner * inner) * (1.0 / math.sqrt(2.0 * math.pi))
    slope_ref[...] = below + inner * bell
    active = (inner * below).astype(BF16)
    active_ref[...] = active
    out = full_ref[:, skip + units : skip + 2 * units]
    part_ref[...] = dot(active, out, 1, 1).astype(BF16)


def end_kernel(rows_of, hidden_ref, *refs):
    pieces, (vec_ref, pre_ref, out_ref) = refs[:4], refs[4:]
    gain, bias = rows_of
    pre = hidden_ref[...] + sum_pieces(pieces)
    pre_ref[...] = pre
    unit, _ = unit_of(pre)
    stream = unit * vec_ref[gain : gain + 1, :] + vec_ref[bias : bias + 1, :]
    out_ref[...] = stream.astype(BF16)


def column_sums(ref, first, second):
    ref[...] = jnp.zeros_like(ref)
    ref[0:1, :] = jnp.sum(first, axis=0, keepdims=True)
    ref[1:2, :] = jnp.sum(second, axis=0, keepdims=True)


def feed_back_kernel(gain, skip, has_pieces, grad_ref, *refs):
    pieces, rest = (refs[:4], refs[4:]) if has_pieces else ((), refs)
    pre_ref, vec_ref, slope_ref, full_ref = rest[:4]
    d_pre_ref, d_low_ref, d_inner_ref, part_ref, norm_ref = rest[4:]
    units = slope_ref.shape[1]
    grad = grad_ref[...].astype(F32)
    if has_pieces:
        grad = grad + sum_pieces(pieces)
    back, gain_terms = normalize_back(pre_ref[...], vec_ref[gain : gain + 1, :], grad)
    column_sums(norm_ref, gain_terms, grad)
    d_pre_ref[...] = back
    low = back.astype(BF16)
    d_low_ref[...] = low
    out = full_ref[:, skip + units : skip + 2 * units]
    inner = (dot(low, out, 1, 0) * slope_ref[...]).astype(BF16)
    d_inner_ref[...] = inner
    part_ref[...] = dot(inner, full_ref[:, skip : skip + units], 1, 1).astype(BF16)


def attention_back_kernel(gain, skip, scale, place_ref, *refs):
    pieces, rest = refs[:4], refs[4:]
    d_out_ref, pre_ref, vec_ref, full_ref, q_ref, kv_ref, pk_ref, pq_ref, p_ref = rest[:9]
    d_pre_ref, d_low_ref, dq_ref, dpk_ref, dpq_ref, norm_ref = rest[9:15]
    ds_all, to_all, dk_pos, dm_all, q_all, qr_all, dpq_sum, dkv = rest[-8:]
    dkv_refs = rest[15:-8]
    rows, width = q_ref.shape
    keys = kv_ref.shape[0]
    heads = width // HEAD_DIM
    win = pk_ref.shape[1]

    grad = d_out_ref[...] + sum_pieces(pieces)
    back, gain_terms = normalize_back(pre_ref[...], vec_ref[gain : gain + 1, :], grad)
    column_sums(norm_ref, gain_terms, grad)
    d_pre_ref[...] = back
    d_low = back.astype(BF16)
    d_low_ref[...] = d_low
    d_mixture = dot(d_low, full_ref[:, skip : skip + width], 1, 0)

    row = lax.broadcasted_iota(jnp.int32, (rows, rows), 0)
    col = lax.broadcasted_iota(jnp.int32, (rows, rows), 1)
    flip = jnp.where(row + col == rows - 1, 1.0, 0.0).astype(BF16)
    q_back = dot(flip, q_ref[...], 1, 0)
    content = jnp.zeros((rows, width), F32)
    position = jnp.zeros((rows, width), F32)
    dpq_sum[...] = jnp.zeros_like(dpq_sum)
    for head in range(heads):
        here = slice(head * rows, (head + 1) * rows)
        mask = head_mask((rows, width), head)
        dm = only_head(d_mixture, head)
        dm_all[here, :] = dm
        q_all[here, :] = only_head(q_ref[...], head)
        qr_all[here, :] = only_head(q_back, head)
        p = p_ref[head].astype(F32)
        da = dot(dm, kv_ref[:, width:], 1, 1)
        ds = (p * (da - jnp.sum(p * da, axis=1, keepdims=True))).astype(BF16)
        ds_all[here, :] = ds
        content = jnp.where(mask, dot(ds, kv_ref[:, :width], 1, 0), content)
        ds_back = dot(flip, ds, 1, 0)
        to = jnp.concatenate([ds_back, jnp.zeros((rows, win - keys), F32)], axis=1)
        to = pltpu.roll(to, 0, 1, stride=1, stride_axis=0).astype(BF16)
        to_all[here, :] = to
        position = jnp.where(mask, dot(to, pk_ref[...], 1, 1), position)
        for start in range(0, keys, BLOCK):
            off = ds_back[:, start : start + BLOCK].T
            off = jnp.concatenate([off, jnp.zeros((BLOCK, BLOCK), F32)], axis=1)
            off = pltpu.roll(off, 0, 1, stride=1, stride_axis=0).astype(BF16)
            key_block = only_head(kv_ref[start : start + BLOCK, :width], head)
            dpq_sum[start : start + 2 * BLOCK, :] += dot(off, key_block, 0, 0)
            more = dot(off, pq_ref[:, start : start + 2 * BLOCK], 1, 1)
            if head:
                more = jnp.where(
                    head_mask(more.shape, head), more, dk_pos[start : start + BLOCK, :]
                )
            dk_pos[start : start + BLOCK, :] = more
    high = position.astype(BF16)
    low = (position - high.astype(F32)).astype(BF16)
    dq = content + dot(flip, high, 1, 0) + dot(flip, low, 1, 0)
    dq_ref[...] = (scale * dq).astype(BF16)
    dkv[:, :width] = (dot(ds_all[...], q_all[...], 0, 0) + dk_pos[...]).astype(BF16)
    p_all = p_ref[...].reshape(heads * rows, keys)
    dkv[:, width:] = dot(p_all, dm_all[...], 0, 0).astype(BF16)
    x_count = len(dkv_refs)
    zl_count = keys // (rows * x_count)
    for shift, target in enumerate(dkv_refs):
        x = lax.rem(place_ref[1] + shift, x_count)
        for side in range(zl_count):
            zl = lax.rem(place_ref[2] + side, zl_count)
            start = pl.multiple_of((x * zl_count + zl) * rows, rows)
            target[side * rows : (side + 1) * rows, :] = dkv[pl.ds(start, rows), :]
    dpk_ref[...] = dot(to_all[...], qr_all[...], 0, 0).astype(BF16)
    dpq_ref[...] = (scale * dpq_sum[...]).astype(BF16)


def position_back_kernel(table_ref, dpk_ref, dpq_ref, low_ref, rows_ref):
    width = dpk_ref.shape[1]
    d_k = dot(table_ref[0], dpk_ref[...], 1, 0).astype(BF16)
    d_q = dot(table_ref[2], dpq_ref[...], 1, 0).astype(BF16)
    low_ref[:, :width] = d_q
    low_ref[:, width:] = d_k
    owners, step = rows_ref.shape[0], rows_ref.shape[1] // 2
    for owner in range(owners):
        rows_ref[owner, :step, :] = d_q[owner * step : (owner + 1) * step, :]
        rows_ref[owner, step:, :] = d_k[owner * step : (owner + 1) * step, :]


def picked_columns(ref, core, parts=2):
    run = ref.shape[1] // (2 * parts)
    picked = [ref[:, pl.ds(pl.multiple_of((2 * i + core) * run, run), run)] for i in range(parts)]
    return jnp.concatenate(picked, axis=1)


def scatter_kernel(own_core, names, place_ref, *refs):
    refs = list(refs)
    core = place_ref[3] if own_core else 1 - place_ref[3]
    parts = []
    for name in names:
        if name == "qkv":
            low_ref, all_ref, rel_ref, pos_ref = refs[:4]
            del refs[:4]
            value = dot(picked_columns(low_ref, core), all_ref[...], 0, 0)
            terms = dot(picked_columns(rel_ref, core), pos_ref[...], 0, 0)
            wide = pos_ref.shape[1]
            parts += [value[:, :wide] + terms, value[:, wide:]]
        elif name == "norm":
            hid = picked_columns(refs.pop(0), core)
            out = picked_columns(refs.pop(0), core)
            rows = jnp.concatenate([hid[0:1], out[0:1], hid[1:2], out[1:2]], axis=0)
            rows = jnp.concatenate([rows, jnp.zeros((LANES - 4, rows.shape[1]), F32)], axis=0)
            parts.append(rows.T)
        elif name == "pos":
            rows_ref = refs.pop(0)
            run = rows_ref.shape[0] // 4
            picked = [rows_ref[pl.ds((2 * i + core) * run, run)] for i in range(2)]
            picked = jnp.concatenate(picked, axis=0).astype(F32)
            parts.append(picked.reshape(-1, rows_ref.shape[2]))
        else:
            left, right = refs[:2]
            del refs[:2]
            parts.append(dot(picked_columns(left, core), right[...], 0, 0))
    if not own_core:
        out_ref = refs[0]
        at = 0
        for part in parts:
            out_ref[:, at : at + part.shape[1]] = part.astype(BF16)
            at += part.shape[1]
        return
    if len(refs) == 2:
        arrived, outs, scr = refs[0], (), refs[1]
    else:
        arrived, outs, scr = refs[0], refs[1:-1], refs[-1]
    at = 0
    for part in parts:
        cols = part.shape[1]
        scr[:, at : at + cols] = (part + arrived[:, at : at + cols].astype(F32)).astype(BF16)
        at += cols
    if not outs:
        return
    z_count = len(outs)
    own = scr.shape[0] // 16
    x_count = outs[0].shape[0] // own
    zl_count = scr.shape[0] // (own * x_count * 2)
    for shift, out_ref in enumerate(outs):
        z = lax.rem(place_ref[4] + shift, z_count)
        zh, zl = lax.div(z, zl_count), lax.rem(z, zl_count)
        for x in range(x_count):
            start = pl.multiple_of(((zh * x_count + x) * zl_count + zl) * own, own)
            out_ref[x * own : (x + 1) * own, :] = scr[pl.ds(start, own), :]


def middle_kernel(count, place_ref, *refs):
    pieces, outs, scr = refs[:count], refs[count:-1], refs[-1]
    total = pieces[0][...].astype(F32)
    for piece in pieces[1:]:
        total = total + piece[...].astype(F32)
    scr[...] = total.astype(BF16)
    own = outs[0].shape[0]
    for shift, out_ref in enumerate(outs):
        x = lax.rem(place_ref[1] + shift, len(outs))
        out_ref[...] = scr[pl.ds(pl.multiple_of(x * own, own), own), :]


def halves_kernel(count, *refs):
    pieces, (mine_ref, other_ref) = refs[:count], refs[count:]
    total = pieces[0][...].astype(F32)
    for piece in pieces[1:]:
        total = total + piece[...].astype(F32)
    rows = mine_ref.shape[0]
    mine_ref[...] = total[:rows, :]
    other_ref[...] = total[rows:, :].astype(BF16)


def stream_back_kernel(skip, dq_ref, mine_ref, other_ref, qkv_ref, all_ref, part_ref):
    total = mine_ref[...] + other_ref[...].astype(F32)
    both = jnp.concatenate([dq_ref[...], total.astype(BF16)], axis=1)
    all_ref[...] = both
    qkv = qkv_ref[:, skip : skip + both.shape[1]]
    part_ref[...] = dot(both, qkv, 1, 1).astype(BF16)


def total_of(refs, first, cols):
    total = refs[0][:, first : first + cols].astype(F32)
    for ref in refs[1:]:
        total = total + ref[:, first : first + cols].astype(F32)
    return total


def total_kernel(*refs):
    refs[-1][...] = total_of(refs[:-1], 0, refs[-1].shape[1])


def groups_of(counts, refs):
    return [refs[sum(counts[:i]) : sum(counts[: i + 1])] for i in range(len(counts))]


def early_end_kernel(counts, firsts, *refs):
    in_ref, out_ref = refs[-2:]
    hidden = in_ref.shape[2]
    for layer, pieces in enumerate(groups_of(counts, refs)):
        in_ref[layer] = total_of(pieces, firsts[layer], hidden)
        out_ref[layer] = total_of(pieces, firsts[layer] + hidden, hidden)


def middle_end_kernel(counts, firsts, *refs):
    attn_ref, gain_ref, bias_ref = refs[-3:]
    width = attn_ref.shape[2]
    for layer, pieces in enumerate(groups_of(counts, refs)):
        attn_ref[layer] = total_of(pieces, firsts[layer], width)
        norms = total_of(pieces, firsts[layer] + width, LANES).T
        gain_ref[layer] = norms[0:2, :]
        bias_ref[layer] = norms[2:4, :]


def late_end_kernel(counts, *refs):
    out_ref = refs[-1]
    width = out_ref.shape[3]
    for layer, pieces in enumerate(groups_of(counts, refs)):
        for i in range(3):
            out_ref[layer, i] = total_of(pieces, i * width, width)


def relative_term_kernel(counts, firsts, skips, width, *refs):
    out_ref = refs[-1]
    layers = len(counts)
    total = None
    for layer, pieces in enumerate(groups_of(counts, refs)):
        qkv_ref, skip = refs[sum(counts) + layer], skips[layer]
        moved = total_of(pieces, firsts[layer], width).astype(BF16)
        step = moved.shape[0] // 2
        term = dot(moved[:step], qkv_ref[:, skip : skip + width], 1, 1)
        term = term + dot(moved[step:], qkv_ref[:, skip + width : skip + 2 * width], 1, 1)
        total = term if total is None else total + term
    out_ref[...] = total


def token_end_kernel(grad_ref, *refs):
    refs[-1][...] = (grad_ref[...] + sum_pieces(refs[:-1])).astype(BF16)


def relative_end_kernel(gain, *refs):
    pieces, (rel_ref, vec_ref, grad_ref, ends_ref) = refs[:4], refs[4:]
    d_rel = sum_pieces(pieces)
    back, gain_terms = normalize_back(
        rel_ref[...].astype(F32), vec_ref[gain : gain + 1, :], d_rel
    )
    grad_ref[...] = back
    owners, _, own = ends_ref.shape
    for k, terms in enumerate((gain_terms, d_rel)):
        sums = jnp.sum(terms, axis=0, keepdims=True)
        for owner in range(owners):
            first = owner * own // LANES * LANES
            chunk = sums[:, first : first + LANES]
            offset = owner * own - first
            if offset:
                chunk = pltpu.roll(chunk, LANES - offset, 1)
            ends_ref[owner, k : k + 1, :] = chunk[:, :own]


def shifted(values, axes, shift):
    count = lax.axis_size(axes)
    return lax.ppermute(values, axes, [(i, (i + shift) % count) for i in range(count)])


def along(run, values, axes):
    pieces = moved_on([values] * lax.axis_size(axes), axes)
    rows, cols = values.shape
    (out,) = run(
        functools.partial(stack_kernel, len(pieces)),
        [((len(pieces) * rows, cols), BF16)],
        pieces,
        name="stack",
    )
    return out


def ctx_shifted(values):
    x_count, zl_count = lax.axis_size("x"), lax.axis_size("zl")
    shifts = ctx_shifts(x_count, zl_count)
    moved = [values[0]]
    for i in reversed(range(1, len(shifts))):
        dx, dz = shifts[i]
        pairs = []
        for x in range(x_count):
            for z in range(zl_count):
                target = (x + dx) % x_count * zl_count + (z + dz) % zl_count
                pairs.append((x * zl_count + z, target))
        moved.insert(1, lax.ppermute(values[i], CTX, pairs))
    return moved


def tp_pieces(low):
    count = lax.axis_size("tp")
    order = sorted(range(1, count), key=lambda s: -min(s, count - s))
    moved = {s: shifted(low, "tp", s) for s in order}
    return [low] + [moved[s] for s in range(1, count)]


def moved_on(pieces, axes):
    count = len(pieces)
    order = sorted(range(1, count), key=lambda s: -min(s, count - s))
    moved = {s: shifted(pieces[s], axes, s) for s in order}
    return [pieces[0]] + [moved[s] for s in range(1, count)]


def local(
    tokens,
    cotangent,
    w_qkv,
    w_attn,
    w_in,
    w_out,
    ln_gain,
    ln_bias,
    rel_emb,
    rel_gain,
    rel_bias,
    doc_ids,
    rel_bucket,
):
    _, rows, model = tokens.shape
    layers, _, own, width = w_qkv.shape
    hidden_units = w_in.shape[2]
    heads = width // HEAD_DIM
    ctx_count = lax.axis_size(CTX)
    owners = lax.axis_size(OWNERS)
    length = rows * ctx_count
    row_start = lax.axis_index(CTX) * rows
    scale = 1.0 / math.sqrt(3.0 * HEAD_DIM)
    win = length + rows
    rel_own = rel_emb.shape[0]
    buckets = rel_own * owners
    wide = 3 * width

    shape = (lax.axis_size("x"), lax.axis_size("zl"))
    dims = (lax.axis_size("core"), lax.axis_size(ZED), *shape, own)
    place = [("zh", "core"), "x", "zl", "core", ZED]
    place = jnp.stack([lax.axis_index(axes) for axes in place]).astype(jnp.int32)
    dma = pltpu.SemaphoreType.DMA

    previous = []

    def run(*args, **kwargs):
        outs = call(*args, after=tuple(previous), **kwargs)
        previous[:] = [outs[-1]]
        return outs

    attn_rows, out_rows = jnp.swapaxes(w_attn, 1, 2), jnp.swapaxes(w_out, 1, 2)
    start_cols = wide + width + model // 2 + LANES
    (start_pack,) = run(
        pack_start_kernel,
        [((own, start_cols), BF16)],
        [w_qkv, attn_rows, rel_emb, ln_gain, ln_bias, rel_gain[None], rel_bias[None], doc_ids],
        hbm=range(8),
        scratch=[
            pltpu.VMEM((LANES, LANES), F32),
            pltpu.VMEM(ln_gain.shape, BF16),
            pltpu.VMEM(ln_bias.shape, BF16),
            pltpu.VMEM((1, own), BF16),
            pltpu.VMEM((1, own), BF16),
            pltpu.VMEM((1, rows), jnp.int32),
            dma((11,)),
        ],
        name="pack_start",
    )
    arrays, index = [w_in, out_rows], [0, 0]
    feed_at, qkv_at, attn_at = [0], [0], [0]
    at = 2 * hidden_units
    for layer in range(1, layers):
        arrays += [w_qkv, w_qkv, w_qkv, attn_rows, w_in, out_rows]
        index += [(layer, 0), (layer, 1), (layer, 2), layer, layer, layer]
        qkv_at.append(at)
        attn_at.append(at + wide)
        feed_at.append(at + wide + width)
        at += wide + width + 2 * hidden_units
    (rest,) = run(
        functools.partial(pack_kernel, index),
        [((own, at), BF16)],
        arrays,
        hbm=range(len(arrays)),
        scratch=[dma((len(arrays),))],
        name="pack",
    )
    full = lax.all_gather(rest, OWNERS, axis=0, tiled=True)

    padded = jnp.pad(rel_bucket, (1, 1), mode="edge")
    to_index = lax.dynamic_slice_in_dim(padded, row_start, win, 0)
    from_index = lax.dynamic_slice_in_dim(padded, length - rows - row_start + 1, win, 0)
    index = jnp.stack([to_index[::-1], from_index[::-1], from_index])
    (tables,) = run(table_kernel, [((3, buckets, win), BF16)], [index], limit=8, name="tables")

    start_x = along(run, start_pack, "x")
    start_z = along(run, start_x, ZED)
    start_pieces = [start_z, shifted(start_z, "core", 1)]
    qkv, attn, small, q, key_value = run(
        functools.partial(start_kernel, dims, scale),
        [
            ((model, wide), BF16),
            ((model, width), BF16),
            ((model, LANES), BF16),
            ((rows, width), BF16),
            ((rows, 2 * width), BF16),
        ],
        [place, *start_pieces, tokens[0]],
        smem=(0,),
        anys=(1, 2),
        scratch=[dma((3 * owners,))],
        name="start",
    )
    rel_low, vecs, doc_j = run(
        functools.partial(relative_kernel, dims, layers),
        [((buckets, model), BF16), ((16, model), F32), ((1, length), F32)],
        [place, *start_pieces, small],
        smem=(0,),
        anys=(1, 2),
        scratch=[pltpu.VMEM((buckets, model), BF16), dma((2 * owners,))],
        name="relative",
    )
    qkvs = [qkv] + [full] * (layers - 1)
    attns = [attn] + [full] * (layers - 1)

    token_low = tokens[0]
    stream = token_low
    kept = []
    hidden, pieces = None, None
    tile = (rows, model)
    for layer in range(layers):
        if layer:
            pre_out, stream, stream_low, q, key_value = run(
                functools.partial(
                    project_kernel,
                    scale,
                    (2 * layer - 1, 2 * layers + 2 * layer - 1),
                    qkv_at[layer],
                ),
                [
                    (tile, F32),
                    (tile, F32),
                    (tile, BF16),
                    ((rows, width), BF16),
                    ((rows, 2 * width), BF16),
                ],
                [hidden, *pieces, vecs, qkvs[layer]],
                name="project",
            )
            kept[-1]["pre_out"] = pre_out
        else:
            stream_low = token_low
        blocks = ctx_shifted([key_value] * ctx_count)
        pk, pq_rev, pq = run(
            functools.partial(position_kernel, scale, qkv_at[layer]),
            [((width, win), BF16)] * 3,
            [rel_low, qkvs[layer], tables],
            name="position",
        )
        (kv,) = run(
            functools.partial(gather_kernel, shape),
            [((length, 2 * width), BF16)],
            [place, *blocks],
            smem=(0,),
            anys=range(1, 1 + ctx_count),
            scratch=[dma((ctx_count,))],
            name="gather",
        )
        mixture, p = run(
            attention_kernel,
            [((rows, width), BF16), ((heads, rows, length), BF16)],
            [q, kv, pk, pq_rev, doc_ids, doc_j],
            scratch=[
                pltpu.VMEM((heads, rows, length), F32),
                pltpu.VMEM((heads, rows, width), BF16),
            ],
            limit=16,
            name="attention",
        )
        (part,) = run(
            functools.partial(attended_kernel, attn_at[layer]),
            [(tile, BF16)],
            [mixture, attns[layer]],
            name="attended",
        )
        pre_hidden, hidden, hidden_low, slope, active, part = run(
            functools.partial(feed_kernel, (2 * layer, 2 * layers + 2 * layer), feed_at[layer]),
            [
                (tile, F32),
                (tile, F32),
                (tile, BF16),
                ((rows, hidden_units), F32),
                ((rows, hidden_units), BF16),
                (tile, BF16),
            ],
            [stream, *tp_pieces(part), vecs, full],
            name="feed",
        )
        pieces = tp_pieces(part)
        kept.append(
            dict(
                stream_low=stream_low,
                q=q,
                kv=kv,
                pk=pk,
                pq=pq,
                p=p,
                mixture=mixture,
                pre_hidden=pre_hidden,
                hidden_low=hidden_low,
                slope=slope,
                active=active,
            )
        )
    last = layers - 1
    pre_out, out_local = run(
        functools.partial(end_kernel, (2 * last + 1, 2 * layers + 2 * last + 1)),
        [(tile, F32), (tile, BF16)],
        [hidden, *pieces, vecs],
        name="end",
    )
    kept[-1]["pre_out"] = pre_out

    grad_parts = [cotangent[0]]
    z_count, x_count = lax.axis_size(ZED), lax.axis_size("x")

    def scatter_other(names, ins, cols, label):
        (other,) = run(
            functools.partial(scatter_kernel, False, names),
            [((model // 2, cols), BF16)],
            [place, *ins],
            smem=(0,),
            limit=12,
            name=label + "_other",
        )
        return shifted(other, "core", 1)

    def scatter_own(names, ins, arrived, label):
        half, cols = arrived.shape
        pieces = run(
            functools.partial(scatter_kernel, True, names),
            [((half // z_count, cols), BF16)] * z_count,
            [place, *ins, arrived],
            smem=(0,),
            scratch=[pltpu.VMEM((half, cols), BF16)],
            limit=12,
            name=label + "_own",
        )
        return moved_on(pieces, ZED)

    def scatter_middle(pieces, label):
        rows_here, cols = pieces[0].shape
        pieces = run(
            functools.partial(middle_kernel, len(pieces)),
            [((rows_here // x_count, cols), BF16)] * x_count,
            [place, *pieces],
            smem=(0,),
            scratch=[pltpu.VMEM((rows_here, cols), BF16)],
            name=label + "_middle",
        )
        return moved_on(pieces, "x")

    def scatter_total(pieces, label):
        return list(run(total_kernel, [(pieces[0].shape, F32)], pieces, name=label + "_total"))

    early_names, early_cols = ("in", "out"), 2 * hidden_units
    middle_names, middle_cols = ("attn", "norm", "pos"), 2 * width + LANES
    late_names, late_cols = ("qkv",), wide
    both_names, both_cols = late_names + middle_names, late_cols + middle_cols
    early_sums, middle_sums, late_sums = [None] * layers, [None] * layers, [None] * layers
    both = None
    for layer in reversed(range(layers)):
        k = kept[layer]
        d_pre_out, d_out_low, d_inner, part, norm_out = run(
            functools.partial(
                feed_back_kernel, 2 * layer + 1, feed_at[layer], len(grad_parts) > 1
            ),
            [
                (tile, F32),
                (tile, BF16),
                ((rows, hidden_units), BF16),
                (tile, BF16),
                ((8, model), F32),
            ],
            [*grad_parts, k["pre_out"], vecs, k["slope"], full],
            name="feed_back",
        )
        pieces = tp_pieces(part)
        early_in = [k["hidden_low"], d_inner, d_out_low, k["active"]]
        arrived = scatter_other(early_names, early_in, early_cols, "early")
        if both is not None:
            both = scatter_middle(both, "late")
        early = scatter_own(early_names, early_in, arrived, "early")
        backs = run(
            functools.partial(attention_back_kernel, 2 * layer, attn_at[layer], scale),
            [
                (tile, F32),
                (tile, BF16),
                ((rows, width), BF16),
                ((win, width), BF16),
                ((win, width), BF16),
                ((8, model), F32),
            ]
            + [((length // x_count, 2 * width), BF16)] * x_count,
            [place, *pieces, d_pre_out, k["pre_hidden"], vecs, attns[layer]]
            + [k["q"], k["kv"], k["pk"], k["pq"], k["p"]],
            smem=(0,),
            scratch=[
                pltpu.VMEM((heads * rows, length), BF16),
                pltpu.VMEM((heads * rows, win), BF16),
                pltpu.VMEM((length, width), F32),
                pltpu.VMEM((heads * rows, width), BF16),
                pltpu.VMEM((heads * rows, width), BF16),
                pltpu.VMEM((heads * rows, width), BF16),
                pltpu.VMEM((win, width), F32),
                pltpu.VMEM((length, 2 * width), BF16),
            ],
            limit=20,
            name="attention_back",
        )
        d_pre_hidden, d_attended, dq, dpk, dpq, norm_hidden = backs[:6]
        dkv = moved_on(backs[6:], "x")
        pos_low, pos_rows = run(
            position_back_kernel,
            [((buckets, 2 * width), BF16), ((owners, 2 * rel_own, width), BF16)],
            [tables, dpk, dpq],
            name="position_back",
        )
        middle_in = [d_attended, k["mixture"], norm_hidden, norm_out, pos_rows]
        if both is not None:
            both = scatter_total(both, "late")
            middle_sums[layer + 1] = late_sums[layer + 1] = both
        if layer:
            early = scatter_middle(early, "early")
        else:
            arrived = scatter_other(middle_names, middle_in, middle_cols, "middle")
            middle = scatter_own(middle_names, middle_in, arrived, "middle")
            early = scatter_middle(early, "early")
        mine, other = run(
            functools.partial(halves_kernel, x_count),
            [((rows, 2 * width), F32), ((rows, 2 * width), BF16)],
            dkv,
            name="halves",
        )
        other = shifted(other, "zl", 1)
        if not layer:
            middle_sums[layer] = scatter_middle(middle, "middle")
        dqkv, part = run(
            functools.partial(stream_back_kernel, qkv_at[layer]),
            [((rows, wide), BF16), (tile, BF16)],
            [dq, mine, other, qkvs[layer]],
            name="stream_back",
        )
        grad_parts = [d_pre_hidden] + tp_pieces(part)
        late_in = [k["stream_low"], dqkv, rel_low, pos_low]
        if layer:
            arrived = scatter_other(both_names, late_in + middle_in, both_cols, "late")
            early_sums[layer] = scatter_total(early, "early")
            both = scatter_own(both_names, late_in + middle_in, arrived, "late")
        else:
            arrived = scatter_other(late_names, late_in, late_cols, "late")
            early_sums[layer] = early
            late = scatter_own(late_names, late_in, arrived, "late")

    counts = [len(pieces) for pieces in middle_sums]
    (term,) = run(
        functools.partial(
            relative_term_kernel,
            counts,
            [width + LANES] + [wide + width + LANES] * (layers - 1),
            qkv_at,
            width,
        ),
        [((rel_own, model), F32)],
        sum(middle_sums, []) + qkvs,
        name="relative_term",
    )
    terms = tp_pieces(term)
    late_sums[0] = scatter_middle(late, "late")
    grad_rel, ends = run(
        functools.partial(relative_end_kernel, 4 * layers),
        [((rel_own, model), F32), ((owners, 2, own), F32)],
        [*terms, rel_emb, vecs],
        name="relative_end",
    )
    ends = lax.all_to_all(ends, OWNERS, 0, 0)
    (grad_tokens,) = run(token_end_kernel, [(tile, BF16)], grad_parts, name="token_end")
    grad_in, grad_out = run(
        functools.partial(early_end_kernel, [len(p) for p in early_sums], [0] * layers),
        [((layers, own, hidden_units), F32)] * 2,
        sum(early_sums, []),
        name="early_end",
    )
    grad_attn, grad_gain, grad_bias = run(
        functools.partial(middle_end_kernel, counts, [0] + [wide] * (layers - 1)),
        [((layers, own, width), F32), ((layers, 2, own), F32), ((layers, 2, own), F32)],
        sum(middle_sums, []),
        name="middle_end",
    )
    (grad_qkv,) = run(
        functools.partial(late_end_kernel, [len(p) for p in late_sums]),
        [((layers, 3, own, width), F32)],
        sum(late_sums, []),
        name="late_end",
    )
    grad_attn, grad_out = jnp.swapaxes(grad_attn, 1, 2), jnp.swapaxes(grad_out, 1, 2)
    ends = jnp.sum(ends, axis=0)
    return (
        out_local[None],
        grad_tokens[None],
        grad_qkv,
        grad_attn,
        grad_in,
        grad_out,
        grad_gain,
        grad_bias,
        grad_rel,
        ends[0],
        ends[1],
    )


def solution(mesh):
    sizes = mesh.shape
    zh, zl = 2, 2
    finer = Mesh(
        mesh.devices.reshape(zh, sizes["fsdp"] // zh, sizes["ctx"] // zl, zl, sizes["tp"]),
        ("zh", "core", "x", "zl", "tp"),
    )
    own = OWNERS
    fsdp = ("zh", "core")
    return jax.shard_map(
        local,
        mesh=finer,
        in_specs=(
            P(fsdp, CTX, None),
            P(fsdp, CTX, None),
            P(None, None, own, "tp"),
            P(None, "tp", own),
            P(None, own, "tp"),
            P(None, "tp", own),
            P(None, None, own),
            P(None, None, own),
            P(own, None),
            P(own),
            P(own),
            P(fsdp, CTX),
            P(),
        ),
        out_specs=(
            P(fsdp, CTX, None),
            P(fsdp, CTX, None),
            P(None, None, own, "tp"),
            P(None, "tp", own),
            P(None, own, "tp"),
            P(None, "tp", own),
            P(None, None, own),
            P(None, None, own),
            P(own, None),
            P(own),
            P(own),
        ),
        check_vma=False,
    )
```

```python
import functools
import math

import jax
import jax.numpy as jnp
from jax import lax
from jax.experimental import pallas as pl
from jax.experimental.pallas import tpu as pltpu
from jax.sharding import Mesh
from jax.sharding import PartitionSpec as P

HEAD_DIM = 64
EPS = 1e-07
NEG = -1e30
BLOCK = 128
LANES = 128
START_WAY = (True, 0)
F32 = jnp.float32
BF16 = jnp.bfloat16
CTX = ("x", "zl")
ZED = ("zh", "zl")
PLANE = ("zh", "x", "zl")
OWNERS = ("zh", "core", "x", "zl")


def dot(a, b, ca, cb):
    return lax.dot_general(a, b, (((ca,), (cb,)), ((), ())), preferred_element_type=F32)


def call(body, outs, ins, *, anys=(), hbm=(), smem=(), scratch=(), after=(), limit=8, name=None):
    specs = []
    for i in range(len(ins)):
        space = pltpu.VMEM
        if i in anys:
            space = pl.ANY
        if i in hbm:
            space = pltpu.HBM
        if i in smem:
            space = pltpu.SMEM
        specs.append(pl.BlockSpec(memory_space=space))
    count, late = len(ins), len(after)
    specs += [pl.BlockSpec(memory_space=pl.ANY)] * late
    ins = [
        pltpu.with_memory_space_constraint(value, pltpu.HBM) if i in hbm else value
        for i, value in enumerate(ins)
    ]

    def without(*refs):
        body(*refs[:count], *refs[count + late :])

    return pl.pallas_call(
        without,
        in_specs=specs,
        out_specs=tuple(pl.BlockSpec(memory_space=pltpu.VMEM) for _ in outs),
        out_shape=tuple(jax.ShapeDtypeStruct(shape, dtype) for shape, dtype in outs),
        scratch_shapes=list(scratch),
        compiler_params=pltpu.CompilerParams(vmem_limit_bytes=limit << 20),
        name=name,
    )(*ins, *after)


def ctx_shifts(x_count, zl_count):
    pairs = [(dx, dz) for dx in range(x_count) for dz in range(zl_count)]
    return sorted(pairs, key=lambda p: (min(p[0], x_count - p[0]) + p[1], p[1], p[0]))


def ctx_owner(place_ref, shift, sign, x_count, zl_count):
    x = lax.rem(place_ref[1] + (sign * shift[0]) % x_count, x_count)
    zl = lax.rem(place_ref[2] + (sign * shift[1]) % zl_count, zl_count)
    return x * zl_count + zl


def head_mask(shape, head, axis=1):
    index = lax.broadcasted_iota(jnp.int32, shape, axis)
    return (index >= head * HEAD_DIM) & (index < (head + 1) * HEAD_DIM)


def only_head(values, head, axis=1):
    mask = head_mask(values.shape, head, axis)
    return jnp.where(mask, values.astype(F32), 0.0).astype(BF16)


def unit_of(values):
    average = jnp.mean(values, axis=-1, keepdims=True)
    centered = values - average
    spread = jnp.mean(centered * centered, axis=-1, keepdims=True)
    inverse = lax.rsqrt(spread + EPS)
    return centered * inverse, inverse


def normalize_back(values, gain_vec, grad):
    unit, inverse = unit_of(values)
    scaled = grad * gain_vec
    back = (
        scaled
        - jnp.mean(scaled, axis=-1, keepdims=True)
        - unit * jnp.mean(scaled * unit, axis=-1, keepdims=True)
    ) * inverse
    return back, grad * unit


def sum_pieces(pieces):
    parts = [piece[...].astype(F32) for piece in pieces]
    return (parts[0] + parts[2]) + (parts[1] + parts[3])


def run_copies(pairs, sems):
    copies = [
        pltpu.make_async_copy(source, target, sems.at[i])
        for i, (source, target) in enumerate(pairs)
    ]
    for copy in copies:
        copy.start()
    for copy in copies:
        copy.wait()


def pack_start_kernel(rel_ref, gain_ref, bias_ref, rgain_ref, rbias_ref, doc_ref, *refs):
    out_ref, scr, gain, bias, rgain, rbias, doc, sems = refs[-8:]
    index, others, parts = refs[0], refs[1], refs[2:-8]
    parts, other_refs = parts[: -len(others)], parts[-len(others) :]
    layers, _, own = gain_ref.shape
    half = rel_ref.shape[1] // 2
    part = rel_ref.shape[0]
    pairs = [(gain_ref, gain), (bias_ref, bias), (rgain_ref, rgain), (rbias_ref, rbias)]
    pairs += [(doc_ref, doc)]
    at = 0
    for i in range(2):
        pairs.append(
            (
                rel_ref.at[:, pl.ds(i * half, half)],
                out_ref.at[pl.ds(i * part, part), pl.ds(LANES, half)],
            )
        )
    taken = 0
    for leads, target, at in [(index, out_ref, LANES + half)] + [
        (leads, target, 0) for leads, target in zip(others, other_refs)
    ]:
        for lead, ref in zip(leads, parts[taken:]):
            cols = ref.shape[-1]
            pairs.append((ref.at[lead], target.at[:, pl.ds(at, cols)]))
            at += cols
        taken += len(leads)
    run_copies(pairs, sems)
    scr[...] = jnp.zeros_like(scr)
    for layer in range(layers):
        scr[2 * layer : 2 * layer + 2, :own] = gain[layer].astype(F32)
        base = 2 * layers + 2 * layer
        scr[base : base + 2, :own] = bias[layer].astype(F32)
    scr[4 * layers : 4 * layers + 1, :own] = rgain[...].astype(F32)
    scr[4 * layers + 1 : 4 * layers + 2, :own] = rbias[...].astype(F32)
    small = scr[...].T[:own, :]
    row = lax.broadcasted_iota(jnp.int32, small.shape, 0)
    upper = lax.broadcasted_iota(jnp.int32, small.shape, 1) >= LANES // 2
    doc_row = doc[...].astype(F32)
    turned = pltpu.roll(doc_row, LANES // 2, 1)
    small = jnp.where(upper & (row == 0), turned, small)
    small = jnp.where(upper & (row == 1), doc_row, small)
    out_ref[:, :LANES] = small.astype(BF16)


def ring_order(place, pairing):
    even = place + 1 - 2 * lax.rem(place, 2)
    odd = 3 - place
    if pairing:
        return [place, odd, even, 3 - even]
    return [place, even, odd, odd + 1 - 2 * lax.rem(odd, 2)]


def assemble(dims, way, place_ref, pieces, moves, sems):
    core_count, x_count, zh_count, zl_count, own = dims
    x_first, pairing = way
    core = place_ref[3]
    xs, zs = ring_order(place_ref[1], pairing), ring_order(place_ref[4], pairing)
    pairs = []
    for c_shift, piece in enumerate(pieces):
        from_c = lax.rem(core + c_shift, core_count)
        for i, z in enumerate(zs):
            zh, zl = lax.div(z, zl_count), lax.rem(z, zl_count)
            for j, x in enumerate(xs):
                owner = ((zh * core_count + from_c) * x_count + x) * zl_count + zl
                place = (i * x_count + j if x_first else j * len(zs) + i) * own
                for row, rows, col, cols, target, step, to_col in moves:
                    start = pl.multiple_of(owner * step, step)
                    pairs.append(
                        (
                            piece.at[pl.ds(place + row, rows), pl.ds(col, cols)],
                            target.at[pl.ds(start, rows), pl.ds(to_col, cols)],
                        )
                    )
    run_copies(pairs, sems)


def stack_kernel(one_ref, two_ref, out_ref):
    rows = one_ref.shape[0]
    out_ref[:rows, :] = one_ref[...]
    out_ref[rows:, :] = two_ref[...]


def rest_kernel(dims, way, columns, place_ref, one_ref, two_ref, *refs):
    targets, sems = refs[:-1], refs[-1]
    own = dims[-1]
    moves = [
        (0, own, first, target.shape[1], target, own, 0)
        for first, target in zip(columns, targets)
    ]
    assemble(dims, way, place_ref, (one_ref, two_ref), moves, sems)


def start_kernel(dims, scale, columns, place_ref, tokens_ref, *refs):
    pieces, (qkv_ref, attn_ref, small_ref, q_ref, kv_ref, sems) = refs[:-6], refs[-6:]
    own = dims[-1]
    width = q_ref.shape[1]
    moves = [
        (0, own, first, target.shape[1], target, own, 0)
        for first, target in zip(columns, (qkv_ref, attn_ref, small_ref))
    ]
    assemble(dims, START_WAY, place_ref, pieces, moves, sems)
    low = tokens_ref[...]
    kv_ref[...] = dot(low, qkv_ref[:, width:], 1, 0).astype(BF16)
    q_ref[...] = (scale * dot(low, qkv_ref[:, :width], 1, 0)).astype(BF16)


def relative_kernel(dims, layers, place_ref, small_ref, *refs):
    pieces, (low_ref, unit_ref, vec_ref, doc_ref, rel, sems) = refs[:-6], refs[-6:]
    own = dims[-1]
    half = rel.shape[1] // 2
    part = own // 2
    moves = [(i * part, part, LANES, half, rel, part, i * half) for i in range(2)]
    assemble(dims, START_WAY, place_ref, pieces, moves, sems)
    turned = small_ref[...].astype(F32).T[: vec_ref.shape[0], :]
    vec_ref[...] = turned
    unit, _ = unit_of(rel[...].astype(F32))
    unit_ref[...] = unit
    gain, bias = turned[4 * layers : 4 * layers + 1], turned[4 * layers + 1 : 4 * layers + 2]
    low_ref[...] = (unit * gain + bias).astype(BF16)
    blocks = doc_ref.shape[1] // LANES
    span = blocks * own
    start = pl.multiple_of(place_ref[0] * span, span)
    mine = small_ref[pl.ds(start, span), :].astype(F32)
    upper = lax.broadcasted_iota(jnp.int32, (1, LANES), 1) >= LANES // 2
    for block in range(blocks):
        first = pltpu.roll(mine[block * own : block * own + 1, :], LANES // 2, 1)
        second = mine[block * own + 1 : block * own + 2, :]
        doc_ref[:, block * LANES : (block + 1) * LANES] = jnp.where(upper, second, first)


def table_kernel(index_ref, table_ref):
    count, buckets, win = table_ref.shape
    bucket = lax.broadcasted_iota(jnp.int32, (buckets, win), 0)
    for i in range(count):
        same = bucket == index_ref[i : i + 1, :]
        table_ref[i] = jnp.where(same, 1.0, 0.0).astype(BF16)


def position_kernel(scale, skip, rel_ref, qkv_ref, table_ref, pk_ref, pq_rev_ref, pq_ref):
    width = pk_ref.shape[0]
    pos_q = (scale * dot(rel_ref[...], qkv_ref[:, skip : skip + width], 1, 0)).astype(BF16)
    pos_k = dot(rel_ref[...], qkv_ref[:, skip + width : skip + 2 * width], 1, 0).astype(BF16)
    pk_ref[...] = dot(pos_k, table_ref[0], 0, 0).astype(BF16)
    pq_rev_ref[...] = dot(pos_q, table_ref[1], 0, 0).astype(BF16)
    pq_ref[...] = dot(pos_q, table_ref[2], 0, 0).astype(BF16)


def project_kernel(scale, rows_of, skip, hidden_ref, *refs):
    pieces, rest = refs[:4], refs[4:]
    vec_ref, qkv_ref, pre_ref, stream_ref, low_ref, q_ref, kv_ref = rest
    width = q_ref.shape[1]
    gain, bias = rows_of
    pre = hidden_ref[...] + sum_pieces(pieces)
    pre_ref[...] = pre
    unit, _ = unit_of(pre)
    stream = unit * vec_ref[gain : gain + 1, :] + vec_ref[bias : bias + 1, :]
    stream_ref[...] = stream
    low = stream.astype(BF16)
    low_ref[...] = low
    kv_ref[...] = dot(low, qkv_ref[:, skip + width : skip + 3 * width], 1, 0).astype(BF16)
    q_ref[...] = (scale * dot(low, qkv_ref[:, skip : skip + width], 1, 0)).astype(BF16)


def gather_kernel(shape, place_ref, *refs):
    blocks, kv_ref, sems = refs[:-2], refs[-2], refs[-1]
    rows = blocks[0].shape[0]
    pairs = []
    for block, shift in zip(blocks, ctx_shifts(*shape)):
        owner = ctx_owner(place_ref, shift, -1, *shape)
        start = pl.multiple_of(owner * rows, rows)
        pairs.append((block, kv_ref.at[pl.ds(start, rows), :]))
    run_copies(pairs, sems)


def attention_kernel(q_ref, kv_ref, *refs):
    pk_ref, pq_ref, doc_i_ref, doc_j_ref = refs[:4]
    mix_ref, p_ref, to_ref, q_all = refs[4:]
    rows, width = q_ref.shape
    keys = kv_ref.shape[0]
    win = pk_ref.shape[1]
    heads = width // HEAD_DIM
    for head in range(heads):
        q = only_head(q_ref[...], head)
        q_all[head] = q
        to = dot(q, pk_ref[...], 1, 0)
        to = pltpu.roll(to, win + 1 - rows, 1, stride=1, stride_axis=0)
        to_ref[head] = to[:, :keys]
    doc_i = jnp.broadcast_to(doc_i_ref[...].astype(F32), (rows, rows)).T
    mix = jnp.zeros((rows, width), F32)
    for head in range(heads):
        q = q_all[head]
        parts = []
        for start in range(0, keys, BLOCK):
            key_block = kv_ref[start : start + BLOCK, :width]
            first = win - 2 * BLOCK - start
            pq = only_head(pq_ref[:, first : first + 2 * BLOCK], head, 0)
            off = dot(key_block, pq, 1, 0)
            off = pltpu.roll(off, BLOCK, 1, stride=1, stride_axis=0)
            s = dot(q, key_block, 1, 1) + to_ref[head, :, start : start + BLOCK]
            s = s + off[:, :BLOCK].T
            same = doc_i == doc_j_ref[:, start : start + BLOCK]
            parts.append(jnp.where(same, s, NEG))
        s = jnp.concatenate(parts, axis=1)
        e = jnp.exp(s - jnp.max(s, axis=1, keepdims=True))
        p = (e / jnp.sum(e, axis=1, keepdims=True)).astype(BF16)
        p_ref[head] = p
        mix = jnp.where(head_mask(mix.shape, head), dot(p, kv_ref[:, width:], 1, 0), mix)
    mix_ref[...] = mix.astype(BF16)


def attended_kernel(skip, mix_ref, full_ref, part_ref):
    attn = full_ref[:, skip : skip + mix_ref.shape[1]]
    part_ref[...] = dot(mix_ref[...], attn, 1, 1).astype(BF16)


def feed_kernel(rows_of, stream_ref, *refs):
    pieces, rest = refs[:4], refs[4:]
    vec_ref, in_ref, out_ref = rest[:3]
    pre_ref, hidden_ref, low_ref, slope_ref, active_ref, part_ref = rest[3:]
    gain, bias = rows_of
    pre = stream_ref[...].astype(F32) + sum_pieces(pieces)
    pre_ref[...] = pre
    unit, _ = unit_of(pre)
    hidden = unit * vec_ref[gain : gain + 1, :] + vec_ref[bias : bias + 1, :]
    hidden_ref[...] = hidden
    low = hidden.astype(BF16)
    low_ref[...] = low
    inner = dot(low, in_ref[...], 1, 0)
    below = 0.5 * (1.0 + lax.erf(inner * math.sqrt(0.5)))
    bell = jnp.exp(-0.5 * inner * inner) * (1.0 / math.sqrt(2.0 * math.pi))
    slope_ref[...] = below + inner * bell
    active = (inner * below).astype(BF16)
    active_ref[...] = active
    part_ref[...] = dot(active, out_ref[...], 1, 1).astype(BF16)


def end_kernel(rows_of, hidden_ref, *refs):
    pieces, (vec_ref, pre_ref, out_ref) = refs[:4], refs[4:]
    gain, bias = rows_of
    pre = hidden_ref[...] + sum_pieces(pieces)
    pre_ref[...] = pre
    unit, _ = unit_of(pre)
    stream = unit * vec_ref[gain : gain + 1, :] + vec_ref[bias : bias + 1, :]
    out_ref[...] = stream.astype(BF16)


def column_sums(ref, first, second):
    ref[...] = jnp.zeros_like(ref)
    ref[0:1, :] = jnp.sum(first, axis=0, keepdims=True)
    ref[1:2, :] = jnp.sum(second, axis=0, keepdims=True)


def feed_back_kernel(gain, has_pieces, grad_ref, *refs):
    pieces, rest = (refs[:4], refs[4:]) if has_pieces else ((), refs)
    pre_ref, vec_ref, slope_ref, in_ref, out_ref = rest[:5]
    d_pre_ref, d_low_ref, d_inner_ref, part_ref, norm_ref = rest[5:]
    grad = grad_ref[...].astype(F32)
    if has_pieces:
        grad = grad + sum_pieces(pieces)
    back, gain_terms = normalize_back(pre_ref[...], vec_ref[gain : gain + 1, :], grad)
    column_sums(norm_ref, gain_terms, grad)
    d_pre_ref[...] = back
    low = back.astype(BF16)
    d_low_ref[...] = low
    inner = (dot(low, out_ref[...], 1, 0) * slope_ref[...]).astype(BF16)
    d_inner_ref[...] = inner
    part_ref[...] = dot(inner, in_ref[...], 1, 1).astype(BF16)


def attention_back_kernel(gain, skip, scale, place_ref, *refs):
    pieces, rest = refs[:4], refs[4:]
    d_out_ref, pre_ref, vec_ref, full_ref, q_ref, kv_ref, pk_ref, pq_ref, p_ref = rest[:9]
    d_pre_ref, d_low_ref, dq_ref, dpk_ref, dpq_ref, norm_ref = rest[9:15]
    ds_all, to_all, dk_pos, dm_all, q_all, qr_all, dpq_sum, dkv = rest[-8:]
    dkv_refs = rest[15:-8]
    rows, width = q_ref.shape
    keys = kv_ref.shape[0]
    heads = width // HEAD_DIM
    win = pk_ref.shape[1]

    grad = d_out_ref[...] + sum_pieces(pieces)
    back, gain_terms = normalize_back(pre_ref[...], vec_ref[gain : gain + 1, :], grad)
    column_sums(norm_ref, gain_terms, grad)
    d_pre_ref[...] = back
    d_low = back.astype(BF16)
    d_low_ref[...] = d_low
    d_mixture = dot(d_low, full_ref[:, skip : skip + width], 1, 0)

    row = lax.broadcasted_iota(jnp.int32, (rows, rows), 0)
    col = lax.broadcasted_iota(jnp.int32, (rows, rows), 1)
    flip = jnp.where(row + col == rows - 1, 1.0, 0.0).astype(BF16)
    q_back = dot(flip, q_ref[...], 1, 0)
    content = jnp.zeros((rows, width), F32)
    position = jnp.zeros((rows, width), F32)
    dpq_sum[...] = jnp.zeros_like(dpq_sum)
    for head in range(heads):
        here = slice(head * rows, (head + 1) * rows)
        mask = head_mask((rows, width), head)
        dm = only_head(d_mixture, head)
        dm_all[here, :] = dm
        q_all[here, :] = only_head(q_ref[...], head)
        qr_all[here, :] = only_head(q_back, head)
        p = p_ref[head].astype(F32)
        da = dot(dm, kv_ref[:, width:], 1, 1)
        ds = (p * (da - jnp.sum(p * da, axis=1, keepdims=True))).astype(BF16)
        ds_all[here, :] = ds
        content = jnp.where(mask, dot(ds, kv_ref[:, :width], 1, 0), content)
        ds_back = dot(flip, ds, 1, 0)
        to = jnp.concatenate([ds_back, jnp.zeros((rows, win - keys), F32)], axis=1)
        to = pltpu.roll(to, 0, 1, stride=1, stride_axis=0).astype(BF16)
        to_all[here, :] = to
        position = jnp.where(mask, dot(to, pk_ref[...], 1, 1), position)
        for start in range(0, keys, BLOCK):
            off = ds_back[:, start : start + BLOCK].T
            off = jnp.concatenate([off, jnp.zeros((BLOCK, BLOCK), F32)], axis=1)
            off = pltpu.roll(off, 0, 1, stride=1, stride_axis=0).astype(BF16)
            key_block = only_head(kv_ref[start : start + BLOCK, :width], head)
            dpq_sum[start : start + 2 * BLOCK, :] += dot(off, key_block, 0, 0)
            more = dot(off, pq_ref[:, start : start + 2 * BLOCK], 1, 1)
            if head:
                more = jnp.where(
                    head_mask(more.shape, head), more, dk_pos[start : start + BLOCK, :]
                )
            dk_pos[start : start + BLOCK, :] = more
    high = position.astype(BF16)
    low = (position - high.astype(F32)).astype(BF16)
    dq = content + dot(flip, high, 1, 0) + dot(flip, low, 1, 0)
    dq_ref[...] = (scale * dq).astype(BF16)
    dkv[:, :width] = (dot(ds_all[...], q_all[...], 0, 0) + dk_pos[...]).astype(BF16)
    p_all = p_ref[...].reshape(heads * rows, keys)
    dkv[:, width:] = dot(p_all, dm_all[...], 0, 0).astype(BF16)
    x_count = len(dkv_refs)
    zl_count = keys // (rows * x_count)
    for shift, target in enumerate(dkv_refs):
        x = lax.rem(place_ref[1] + shift, x_count)
        for side in range(zl_count):
            zl = lax.rem(place_ref[2] + side, zl_count)
            start = pl.multiple_of((x * zl_count + zl) * rows, rows)
            target[side * rows : (side + 1) * rows, :] = dkv[pl.ds(start, rows), :]
    dpk_ref[...] = dot(to_all[...], qr_all[...], 0, 0).astype(BF16)
    dpq_ref[...] = (scale * dpq_sum[...]).astype(BF16)


def position_back_kernel(table_ref, dpk_ref, dpq_ref, low_ref, rows_ref):
    width = dpk_ref.shape[1]
    d_k = dot(table_ref[0], dpk_ref[...], 1, 0).astype(BF16)
    d_q = dot(table_ref[2], dpq_ref[...], 1, 0).astype(BF16)
    low_ref[:, :width] = d_q
    low_ref[:, width:] = d_k
    owners, step = rows_ref.shape[0], rows_ref.shape[1] // 2
    for owner in range(owners):
        rows_ref[owner, :step, :] = d_q[owner * step : (owner + 1) * step, :]
        rows_ref[owner, step:, :] = d_k[owner * step : (owner + 1) * step, :]


def relative_sums_kernel(unit_ref, *refs):
    out_ref = refs[-1]
    width = refs[0].shape[1] // 2
    total = None
    for pos_ref, qkv_ref in zip(refs[:-1:2], refs[1:-1:2]):
        term = dot(pos_ref[...], qkv_ref[:, : 2 * width], 1, 1)
        total = term if total is None else total + term
    column_sums(out_ref, total * unit_ref[...], total)


def picked_columns(ref, core, parts=2):
    run = ref.shape[1] // (2 * parts)
    picked = [ref[:, pl.ds(pl.multiple_of((2 * i + core) * run, run), run)] for i in range(parts)]
    return jnp.concatenate(picked, axis=1)


def scatter_kernel(own_core, names, x_first, place_ref, *refs):
    refs = list(refs)
    core = place_ref[3] if own_core else 1 - place_ref[3]
    parts = []
    for name in names:
        if name == "qkv":
            low_ref, all_ref, rel_ref, pos_ref = refs[:4]
            del refs[:4]
            value = dot(picked_columns(low_ref, core), all_ref[...], 0, 0)
            terms = dot(picked_columns(rel_ref, core), pos_ref[...], 0, 0)
            wide = pos_ref.shape[1]
            parts += [value[:, :wide] + terms, value[:, wide:]]
        elif name == "norm":
            hid = picked_columns(refs.pop(0), core)
            out = picked_columns(refs.pop(0), core)
            rel = picked_columns(refs.pop(0), core)
            rows = [hid[0:1], out[0:1], hid[1:2], out[1:2], rel[0:2]]
            rows.append(jnp.zeros((LANES - 6, hid.shape[1]), F32))
            rows = jnp.concatenate(rows, axis=0)
            parts.append(rows.T)
        elif name == "pos":
            rows_ref = refs.pop(0)
            run = rows_ref.shape[0] // 4
            picked = [rows_ref[pl.ds((2 * i + core) * run, run)] for i in range(2)]
            picked = jnp.concatenate(picked, axis=0).astype(F32)
            parts.append(picked.reshape(-1, rows_ref.shape[2]))
        else:
            left, right = refs[:2]
            del refs[:2]
            parts.append(dot(picked_columns(left, core), right[...], 0, 0))
    if not own_core:
        out_ref = refs[0]
        at = 0
        for part in parts:
            out_ref[:, at : at + part.shape[1]] = part.astype(BF16)
            at += part.shape[1]
        return
    arrived, outs, scr = refs[0], refs[1:-1], refs[-1]
    if x_first is None:
        outs = ()
    at = 0
    for part in parts:
        cols = part.shape[1]
        scr[:, at : at + cols] = (part + arrived[:, at : at + cols].astype(F32)).astype(BF16)
        at += cols
    if not outs:
        return
    count = len(outs)
    own = outs[0].shape[0] // count
    zl_count = scr.shape[0] // (own * count * 2)
    for shift, out_ref in enumerate(outs):
        near = lax.rem(place_ref[1 if x_first else 4] + shift, count)
        for far in range(count):
            x, z = (near, far) if x_first else (far, near)
            zh, zl = lax.div(z, zl_count), lax.rem(z, zl_count)
            start = pl.multiple_of(((zh * count + x) * zl_count + zl) * own, own)
            out_ref[far * own : (far + 1) * own, :] = scr[pl.ds(start, own), :]


def middle_kernel(count, x_first, place_ref, *refs):
    pieces, outs, scr = refs[:count], refs[count:-1], refs[-1]
    total = pieces[0][...].astype(F32)
    for piece in pieces[1:]:
        total = total + piece[...].astype(F32)
    scr[...] = total.astype(BF16)
    own = outs[0].shape[0]
    for shift, out_ref in enumerate(outs):
        far = lax.rem(place_ref[4 if x_first else 1] + shift, len(outs))
        out_ref[...] = scr[pl.ds(pl.multiple_of(far * own, own), own), :]


def halves_kernel(count, *refs):
    pieces, (mine_ref, other_ref) = refs[:count], refs[count:]
    total = pieces[0][...].astype(F32)
    for piece in pieces[1:]:
        total = total + piece[...].astype(F32)
    rows = mine_ref.shape[0]
    mine_ref[...] = total[:rows, :]
    other_ref[...] = total[rows:, :].astype(BF16)


def stream_back_kernel(skip, dq_ref, mine_ref, other_ref, qkv_ref, all_ref, part_ref):
    total = mine_ref[...] + other_ref[...].astype(F32)
    both = jnp.concatenate([dq_ref[...], total.astype(BF16)], axis=1)
    all_ref[...] = both
    qkv = qkv_ref[:, skip : skip + both.shape[1]]
    part_ref[...] = dot(both, qkv, 1, 1).astype(BF16)


def total_of(refs, first, cols):
    total = refs[0][:, first : first + cols].astype(F32)
    for ref in refs[1:]:
        total = total + ref[:, first : first + cols].astype(F32)
    return total


def total_kernel(*refs):
    refs[-1][...] = total_of(refs[:-1], 0, refs[-1].shape[1])


def groups_of(counts, refs):
    return [refs[sum(counts[:i]) : sum(counts[: i + 1])] for i in range(len(counts))]


def early_end_kernel(counts, firsts, *refs):
    in_ref, out_ref = refs[-2:]
    hidden = in_ref.shape[2]
    for layer, pieces in enumerate(groups_of(counts, refs)):
        in_ref[layer] = total_of(pieces, firsts[layer], hidden)
        out_ref[layer] = total_of(pieces, firsts[layer] + hidden, hidden)


def middle_end_kernel(counts, firsts, *refs):
    attn_ref, gain_ref, bias_ref = refs[-3:]
    width = attn_ref.shape[2]
    for layer, pieces in enumerate(groups_of(counts, refs)):
        attn_ref[layer] = total_of(pieces, firsts[layer], width)
        norms = total_of(pieces, firsts[layer] + width, LANES).T
        gain_ref[layer] = norms[0:2, :]
        bias_ref[layer] = norms[2:4, :]


def late_end_kernel(firsts, early_first, late_ref, early_ref, qkv_ref, in_ref, out_ref):
    width, hidden = qkv_ref.shape[3], in_ref.shape[2]

    def total(first, cols):
        value = late_ref[0, :, first : first + cols].astype(F32)
        for i in range(1, late_ref.shape[0]):
            value = value + late_ref[i, :, first : first + cols].astype(F32)
        return value

    for layer, first in enumerate(firsts):
        for i in range(3):
            qkv_ref[layer, i] = total(first + i * width, width)
    in_ref[0] = total(early_first, hidden)
    out_ref[0] = total(early_first + hidden, hidden)
    in_ref[1] = early_ref[:, :hidden]
    out_ref[1] = early_ref[:, hidden:]


def relative_term_kernel(counts, firsts, skips, width, *refs):
    out_ref = refs[-1]
    layers = len(counts)
    total = None
    for layer, pieces in enumerate(groups_of(counts, refs)):
        qkv_ref, skip = refs[sum(counts) + layer], skips[layer]
        moved = total_of(pieces, firsts[layer], width).astype(BF16)
        step = moved.shape[0] // 2
        term = dot(moved[:step], qkv_ref[:, skip : skip + width], 1, 1)
        term = term + dot(moved[step:], qkv_ref[:, skip + width : skip + 2 * width], 1, 1)
        total = term if total is None else total + term
    out_ref[: total.shape[0], :] = total
    sums = total_of(groups_of(counts, refs)[0], firsts[0] - LANES, LANES).T
    rest = jnp.zeros((8, total.shape[1] - sums.shape[1]), F32)
    out_ref[total.shape[0] :, :] = jnp.concatenate([sums[:8], rest], axis=1)


def token_end_kernel(grad_ref, *refs):
    refs[-1][...] = (grad_ref[...] + sum_pieces(refs[:-1])).astype(BF16)


def relative_end_kernel(gain, *refs):
    pieces, (rel_ref, vec_ref, grad_ref, ends_ref) = refs[:4], refs[4:]
    total = sum_pieces(pieces)
    rows = rel_ref.shape[0]
    back, _ = normalize_back(
        rel_ref[...].astype(F32), vec_ref[gain : gain + 1, :], total[:rows]
    )
    grad_ref[...] = back
    ends_ref[...] = total[rows : rows + 8, :LANES]


def shifted(values, axes, shift):
    count = lax.axis_size(axes)
    return lax.ppermute(values, axes, [(i, (i + shift) % count) for i in range(count)])


def ctx_shifted(values):
    x_count, zl_count = lax.axis_size("x"), lax.axis_size("zl")
    shifts = ctx_shifts(x_count, zl_count)
    moved = [values[0]]
    for i in reversed(range(1, len(shifts))):
        dx, dz = shifts[i]
        pairs = []
        for x in range(x_count):
            for z in range(zl_count):
                target = (x + dx) % x_count * zl_count + (z + dz) % zl_count
                pairs.append((x * zl_count + z, target))
        moved.insert(1, lax.ppermute(values[i], CTX, pairs))
    return moved


def tp_pieces(low):
    count = lax.axis_size("tp")
    order = sorted(range(1, count), key=lambda s: -min(s, count - s))
    moved = {s: shifted(low, "tp", s) for s in order}
    return [low] + [moved[s] for s in range(1, count)]


def moved_on(pieces, axes):
    count = len(pieces)
    order = sorted(range(1, count), key=lambda s: -min(s, count - s))
    moved = {s: shifted(pieces[s], axes, s) for s in order}
    return [pieces[0]] + [moved[s] for s in range(1, count)]


def local(
    tokens,
    cotangent,
    w_qkv,
    w_attn,
    w_in,
    w_out,
    ln_gain,
    ln_bias,
    rel_emb,
    rel_gain,
    rel_bias,
    doc_ids,
    rel_bucket,
):
    _, rows, model = tokens.shape
    layers, _, own, width = w_qkv.shape
    hidden_units = w_in.shape[2]
    heads = width // HEAD_DIM
    ctx_count = lax.axis_size(CTX)
    owners = lax.axis_size(OWNERS)
    length = rows * ctx_count
    row_start = lax.axis_index(CTX) * rows
    scale = 1.0 / math.sqrt(3.0 * HEAD_DIM)
    win = length + rows
    rel_own = rel_emb.shape[0]
    buckets = rel_own * owners
    wide = 3 * width

    shape = (lax.axis_size("x"), lax.axis_size("zl"))
    x_count, z_count = lax.axis_size("x"), lax.axis_size(ZED)
    dims = (lax.axis_size("core"), x_count, lax.axis_size("zh"), lax.axis_size("zl"), own)
    plane = lax.axis_size(PLANE)
    place = [("zh", "core"), "x", "zl", "core", ZED]
    place = jnp.stack([lax.axis_index(axes) for axes in place]).astype(jnp.int32)
    dma = pltpu.SemaphoreType.DMA

    previous = []

    def run(*args, after=(), **kwargs):
        outs = call(*args, after=(*previous, *after), **kwargs)
        previous[:] = [outs[-1]]
        return outs

    attn_rows, out_rows = jnp.swapaxes(w_attn, 1, 2), jnp.swapaxes(w_out, 1, 2)
    table = [{"qkv0": wide, "attn0": width}, {"in0": hidden_units}, {"out0": hidden_units}, {}]
    for layer in range(1, layers):
        table[1]["qkv%d" % layer] = wide
        table[2]["in%d" % layer] = hidden_units
        table[3].update({"out%d" % layer: hidden_units, "attn%d" % layer: width})
    ways = [START_WAY, (True, 1), (False, 0), (False, 1)]
    sources = {"attn": attn_rows, "in": w_in, "out": out_rows}

    def listed(table, at):
        arrays, index, columns = [], [], {}
        for name, cols in table.items():
            kind, layer = name[:-1], int(name[-1])
            columns[name] = at
            at += cols
            if kind == "qkv":
                arrays += [w_qkv] * 3
                index += [(layer, i) for i in range(3)]
            else:
                arrays.append(sources[kind])
                index.append(layer)
        return arrays, index, columns, at

    one_arrays, one_index, one_at, one_cols = listed(table[0], LANES + model // 2)
    vectors = [rel_emb, ln_gain, ln_bias, rel_gain[None], rel_bias[None], doc_ids]

    found = {name: (0, at) for name, at in one_at.items()}
    arrays, other_index, sizes = list(one_arrays), [], []
    for lot in range(1, len(table)):
        more, index, columns, cols = listed(table[lot], 0)
        found.update({name: (lot, at) for name, at in columns.items()})
        arrays += more
        other_index.append(index)
        sizes.append(cols)

    def pack_start(*refs):
        pack_start_kernel(*refs[:6], one_index, other_index, *refs[6:])

    lots = run(
        pack_start,
        [((own, cols), BF16) for cols in sizes + [one_cols]],
        vectors + arrays,
        hbm=range(len(vectors) + len(arrays)),
        scratch=[
            pltpu.VMEM((LANES, LANES), F32),
            pltpu.VMEM(ln_gain.shape, BF16),
            pltpu.VMEM(ln_bias.shape, BF16),
            pltpu.VMEM((1, own), BF16),
            pltpu.VMEM((1, own), BF16),
            pltpu.VMEM((1, rows), jnp.int32),
            dma((7 + len(arrays),)),
        ],
        name="pack_start",
    )
    lots = [lots[-1], *lots[:-1]]

    padded = jnp.pad(rel_bucket, (1, 1), mode="edge")
    to_index = lax.dynamic_slice_in_dim(padded, row_start, win, 0)
    from_index = lax.dynamic_slice_in_dim(padded, length - rows - row_start + 1, win, 0)
    index = jnp.stack([to_index[::-1], from_index[::-1], from_index])
    (tables,) = run(table_kernel, [((3, buckets, win), BF16)], [index], limit=8, name="tables")

    def stack(one, two, after):
        rows_here, cols = one.shape
        return run(
            stack_kernel,
            [((2 * rows_here, cols), BF16)],
            [one, two],
            after=after,
            name="stack",
        )[0]

    even, odd = [(0, 1), (1, 0), (2, 3), (3, 2)], [(1, 2), (2, 1), (3, 0), (0, 3)]
    for step in range(4):
        moved = []
        for lot, (x_first, pairing) in zip(lots, ways):
            axes = "x" if x_first == (step < 2) else ZED
            moved.append(lax.ppermute(lot, axes, odd if pairing ^ (step % 2) else even))
        for i in range(len(lots)):
            lots[i] = stack(lots[i], moved[i], moved if i == 0 else ())
    for i in range(4):
        lots[i] = [lots[i], shifted(lots[i], "core", 1)]
    one_pieces = lots[0]
    qkv, attn, small, q, key_value = run(
        functools.partial(start_kernel, dims, scale, [one_at["qkv0"], one_at["attn0"], 0]),
        [
            ((model, wide), BF16),
            ((model, width), BF16),
            ((model, LANES), BF16),
            ((rows, width), BF16),
            ((rows, 2 * width), BF16),
        ],
        [place, tokens[0], *one_pieces],
        smem=(0,),
        anys=range(2, 2 + len(one_pieces)),
        scratch=[dma((3 * owners,))],
        name="start",
    )
    rel_low, rel_unit, vecs, doc_j = run(
        functools.partial(relative_kernel, dims, layers),
        [
            ((buckets, model), BF16),
            ((buckets, model), F32),
            ((16, model), F32),
            ((1, length), F32),
        ],
        [place, small, *one_pieces],
        smem=(0,),
        anys=range(2, 2 + len(one_pieces)),
        limit=16,
        scratch=[pltpu.VMEM((buckets, model), BF16), dma((2 * owners,))],
        name="relative",
    )

    def rest(names):
        lot = found[names[0]][0]
        return run(
            functools.partial(rest_kernel, dims, ways[lot], [found[name][1] for name in names]),
            [((model, table[lot][name]), BF16) for name in names],
            [place, *lots[lot]],
            smem=(0,),
            anys=(1, 2),
            scratch=[dma((len(names) * owners,))],
            name="rest",
        )

    qkvs, attns, ins, outs = [qkv], [attn], [], []

    token_low = tokens[0]
    stream = token_low
    kept = []
    hidden, pieces = None, None
    tile = (rows, model)
    for layer in range(layers):
        if layer:
            pre_out, stream, stream_low, q, key_value = run(
                functools.partial(
                    project_kernel,
                    scale,
                    (2 * layer - 1, 2 * layers + 2 * layer - 1),
                    0,
                ),
                [
                    (tile, F32),
                    (tile, F32),
                    (tile, BF16),
                    ((rows, width), BF16),
                    ((rows, 2 * width), BF16),
                ],
                [hidden, *pieces, vecs, qkvs[layer]],
                name="project",
            )
            kept[-1]["pre_out"] = pre_out
        else:
            stream_low = token_low
        blocks = ctx_shifted([key_value] * ctx_count)
        pk, pq_rev, pq = run(
            functools.partial(position_kernel, scale, 0),
            [((width, win), BF16)] * 3,
            [rel_low, qkvs[layer], tables],
            name="position",
        )
        (kv,) = run(
            functools.partial(gather_kernel, shape),
            [((length, 2 * width), BF16)],
            [place, *blocks],
            smem=(0,),
            anys=range(1, 1 + ctx_count),
            scratch=[dma((ctx_count,))],
            name="gather",
        )
        mixture, p = run(
            attention_kernel,
            [((rows, width), BF16), ((heads, rows, length), BF16)],
            [q, kv, pk, pq_rev, doc_ids, doc_j],
            scratch=[
                pltpu.VMEM((heads, rows, length), F32),
                pltpu.VMEM((heads, rows, width), BF16),
            ],
            limit=16,
            name="attention",
        )
        (part,) = run(
            functools.partial(attended_kernel, 0),
            [(tile, BF16)],
            [mixture, attns[layer]],
            name="attended",
        )
        pieces = tp_pieces(part)
        ins += rest(["in%d" % layer])
        outs += rest(["out%d" % layer])
        pre_hidden, hidden, hidden_low, slope, active, part = run(
            functools.partial(feed_kernel, (2 * layer, 2 * layers + 2 * layer)),
            [
                (tile, F32),
                (tile, F32),
                (tile, BF16),
                ((rows, hidden_units), F32),
                ((rows, hidden_units), BF16),
                (tile, BF16),
            ],
            [stream, *pieces, vecs, ins[layer], outs[layer]],
            name="feed",
        )
        pieces = tp_pieces(part)
        if layer + 1 < layers:
            qkvs += rest(["qkv%d" % (layer + 1)])
            attns += rest(["attn%d" % (layer + 1)])
        kept.append(
            dict(
                stream_low=stream_low,
                q=q,
                kv=kv,
                pk=pk,
                pq=pq,
                p=p,
                mixture=mixture,
                pre_hidden=pre_hidden,
                hidden_low=hidden_low,
                slope=slope,
                active=active,
            )
        )
    last = layers - 1
    pre_out, out_local = run(
        functools.partial(end_kernel, (2 * last + 1, 2 * layers + 2 * last + 1)),
        [(tile, F32), (tile, BF16)],
        [hidden, *pieces, vecs],
        name="end",
    )
    kept[-1]["pre_out"] = pre_out

    grad_parts = [cotangent[0]]
    x_count = lax.axis_size("x")

    def scatter_other(names, ins, cols, label):
        (other,) = run(
            functools.partial(scatter_kernel, False, names, False),
            [((model // 2, cols), BF16)],
            [place, *ins],
            smem=(0,),
            limit=16,
            name=label + "_other",
        )
        return shifted(other, "core", 1)

    def scatter_own(names, ins, arrived, label, x_first=False, after=()):
        half, cols = arrived.shape
        pieces = run(
            functools.partial(scatter_kernel, True, names, x_first),
            [((half // z_count, cols), BF16)] * z_count,
            [place, *ins, arrived],
            smem=(0,),
            scratch=[pltpu.VMEM((half, cols), BF16)],
            after=after,
            limit=16,
            name=label + "_own",
        )
        return moved_on(pieces, "x" if x_first else ZED)

    def scatter_middle(pieces, label, x_first=False):
        rows_here, cols = pieces[0].shape
        pieces = run(
            functools.partial(middle_kernel, len(pieces), x_first),
            [((rows_here // x_count, cols), BF16)] * x_count,
            [place, *pieces],
            smem=(0,),
            scratch=[pltpu.VMEM((rows_here, cols), BF16)],
            name=label + "_middle",
        )
        return moved_on(pieces, ZED if x_first else "x")

    def scatter_total(pieces, label):
        return list(run(total_kernel, [(pieces[0].shape, F32)], pieces, name=label + "_total"))

    early_names, early_cols = ("in", "out"), 2 * hidden_units
    middle_names, middle_cols = ("attn", "norm", "pos"), 2 * width + LANES
    early, middle_ins, late_ins, pos_lows = None, [], [], []
    for layer in reversed(range(layers)):
        k = kept[layer]
        d_pre_out, d_out_low, d_inner, part, norm_out = run(
            functools.partial(feed_back_kernel, 2 * layer + 1, len(grad_parts) > 1),
            [
                (tile, F32),
                (tile, BF16),
                ((rows, hidden_units), BF16),
                (tile, BF16),
                ((8, model), F32),
            ],
            [*grad_parts, k["pre_out"], vecs, k["slope"], ins[layer], outs[layer]],
            name="feed_back",
        )
        pieces = tp_pieces(part)
        early_in = [k["hidden_low"], d_inner, d_out_low, k["active"]]
        if layer:
            arrived = scatter_other(early_names, early_in, early_cols, "early")
            early = scatter_own(early_names, early_in, arrived, "early", True)
        else:
            early = scatter_total(early, "early")
        backs = run(
            functools.partial(attention_back_kernel, 2 * layer, 0, scale),
            [
                (tile, F32),
                (tile, BF16),
                ((rows, width), BF16),
                ((win, width), BF16),
                ((win, width), BF16),
                ((8, model), F32),
            ]
            + [((length // x_count, 2 * width), BF16)] * x_count,
            [place, *pieces, d_pre_out, k["pre_hidden"], vecs, attns[layer]]
            + [k["q"], k["kv"], k["pk"], k["pq"], k["p"]],
            smem=(0,),
            scratch=[
                pltpu.VMEM((heads * rows, length), BF16),
                pltpu.VMEM((heads * rows, win), BF16),
                pltpu.VMEM((length, width), F32),
                pltpu.VMEM((heads * rows, width), BF16),
                pltpu.VMEM((heads * rows, width), BF16),
                pltpu.VMEM((heads * rows, width), BF16),
                pltpu.VMEM((win, width), F32),
                pltpu.VMEM((length, 2 * width), BF16),
            ],
            limit=20,
            name="attention_back",
        )
        d_pre_hidden, d_attended, dq, dpk, dpq, norm_hidden = backs[:6]
        dkv = moved_on(backs[6:], "x")
        pos_low, pos_rows = run(
            position_back_kernel,
            [((buckets, 2 * width), BF16), ((owners, 2 * rel_own, width), BF16)],
            [tables, dpk, dpq],
            name="position_back",
        )
        pos_lows.append(pos_low)
        norm_rel = jnp.zeros((8, model), F32)
        if not layer:
            pairs = [item for pair in zip(pos_lows, qkvs[::-1]) for item in pair]
            (norm_rel,) = run(
                relative_sums_kernel,
                [((8, model), F32)],
                [rel_unit, *pairs],
                limit=16,
                name="relative_sums",
            )
        middle_ins += [d_attended, k["mixture"], norm_hidden, norm_out, norm_rel, pos_rows]
        if not layer:
            arrived = scatter_other(
                middle_names * layers, middle_ins, middle_cols * layers, "middle"
            )
        if layer:
            early = scatter_middle(early, "early", True)
        if not layer:
            middle = scatter_own(middle_names * layers, middle_ins, arrived, "middle")
        mine, other = run(
            functools.partial(halves_kernel, x_count),
            [((rows, 2 * width), F32), ((rows, 2 * width), BF16)],
            dkv,
            name="halves",
        )
        other = shifted(other, "zl", 1)
        if not layer:
            middle = scatter_middle(middle, "middle")
        dqkv, part = run(
            functools.partial(stream_back_kernel, 0),
            [((rows, wide), BF16), (tile, BF16)],
            [dq, mine, other, qkvs[layer]],
            name="stream_back",
        )
        grad_parts = [d_pre_hidden] + tp_pieces(part)
        late_ins += [k["stream_low"], dqkv, rel_low, pos_low]
    late_names, late_cols = ("qkv",) * layers + early_names, wide * layers + early_cols
    late_ins += early_in
    arrived = scatter_other(late_names, late_ins, late_cols, "late")
    middle_at = [(layers - 1 - layer) * middle_cols for layer in range(layers)]
    late_at = [(layers - 1 - layer) * wide for layer in range(layers)]

    counts = [len(middle)] * layers
    (term,) = run(
        functools.partial(
            relative_term_kernel,
            counts,
            [at + width + LANES for at in middle_at],
            [0] * layers,
            width,
        ),
        [((rel_own + 8, model), F32)],
        middle * layers + qkvs,
        name="relative_term",
    )
    terms = tp_pieces(term)
    (late,) = run(
        functools.partial(scatter_kernel, True, late_names, None),
        [((model // 2, late_cols), BF16)],
        [place, *late_ins, arrived],
        smem=(0,),
        limit=16,
        name="late_own",
    )
    late = lax.all_to_all(late.reshape(plane, own, late_cols), PLANE, 0, 0)
    grad_rel, ends = run(
        functools.partial(relative_end_kernel, 4 * layers),
        [((rel_own, model), F32), ((8, LANES), F32)],
        [*terms, rel_emb, vecs],
        name="relative_end",
    )
    (grad_tokens,) = run(token_end_kernel, [(tile, BF16)], grad_parts, name="token_end")
    grad_attn, grad_gain, grad_bias = run(
        functools.partial(middle_end_kernel, counts, middle_at),
        [((layers, own, width), F32), ((layers, 2, own), F32), ((layers, 2, own), F32)],
        middle * layers,
        name="middle_end",
    )
    grad_qkv, grad_in, grad_out = run(
        functools.partial(late_end_kernel, late_at, wide * layers),
        [
            ((layers, 3, own, width), F32),
            ((layers, own, hidden_units), F32),
            ((layers, own, hidden_units), F32),
        ],
        [late, *early],
        name="late_end",
    )
    grad_attn, grad_out = jnp.swapaxes(grad_attn, 1, 2), jnp.swapaxes(grad_out, 1, 2)
    return (
        out_local[None],
        grad_tokens[None],
        grad_qkv,
        grad_attn,
        grad_in,
        grad_out,
        grad_gain,
        grad_bias,
        grad_rel,
        ends[4, :own],
        ends[5, :own],
    )


def solution(mesh):
    sizes = mesh.shape
    zh, zl = 2, 2
    finer = Mesh(
        mesh.devices.reshape(zh, sizes["fsdp"] // zh, sizes["ctx"] // zl, zl, sizes["tp"]),
        ("zh", "core", "x", "zl", "tp"),
    )
    own = OWNERS
    fsdp = ("zh", "core")
    return jax.shard_map(
        local,
        mesh=finer,
        in_specs=(
            P(fsdp, CTX, None),
            P(fsdp, CTX, None),
            P(None, None, own, "tp"),
            P(None, "tp", own),
            P(None, own, "tp"),
            P(None, "tp", own),
            P(None, None, own),
            P(None, None, own),
            P(own, None),
            P(own),
            P(own),
            P(fsdp, CTX),
            P(),
        ),
        out_specs=(
            P(fsdp, CTX, None),
            P(fsdp, CTX, None),
            P(None, None, own, "tp"),
            P(None, "tp", own),
            P(None, own, "tp"),
            P(None, "tp", own),
            P(None, None, own),
            P(None, None, own),
            P(own, None),
            P(own),
            P(own),
        ),
        check_vma=False,
    )
```

```python
import functools
import math

import jax
import jax.numpy as jnp
from jax import lax
from jax.experimental import pallas as pl
from jax.experimental.pallas import tpu as pltpu
from jax.sharding import Mesh
from jax.sharding import PartitionSpec as P

HEAD_DIM = 64
EPS = 1e-07
NEG = -1e30
BLOCK = 128
LANES = 128
START_WAY = (True, 0)
F32 = jnp.float32
BF16 = jnp.bfloat16
CTX = ("x", "zl")
ZED = ("zh", "zl")
PLANE = ("zh", "x", "zl")
OWNERS = ("zh", "core", "x", "zl")


def dot(a, b, ca, cb):
    return lax.dot_general(a, b, (((ca,), (cb,)), ((), ())), preferred_element_type=F32)


def call(body, outs, ins, *, anys=(), hbm=(), smem=(), scratch=(), after=(), limit=8, name=None):
    specs = []
    for i in range(len(ins)):
        space = pltpu.VMEM
        if i in anys:
            space = pl.ANY
        if i in hbm:
            space = pltpu.HBM
        if i in smem:
            space = pltpu.SMEM
        specs.append(pl.BlockSpec(memory_space=space))
    count, late = len(ins), len(after)
    specs += [pl.BlockSpec(memory_space=pl.ANY)] * late
    ins = [
        pltpu.with_memory_space_constraint(value, pltpu.HBM) if i in hbm else value
        for i, value in enumerate(ins)
    ]

    def without(*refs):
        body(*refs[:count], *refs[count + late :])

    return pl.pallas_call(
        without,
        in_specs=specs,
        out_specs=tuple(pl.BlockSpec(memory_space=pltpu.VMEM) for _ in outs),
        out_shape=tuple(jax.ShapeDtypeStruct(shape, dtype) for shape, dtype in outs),
        scratch_shapes=list(scratch),
        compiler_params=pltpu.CompilerParams(vmem_limit_bytes=limit << 20),
        name=name,
    )(*ins, *after)


def ctx_shifts(x_count, zl_count):
    pairs = [(dx, dz) for dx in range(x_count) for dz in range(zl_count)]
    return sorted(pairs, key=lambda p: (min(p[0], x_count - p[0]) + p[1], p[1], p[0]))


def ctx_owner(place_ref, shift, sign, x_count, zl_count):
    x = lax.rem(place_ref[1] + (sign * shift[0]) % x_count, x_count)
    zl = lax.rem(place_ref[2] + (sign * shift[1]) % zl_count, zl_count)
    return x * zl_count + zl


def head_mask(shape, head, axis=1):
    index = lax.broadcasted_iota(jnp.int32, shape, axis)
    return (index >= head * HEAD_DIM) & (index < (head + 1) * HEAD_DIM)


def only_head(values, head, axis=1):
    mask = head_mask(values.shape, head, axis)
    return jnp.where(mask, values.astype(F32), 0.0).astype(BF16)


def unit_of(values):
    average = jnp.mean(values, axis=-1, keepdims=True)
    centered = values - average
    spread = jnp.mean(centered * centered, axis=-1, keepdims=True)
    inverse = lax.rsqrt(spread + EPS)
    return centered * inverse, inverse


def normalize_back(values, gain_vec, grad):
    unit, inverse = unit_of(values)
    scaled = grad * gain_vec
    back = (
        scaled
        - jnp.mean(scaled, axis=-1, keepdims=True)
        - unit * jnp.mean(scaled * unit, axis=-1, keepdims=True)
    ) * inverse
    return back, grad * unit


def sum_pieces(pieces):
    parts = [piece[...].astype(F32) for piece in pieces]
    return (parts[0] + parts[2]) + (parts[1] + parts[3])


def run_copies(pairs, sems):
    copies = [
        pltpu.make_async_copy(source, target, sems.at[i])
        for i, (source, target) in enumerate(pairs)
    ]
    for copy in copies:
        copy.start()
    for copy in copies:
        copy.wait()


def pack_start_kernel(rel_ref, gain_ref, bias_ref, rgain_ref, rbias_ref, doc_ref, *refs):
    out_ref, scr, gain, bias, rgain, rbias, doc, sems = refs[-8:]
    index, others, parts = refs[0], refs[1], refs[2:-8]
    parts, other_refs = parts[: -len(others)], parts[-len(others) :]
    layers, _, own = gain_ref.shape
    half = rel_ref.shape[1] // 2
    part = rel_ref.shape[0]
    pairs = [(gain_ref, gain), (bias_ref, bias), (rgain_ref, rgain), (rbias_ref, rbias)]
    pairs += [(doc_ref, doc)]
    at = 0
    for i in range(2):
        pairs.append(
            (
                rel_ref.at[:, pl.ds(i * half, half)],
                out_ref.at[pl.ds(i * part, part), pl.ds(LANES, half)],
            )
        )
    taken = 0
    for leads, target, at in [(index, out_ref, LANES + half)] + [
        (leads, target, 0) for leads, target in zip(others, other_refs)
    ]:
        for lead, ref in zip(leads, parts[taken:]):
            cols = ref.shape[-1]
            pairs.append((ref.at[lead], target.at[:, pl.ds(at, cols)]))
            at += cols
        taken += len(leads)
    run_copies(pairs, sems)
    scr[...] = jnp.zeros_like(scr)
    for layer in range(layers):
        scr[2 * layer : 2 * layer + 2, :own] = gain[layer].astype(F32)
        base = 2 * layers + 2 * layer
        scr[base : base + 2, :own] = bias[layer].astype(F32)
    scr[4 * layers : 4 * layers + 1, :own] = rgain[...].astype(F32)
    scr[4 * layers + 1 : 4 * layers + 2, :own] = rbias[...].astype(F32)
    small = scr[...].T[:own, :]
    row = lax.broadcasted_iota(jnp.int32, small.shape, 0)
    upper = lax.broadcasted_iota(jnp.int32, small.shape, 1) >= LANES // 2
    doc_row = doc[...].astype(F32)
    turned = pltpu.roll(doc_row, LANES // 2, 1)
    small = jnp.where(upper & (row == 0), turned, small)
    small = jnp.where(upper & (row == 1), doc_row, small)
    out_ref[:, :LANES] = small.astype(BF16)


def ring_order(place, pairing):
    even = place + 1 - 2 * lax.rem(place, 2)
    odd = 3 - place
    if pairing:
        return [place, odd, even, 3 - even]
    return [place, even, odd, odd + 1 - 2 * lax.rem(odd, 2)]


def assemble(dims, way, place_ref, pieces, moves, sems):
    core_count, x_count, zh_count, zl_count, own = dims
    x_first, pairing = way
    core = place_ref[3]
    xs, zs = ring_order(place_ref[1], pairing), ring_order(place_ref[4], pairing)
    pairs = []
    for c_shift, piece in enumerate(pieces):
        from_c = lax.rem(core + c_shift, core_count)
        for i, z in enumerate(zs):
            zh, zl = lax.div(z, zl_count), lax.rem(z, zl_count)
            for j, x in enumerate(xs):
                owner = ((zh * core_count + from_c) * x_count + x) * zl_count + zl
                place = (i * x_count + j if x_first else j * len(zs) + i) * own
                for row, rows, col, cols, target, step, to_col in moves:
                    start = pl.multiple_of(owner * step, step)
                    pairs.append(
                        (
                            piece.at[pl.ds(place + row, rows), pl.ds(col, cols)],
                            target.at[pl.ds(start, rows), pl.ds(to_col, cols)],
                        )
                    )
    run_copies(pairs, sems)


def stack_kernel(one_ref, two_ref, out_ref):
    rows = one_ref.shape[0]
    out_ref[:rows, :] = one_ref[...]
    out_ref[rows:, :] = two_ref[...]


def rest_kernel(dims, way, columns, place_ref, one_ref, two_ref, *refs):
    targets, sems = refs[:-1], refs[-1]
    own = dims[-1]
    moves = [
        (0, own, first, target.shape[1], target, own, 0)
        for first, target in zip(columns, targets)
    ]
    assemble(dims, way, place_ref, (one_ref, two_ref), moves, sems)


def start_kernel(dims, scale, columns, place_ref, tokens_ref, *refs):
    pieces, (qkv_ref, attn_ref, small_ref, q_ref, kv_ref, sems) = refs[:-6], refs[-6:]
    own = dims[-1]
    width = q_ref.shape[1]
    moves = [
        (0, own, first, target.shape[1], target, own, 0)
        for first, target in zip(columns, (qkv_ref, attn_ref, small_ref))
    ]
    assemble(dims, START_WAY, place_ref, pieces, moves, sems)
    low = tokens_ref[...]
    kv_ref[...] = dot(low, qkv_ref[:, width:], 1, 0).astype(BF16)
    q_ref[...] = (scale * dot(low, qkv_ref[:, :width], 1, 0)).astype(BF16)


def relative_kernel(dims, layers, place_ref, small_ref, *refs):
    pieces, (low_ref, unit_ref, vec_ref, doc_ref, rel, sems) = refs[:-6], refs[-6:]
    own = dims[-1]
    half = rel.shape[1] // 2
    part = own // 2
    moves = [(i * part, part, LANES, half, rel, part, i * half) for i in range(2)]
    assemble(dims, START_WAY, place_ref, pieces, moves, sems)
    turned = small_ref[...].astype(F32).T[: vec_ref.shape[0], :]
    vec_ref[...] = turned
    unit, _ = unit_of(rel[...].astype(F32))
    unit_ref[...] = unit
    gain, bias = turned[4 * layers : 4 * layers + 1], turned[4 * layers + 1 : 4 * layers + 2]
    low_ref[...] = (unit * gain + bias).astype(BF16)
    blocks = doc_ref.shape[1] // LANES
    span = blocks * own
    start = pl.multiple_of(place_ref[0] * span, span)
    mine = small_ref[pl.ds(start, span), :].astype(F32)
    upper = lax.broadcasted_iota(jnp.int32, (1, LANES), 1) >= LANES // 2
    for block in range(blocks):
        first = pltpu.roll(mine[block * own : block * own + 1, :], LANES // 2, 1)
        second = mine[block * own + 1 : block * own + 2, :]
        doc_ref[:, block * LANES : (block + 1) * LANES] = jnp.where(upper, second, first)


def table_kernel(index_ref, table_ref):
    count, buckets, win = table_ref.shape
    bucket = lax.broadcasted_iota(jnp.int32, (buckets, win), 0)
    for i in range(count):
        same = bucket == index_ref[i : i + 1, :]
        table_ref[i] = jnp.where(same, 1.0, 0.0).astype(BF16)


def position_kernel(scale, skip, rel_ref, qkv_ref, table_ref, pk_ref, pq_rev_ref, pq_ref):
    width = pk_ref.shape[0]
    pos_q = (scale * dot(rel_ref[...], qkv_ref[:, skip : skip + width], 1, 0)).astype(BF16)
    pos_k = dot(rel_ref[...], qkv_ref[:, skip + width : skip + 2 * width], 1, 0).astype(BF16)
    pk_ref[...] = dot(pos_k, table_ref[0], 0, 0).astype(BF16)
    pq_rev_ref[...] = dot(pos_q, table_ref[1], 0, 0).astype(BF16)
    pq_ref[...] = dot(pos_q, table_ref[2], 0, 0).astype(BF16)


def project_kernel(scale, rows_of, skip, hidden_ref, *refs):
    pieces, rest = refs[:4], refs[4:]
    vec_ref, qkv_ref, pre_ref, stream_ref, low_ref, q_ref, kv_ref = rest
    width = q_ref.shape[1]
    gain, bias = rows_of
    pre = hidden_ref[...] + sum_pieces(pieces)
    pre_ref[...] = pre
    unit, _ = unit_of(pre)
    stream = unit * vec_ref[gain : gain + 1, :] + vec_ref[bias : bias + 1, :]
    stream_ref[...] = stream
    low = stream.astype(BF16)
    low_ref[...] = low
    kv_ref[...] = dot(low, qkv_ref[:, skip + width : skip + 3 * width], 1, 0).astype(BF16)
    q_ref[...] = (scale * dot(low, qkv_ref[:, skip : skip + width], 1, 0)).astype(BF16)


def gather_kernel(shape, place_ref, *refs):
    blocks, kv_ref, sems = refs[:-2], refs[-2], refs[-1]
    rows = blocks[0].shape[0]
    pairs = []
    for block, shift in zip(blocks, ctx_shifts(*shape)):
        owner = ctx_owner(place_ref, shift, -1, *shape)
        start = pl.multiple_of(owner * rows, rows)
        pairs.append((block, kv_ref.at[pl.ds(start, rows), :]))
    run_copies(pairs, sems)


def attention_kernel(q_ref, kv_ref, *refs):
    pk_ref, pq_ref, doc_i_ref, doc_j_ref = refs[:4]
    mix_ref, p_ref, to_ref, q_all = refs[4:]
    rows, width = q_ref.shape
    keys = kv_ref.shape[0]
    win = pk_ref.shape[1]
    heads = width // HEAD_DIM
    for head in range(heads):
        q = only_head(q_ref[...], head)
        q_all[head] = q
        to = dot(q, pk_ref[...], 1, 0)
        to = pltpu.roll(to, win + 1 - rows, 1, stride=1, stride_axis=0)
        to_ref[head] = to[:, :keys]
    doc_i = jnp.broadcast_to(doc_i_ref[...].astype(F32), (rows, rows)).T
    mix = jnp.zeros((rows, width), F32)
    for head in range(heads):
        q = q_all[head]
        parts = []
        for start in range(0, keys, BLOCK):
            key_block = kv_ref[start : start + BLOCK, :width]
            first = win - 2 * BLOCK - start
            pq = only_head(pq_ref[:, first : first + 2 * BLOCK], head, 0)
            off = dot(key_block, pq, 1, 0)
            off = pltpu.roll(off, BLOCK, 1, stride=1, stride_axis=0)
            s = dot(q, key_block, 1, 1) + to_ref[head, :, start : start + BLOCK]
            s = s + off[:, :BLOCK].T
            same = doc_i == doc_j_ref[:, start : start + BLOCK]
            parts.append(jnp.where(same, s, NEG))
        s = jnp.concatenate(parts, axis=1)
        e = jnp.exp(s - jnp.max(s, axis=1, keepdims=True))
        p = (e / jnp.sum(e, axis=1, keepdims=True)).astype(BF16)
        p_ref[head] = p
        mix = jnp.where(head_mask(mix.shape, head), dot(p, kv_ref[:, width:], 1, 0), mix)
    mix_ref[...] = mix.astype(BF16)


def attended_kernel(skip, mix_ref, full_ref, part_ref):
    attn = full_ref[:, skip : skip + mix_ref.shape[1]]
    part_ref[...] = dot(mix_ref[...], attn, 1, 1).astype(BF16)


def feed_kernel(rows_of, stream_ref, *refs):
    pieces, rest = refs[:4], refs[4:]
    vec_ref, in_ref, out_ref = rest[:3]
    pre_ref, hidden_ref, low_ref, slope_ref, active_ref, part_ref = rest[3:]
    gain, bias = rows_of
    pre = stream_ref[...].astype(F32) + sum_pieces(pieces)
    pre_ref[...] = pre
    unit, _ = unit_of(pre)
    hidden = unit * vec_ref[gain : gain + 1, :] + vec_ref[bias : bias + 1, :]
    hidden_ref[...] = hidden
    low = hidden.astype(BF16)
    low_ref[...] = low
    inner = dot(low, in_ref[...], 1, 0)
    below = 0.5 * (1.0 + lax.erf(inner * math.sqrt(0.5)))
    bell = jnp.exp(-0.5 * inner * inner) * (1.0 / math.sqrt(2.0 * math.pi))
    slope_ref[...] = below + inner * bell
    active = (inner * below).astype(BF16)
    active_ref[...] = active
    part_ref[...] = dot(active, out_ref[...], 1, 1).astype(BF16)


def end_kernel(rows_of, hidden_ref, *refs):
    pieces, (vec_ref, pre_ref, out_ref) = refs[:4], refs[4:]
    gain, bias = rows_of
    pre = hidden_ref[...] + sum_pieces(pieces)
    pre_ref[...] = pre
    unit, _ = unit_of(pre)
    stream = unit * vec_ref[gain : gain + 1, :] + vec_ref[bias : bias + 1, :]
    out_ref[...] = stream.astype(BF16)


def column_sums(ref, first, second):
    ref[...] = jnp.zeros_like(ref)
    ref[0:1, :] = jnp.sum(first, axis=0, keepdims=True)
    ref[1:2, :] = jnp.sum(second, axis=0, keepdims=True)


def feed_back_kernel(gain, has_pieces, grad_ref, *refs):
    pieces, rest = (refs[:4], refs[4:]) if has_pieces else ((), refs)
    pre_ref, vec_ref, slope_ref, in_ref, out_ref = rest[:5]
    d_pre_ref, d_low_ref, d_inner_ref, part_ref, norm_ref = rest[5:]
    grad = grad_ref[...].astype(F32)
    if has_pieces:
        grad = grad + sum_pieces(pieces)
    back, gain_terms = normalize_back(pre_ref[...], vec_ref[gain : gain + 1, :], grad)
    column_sums(norm_ref, gain_terms, grad)
    d_pre_ref[...] = back
    low = back.astype(BF16)
    d_low_ref[...] = low
    inner = (dot(low, out_ref[...], 1, 0) * slope_ref[...]).astype(BF16)
    d_inner_ref[...] = inner
    part_ref[...] = dot(inner, in_ref[...], 1, 1).astype(BF16)


def attention_back_kernel(gain, skip, scale, place_ref, *refs):
    pieces, rest = refs[:4], refs[4:]
    d_out_ref, pre_ref, vec_ref, full_ref, q_ref, kv_ref, pk_ref, pq_ref, p_ref = rest[:9]
    d_pre_ref, d_low_ref, dq_ref, dpk_ref, dpq_ref, norm_ref = rest[9:15]
    ds_all, to_all, dk_pos, dm_all, q_all, qr_all, dpq_sum, dkv = rest[-8:]
    dkv_refs = rest[15:-8]
    rows, width = q_ref.shape
    keys = kv_ref.shape[0]
    heads = width // HEAD_DIM
    win = pk_ref.shape[1]

    grad = d_out_ref[...] + sum_pieces(pieces)
    back, gain_terms = normalize_back(pre_ref[...], vec_ref[gain : gain + 1, :], grad)
    column_sums(norm_ref, gain_terms, grad)
    d_pre_ref[...] = back
    d_low = back.astype(BF16)
    d_low_ref[...] = d_low
    d_mixture = dot(d_low, full_ref[:, skip : skip + width], 1, 0)

    row = lax.broadcasted_iota(jnp.int32, (rows, rows), 0)
    col = lax.broadcasted_iota(jnp.int32, (rows, rows), 1)
    flip = jnp.where(row + col == rows - 1, 1.0, 0.0).astype(BF16)
    q_back = dot(flip, q_ref[...], 1, 0)
    content = jnp.zeros((rows, width), F32)
    position = jnp.zeros((rows, width), F32)
    dpq_sum[...] = jnp.zeros_like(dpq_sum)
    for head in range(heads):
        here = slice(head * rows, (head + 1) * rows)
        mask = head_mask((rows, width), head)
        dm = only_head(d_mixture, head)
        dm_all[here, :] = dm
        q_all[here, :] = only_head(q_ref[...], head)
        qr_all[here, :] = only_head(q_back, head)
        p = p_ref[head].astype(F32)
        da = dot(dm, kv_ref[:, width:], 1, 1)
        ds = (p * (da - jnp.sum(p * da, axis=1, keepdims=True))).astype(BF16)
        ds_all[here, :] = ds
        content = jnp.where(mask, dot(ds, kv_ref[:, :width], 1, 0), content)
        ds_back = dot(flip, ds, 1, 0)
        to = jnp.concatenate([ds_back, jnp.zeros((rows, win - keys), F32)], axis=1)
        to = pltpu.roll(to, 0, 1, stride=1, stride_axis=0).astype(BF16)
        to_all[here, :] = to
        position = jnp.where(mask, dot(to, pk_ref[...], 1, 1), position)
        for start in range(0, keys, BLOCK):
            off = ds_back[:, start : start + BLOCK].T
            off = jnp.concatenate([off, jnp.zeros((BLOCK, BLOCK), F32)], axis=1)
            off = pltpu.roll(off, 0, 1, stride=1, stride_axis=0).astype(BF16)
            key_block = only_head(kv_ref[start : start + BLOCK, :width], head)
            dpq_sum[start : start + 2 * BLOCK, :] += dot(off, key_block, 0, 0)
            more = dot(off, pq_ref[:, start : start + 2 * BLOCK], 1, 1)
            if head:
                more = jnp.where(
                    head_mask(more.shape, head), more, dk_pos[start : start + BLOCK, :]
                )
            dk_pos[start : start + BLOCK, :] = more
    high = position.astype(BF16)
    low = (position - high.astype(F32)).astype(BF16)
    dq = content + dot(flip, high, 1, 0) + dot(flip, low, 1, 0)
    dq_ref[...] = (scale * dq).astype(BF16)
    dkv[:, :width] = (dot(ds_all[...], q_all[...], 0, 0) + dk_pos[...]).astype(BF16)
    p_all = p_ref[...].reshape(heads * rows, keys)
    dkv[:, width:] = dot(p_all, dm_all[...], 0, 0).astype(BF16)
    x_count = len(dkv_refs)
    zl_count = keys // (rows * x_count)
    for shift, target in enumerate(dkv_refs):
        x = lax.rem(place_ref[1] + shift, x_count)
        for side in range(zl_count):
            zl = lax.rem(place_ref[2] + side, zl_count)
            start = pl.multiple_of((x * zl_count + zl) * rows, rows)
            target[side * rows : (side + 1) * rows, :] = dkv[pl.ds(start, rows), :]
    dpk_ref[...] = dot(to_all[...], qr_all[...], 0, 0).astype(BF16)
    dpq_ref[...] = (scale * dpq_sum[...]).astype(BF16)


def position_back_kernel(table_ref, dpk_ref, dpq_ref, low_ref, rows_ref):
    width = dpk_ref.shape[1]
    d_k = dot(table_ref[0], dpk_ref[...], 1, 0).astype(BF16)
    d_q = dot(table_ref[2], dpq_ref[...], 1, 0).astype(BF16)
    low_ref[:, :width] = d_q
    low_ref[:, width:] = d_k
    owners, step = rows_ref.shape[0], rows_ref.shape[1] // 2
    for owner in range(owners):
        rows_ref[owner, :step, :] = d_q[owner * step : (owner + 1) * step, :]
        rows_ref[owner, step:, :] = d_k[owner * step : (owner + 1) * step, :]


def relative_sums_kernel(unit_ref, *refs):
    out_ref = refs[-1]
    width = refs[0].shape[1] // 2
    total = None
    for pos_ref, qkv_ref in zip(refs[:-1:2], refs[1:-1:2]):
        term = dot(pos_ref[...], qkv_ref[:, : 2 * width], 1, 1)
        total = term if total is None else total + term
    column_sums(out_ref, total * unit_ref[...], total)


def picked_columns(ref, core, parts=2):
    run = ref.shape[1] // (2 * parts)
    picked = [ref[:, pl.ds(pl.multiple_of((2 * i + core) * run, run), run)] for i in range(parts)]
    return jnp.concatenate(picked, axis=1)


def scatter_kernel(own_core, names, x_first, place_ref, *refs):
    refs = list(refs)
    core = place_ref[3] if own_core else 1 - place_ref[3]
    parts = []
    for name in names:
        if name == "qkv":
            low_ref, all_ref, rel_ref, pos_ref = refs[:4]
            del refs[:4]
            value = dot(picked_columns(low_ref, core), all_ref[...], 0, 0)
            terms = dot(picked_columns(rel_ref, core), pos_ref[...], 0, 0)
            wide = pos_ref.shape[1]
            parts += [value[:, :wide] + terms, value[:, wide:]]
        elif name == "norm":
            hid = picked_columns(refs.pop(0), core)
            out = picked_columns(refs.pop(0), core)
            rel = picked_columns(refs.pop(0), core)
            rows = [hid[0:1], out[0:1], hid[1:2], out[1:2], rel[0:2]]
            rows.append(jnp.zeros((LANES - 6, hid.shape[1]), F32))
            rows = jnp.concatenate(rows, axis=0)
            parts.append(rows.T)
        elif name == "pos":
            rows_ref = refs.pop(0)
            run = rows_ref.shape[0] // 4
            picked = [rows_ref[pl.ds((2 * i + core) * run, run)] for i in range(2)]
            picked = jnp.concatenate(picked, axis=0).astype(F32)
            parts.append(picked.reshape(-1, rows_ref.shape[2]))
        else:
            left, right = refs[:2]
            del refs[:2]
            parts.append(dot(picked_columns(left, core), right[...], 0, 0))
    if not own_core:
        out_ref = refs[0]
        at = 0
        for part in parts:
            out_ref[:, at : at + part.shape[1]] = part.astype(BF16)
            at += part.shape[1]
        return
    arrived, outs, scr = refs[0], refs[1:-1], refs[-1]
    if x_first is None:
        outs = ()
    at = 0
    for part in parts:
        cols = part.shape[1]
        scr[:, at : at + cols] = (part + arrived[:, at : at + cols].astype(F32)).astype(BF16)
        at += cols
    if not outs:
        return
    count = len(outs)
    own = outs[0].shape[0] // count
    zl_count = scr.shape[0] // (own * count * 2)
    for shift, out_ref in enumerate(outs):
        near = lax.rem(place_ref[1 if x_first else 4] + shift, count)
        for far in range(count):
            x, z = (near, far) if x_first else (far, near)
            zh, zl = lax.div(z, zl_count), lax.rem(z, zl_count)
            start = pl.multiple_of(((zh * count + x) * zl_count + zl) * own, own)
            out_ref[far * own : (far + 1) * own, :] = scr[pl.ds(start, own), :]


def last_own_kernel(dims, names, ways, place_ref, *refs):
    count = 2 * len(ways)
    ins, outs, scr = refs[: -count - 1], refs[-count - 1 : -1], refs[-1]
    scatter_kernel(True, names, None, place_ref, *ins, scr)
    _, x_count, zh_count, zl_count, own = dims
    for lot, (x_first, pairing) in enumerate(ways):
        keep_ref, send_ref = outs[2 * lot : 2 * lot + 2]
        half, cols = keep_ref.shape
        xs, zs = ring_order(place_ref[1], pairing), ring_order(place_ref[4], pairing)
        for i, z in enumerate(zs):
            zh, zl = lax.div(z, zl_count), lax.rem(z, zl_count)
            for j, x in enumerate(xs):
                place = (i * x_count + j if x_first else j * len(zs) + i) * own
                target = keep_ref if place < half else send_ref
                start = pl.multiple_of(((zh * x_count + x) * zl_count + zl) * own, own)
                rows = scr[pl.ds(start, own), lot * cols : (lot + 1) * cols]
                target[place % half : place % half + own, :] = rows


def halve_kernel(count, *refs):
    for lot in range(count):
        total = refs[2 * lot][...].astype(F32) + refs[2 * lot + 1][...].astype(F32)
        keep_ref, send_ref = refs[2 * (count + lot) : 2 * (count + lot) + 2]
        half = keep_ref.shape[0]
        keep_ref[...] = total[:half].astype(BF16)
        send_ref[...] = total[half:].astype(BF16)


def middle_kernel(count, x_first, place_ref, *refs):
    pieces, outs, scr = refs[:count], refs[count:-1], refs[-1]
    total = pieces[0][...].astype(F32)
    for piece in pieces[1:]:
        total = total + piece[...].astype(F32)
    scr[...] = total.astype(BF16)
    own = outs[0].shape[0]
    for shift, out_ref in enumerate(outs):
        far = lax.rem(place_ref[4 if x_first else 1] + shift, len(outs))
        out_ref[...] = scr[pl.ds(pl.multiple_of(far * own, own), own), :]


def halves_kernel(count, *refs):
    pieces, (mine_ref, other_ref) = refs[:count], refs[count:]
    total = pieces[0][...].astype(F32)
    for piece in pieces[1:]:
        total = total + piece[...].astype(F32)
    rows = mine_ref.shape[0]
    mine_ref[...] = total[:rows, :]
    other_ref[...] = total[rows:, :].astype(BF16)


def stream_back_kernel(skip, dq_ref, mine_ref, other_ref, qkv_ref, all_ref, part_ref):
    total = mine_ref[...] + other_ref[...].astype(F32)
    both = jnp.concatenate([dq_ref[...], total.astype(BF16)], axis=1)
    all_ref[...] = both
    qkv = qkv_ref[:, skip : skip + both.shape[1]]
    part_ref[...] = dot(both, qkv, 1, 1).astype(BF16)


def total_of(refs, first, cols):
    total = refs[0][:, first : first + cols].astype(F32)
    for ref in refs[1:]:
        total = total + ref[:, first : first + cols].astype(F32)
    return total


def total_kernel(*refs):
    refs[-1][...] = total_of(refs[:-1], 0, refs[-1].shape[1])


def groups_of(counts, refs):
    return [refs[sum(counts[:i]) : sum(counts[: i + 1])] for i in range(len(counts))]


def early_end_kernel(counts, firsts, *refs):
    in_ref, out_ref = refs[-2:]
    hidden = in_ref.shape[2]
    for layer, pieces in enumerate(groups_of(counts, refs)):
        in_ref[layer] = total_of(pieces, firsts[layer], hidden)
        out_ref[layer] = total_of(pieces, firsts[layer] + hidden, hidden)


def middle_end_kernel(counts, firsts, *refs):
    attn_ref, gain_ref, bias_ref = refs[-3:]
    width = attn_ref.shape[2]
    for layer, pieces in enumerate(groups_of(counts, refs)):
        attn_ref[layer] = total_of(pieces, firsts[layer], width)
        norms = total_of(pieces, firsts[layer] + width, LANES).T
        gain_ref[layer] = norms[0:2, :]
        bias_ref[layer] = norms[2:4, :]


def late_end_kernel(qkv_at, early_at, *refs):
    lots, (qkv_ref, in_ref, out_ref) = refs[:-3], refs[-3:]
    width, hidden = qkv_ref.shape[3], in_ref.shape[2]
    totals = [
        lots[i][...].astype(F32) + lots[i + 1][...].astype(F32) for i in range(0, len(lots), 2)
    ]
    total = jnp.concatenate(totals, axis=1)
    for layer, (first, second) in enumerate(zip(qkv_at, early_at)):
        for i in range(3):
            at = first + i * width
            qkv_ref[layer, i] = total[:, at : at + width]
        in_ref[layer] = total[:, second : second + hidden]
        out_ref[layer] = total[:, second + hidden : second + 2 * hidden]


def relative_term_kernel(counts, firsts, skips, width, *refs):
    out_ref = refs[-1]
    layers = len(counts)
    total = None
    for layer, pieces in enumerate(groups_of(counts, refs)):
        qkv_ref, skip = refs[sum(counts) + layer], skips[layer]
        moved = total_of(pieces, firsts[layer], width).astype(BF16)
        step = moved.shape[0] // 2
        term = dot(moved[:step], qkv_ref[:, skip : skip + width], 1, 1)
        term = term + dot(moved[step:], qkv_ref[:, skip + width : skip + 2 * width], 1, 1)
        total = term if total is None else total + term
    out_ref[: total.shape[0], :] = total
    sums = total_of(groups_of(counts, refs)[0], firsts[0] - LANES, LANES).T
    rest = jnp.zeros((8, total.shape[1] - sums.shape[1]), F32)
    out_ref[total.shape[0] :, :] = jnp.concatenate([sums[:8], rest], axis=1)


def token_end_kernel(grad_ref, *refs):
    refs[-1][...] = (grad_ref[...] + sum_pieces(refs[:-1])).astype(BF16)


def relative_end_kernel(gain, *refs):
    pieces, (rel_ref, vec_ref, grad_ref, ends_ref) = refs[:4], refs[4:]
    total = sum_pieces(pieces)
    rows = rel_ref.shape[0]
    back, _ = normalize_back(
        rel_ref[...].astype(F32), vec_ref[gain : gain + 1, :], total[:rows]
    )
    grad_ref[...] = back
    ends_ref[...] = total[rows : rows + 8, :LANES]


def shifted(values, axes, shift):
    count = lax.axis_size(axes)
    return lax.ppermute(values, axes, [(i, (i + shift) % count) for i in range(count)])


def ctx_shifted(values):
    x_count, zl_count = lax.axis_size("x"), lax.axis_size("zl")
    shifts = ctx_shifts(x_count, zl_count)
    moved = [values[0]]
    for i in reversed(range(1, len(shifts))):
        dx, dz = shifts[i]
        pairs = []
        for x in range(x_count):
            for z in range(zl_count):
                target = (x + dx) % x_count * zl_count + (z + dz) % zl_count
                pairs.append((x * zl_count + z, target))
        moved.insert(1, lax.ppermute(values[i], CTX, pairs))
    return moved


def tp_pieces(low):
    count = lax.axis_size("tp")
    order = sorted(range(1, count), key=lambda s: -min(s, count - s))
    moved = {s: shifted(low, "tp", s) for s in order}
    return [low] + [moved[s] for s in range(1, count)]


def moved_on(pieces, axes):
    count = len(pieces)
    order = sorted(range(1, count), key=lambda s: -min(s, count - s))
    moved = {s: shifted(pieces[s], axes, s) for s in order}
    return [pieces[0]] + [moved[s] for s in range(1, count)]


def local(
    tokens,
    cotangent,
    w_qkv,
    w_attn,
    w_in,
    w_out,
    ln_gain,
    ln_bias,
    rel_emb,
    rel_gain,
    rel_bias,
    doc_ids,
    rel_bucket,
):
    _, rows, model = tokens.shape
    layers, _, own, width = w_qkv.shape
    hidden_units = w_in.shape[2]
    heads = width // HEAD_DIM
    ctx_count = lax.axis_size(CTX)
    owners = lax.axis_size(OWNERS)
    length = rows * ctx_count
    row_start = lax.axis_index(CTX) * rows
    scale = 1.0 / math.sqrt(3.0 * HEAD_DIM)
    win = length + rows
    rel_own = rel_emb.shape[0]
    buckets = rel_own * owners
    wide = 3 * width

    shape = (lax.axis_size("x"), lax.axis_size("zl"))
    x_count, z_count = lax.axis_size("x"), lax.axis_size(ZED)
    dims = (lax.axis_size("core"), x_count, lax.axis_size("zh"), lax.axis_size("zl"), own)
    plane = lax.axis_size(PLANE)
    place = [("zh", "core"), "x", "zl", "core", ZED]
    place = jnp.stack([lax.axis_index(axes) for axes in place]).astype(jnp.int32)
    dma = pltpu.SemaphoreType.DMA

    previous = []

    def run(*args, after=(), **kwargs):
        outs = call(*args, after=(*previous, *after), **kwargs)
        previous[:] = [outs[-1]]
        return outs

    attn_rows, out_rows = jnp.swapaxes(w_attn, 1, 2), jnp.swapaxes(w_out, 1, 2)
    table = [{"qkv0": wide, "attn0": width}, {"in0": hidden_units}, {"out0": hidden_units}, {}]
    for layer in range(1, layers):
        table[1]["qkv%d" % layer] = wide
        table[2]["in%d" % layer] = hidden_units
        table[3].update({"out%d" % layer: hidden_units, "attn%d" % layer: width})
    ways = [START_WAY, (True, 1), (False, 0), (False, 1)]
    sources = {"attn": attn_rows, "in": w_in, "out": out_rows}

    def listed(table, at):
        arrays, index, columns = [], [], {}
        for name, cols in table.items():
            kind, layer = name[:-1], int(name[-1])
            columns[name] = at
            at += cols
            if kind == "qkv":
                arrays += [w_qkv] * 3
                index += [(layer, i) for i in range(3)]
            else:
                arrays.append(sources[kind])
                index.append(layer)
        return arrays, index, columns, at

    one_arrays, one_index, one_at, one_cols = listed(table[0], LANES + model // 2)
    vectors = [rel_emb, ln_gain, ln_bias, rel_gain[None], rel_bias[None], doc_ids]

    found = {name: (0, at) for name, at in one_at.items()}
    arrays, other_index, sizes = list(one_arrays), [], []
    for lot in range(1, len(table)):
        more, index, columns, cols = listed(table[lot], 0)
        found.update({name: (lot, at) for name, at in columns.items()})
        arrays += more
        other_index.append(index)
        sizes.append(cols)

    def pack_start(*refs):
        pack_start_kernel(*refs[:6], one_index, other_index, *refs[6:])

    lots = run(
        pack_start,
        [((own, cols), BF16) for cols in sizes + [one_cols]],
        vectors + arrays,
        hbm=range(len(vectors) + len(arrays)),
        scratch=[
            pltpu.VMEM((LANES, LANES), F32),
            pltpu.VMEM(ln_gain.shape, BF16),
            pltpu.VMEM(ln_bias.shape, BF16),
            pltpu.VMEM((1, own), BF16),
            pltpu.VMEM((1, own), BF16),
            pltpu.VMEM((1, rows), jnp.int32),
            dma((7 + len(arrays),)),
        ],
        name="pack_start",
    )
    lots = [lots[-1], *lots[:-1]]

    padded = jnp.pad(rel_bucket, (1, 1), mode="edge")
    to_index = lax.dynamic_slice_in_dim(padded, row_start, win, 0)
    from_index = lax.dynamic_slice_in_dim(padded, length - rows - row_start + 1, win, 0)
    index = jnp.stack([to_index[::-1], from_index[::-1], from_index])
    (tables,) = run(table_kernel, [((3, buckets, win), BF16)], [index], limit=8, name="tables")

    def stack(one, two, after):
        rows_here, cols = one.shape
        return run(
            stack_kernel,
            [((2 * rows_here, cols), BF16)],
            [one, two],
            after=after,
            name="stack",
        )[0]

    even, odd = [(0, 1), (1, 0), (2, 3), (3, 2)], [(1, 2), (2, 1), (3, 0), (0, 3)]
    for step in range(4):
        moved = []
        for lot, (x_first, pairing) in zip(lots, ways):
            axes = "x" if x_first == (step < 2) else ZED
            moved.append(lax.ppermute(lot, axes, odd if pairing ^ (step % 2) else even))
        for i in range(len(lots)):
            lots[i] = stack(lots[i], moved[i], moved if i == 0 else ())
    for i in range(4):
        lots[i] = [lots[i], shifted(lots[i], "core", 1)]
    one_pieces = lots[0]
    qkv, attn, small, q, key_value = run(
        functools.partial(start_kernel, dims, scale, [one_at["qkv0"], one_at["attn0"], 0]),
        [
            ((model, wide), BF16),
            ((model, width), BF16),
            ((model, LANES), BF16),
            ((rows, width), BF16),
            ((rows, 2 * width), BF16),
        ],
        [place, tokens[0], *one_pieces],
        smem=(0,),
        anys=range(2, 2 + len(one_pieces)),
        scratch=[dma((3 * owners,))],
        name="start",
    )
    rel_low, rel_unit, vecs, doc_j = run(
        functools.partial(relative_kernel, dims, layers),
        [
            ((buckets, model), BF16),
            ((buckets, model), F32),
            ((16, model), F32),
            ((1, length), F32),
        ],
        [place, small, *one_pieces],
        smem=(0,),
        anys=range(2, 2 + len(one_pieces)),
        limit=16,
        scratch=[pltpu.VMEM((buckets, model), BF16), dma((2 * owners,))],
        name="relative",
    )

    def rest(names):
        lot = found[names[0]][0]
        return run(
            functools.partial(rest_kernel, dims, ways[lot], [found[name][1] for name in names]),
            [((model, table[lot][name]), BF16) for name in names],
            [place, *lots[lot]],
            smem=(0,),
            anys=(1, 2),
            scratch=[dma((len(names) * owners,))],
            name="rest",
        )

    qkvs, attns, ins, outs = [qkv], [attn], [], []

    token_low = tokens[0]
    stream = token_low
    kept = []
    hidden, pieces = None, None
    tile = (rows, model)
    for layer in range(layers):
        if layer:
            pre_out, stream, stream_low, q, key_value = run(
                functools.partial(
                    project_kernel,
                    scale,
                    (2 * layer - 1, 2 * layers + 2 * layer - 1),
                    0,
                ),
                [
                    (tile, F32),
                    (tile, F32),
                    (tile, BF16),
                    ((rows, width), BF16),
                    ((rows, 2 * width), BF16),
                ],
                [hidden, *pieces, vecs, qkvs[layer]],
                name="project",
            )
            kept[-1]["pre_out"] = pre_out
        else:
            stream_low = token_low
        blocks = ctx_shifted([key_value] * ctx_count)
        pk, pq_rev, pq = run(
            functools.partial(position_kernel, scale, 0),
            [((width, win), BF16)] * 3,
            [rel_low, qkvs[layer], tables],
            name="position",
        )
        (kv,) = run(
            functools.partial(gather_kernel, shape),
            [((length, 2 * width), BF16)],
            [place, *blocks],
            smem=(0,),
            anys=range(1, 1 + ctx_count),
            scratch=[dma((ctx_count,))],
            name="gather",
        )
        mixture, p = run(
            attention_kernel,
            [((rows, width), BF16), ((heads, rows, length), BF16)],
            [q, kv, pk, pq_rev, doc_ids, doc_j],
            scratch=[
                pltpu.VMEM((heads, rows, length), F32),
                pltpu.VMEM((heads, rows, width), BF16),
            ],
            limit=16,
            name="attention",
        )
        (part,) = run(
            functools.partial(attended_kernel, 0),
            [(tile, BF16)],
            [mixture, attns[layer]],
            name="attended",
        )
        pieces = tp_pieces(part)
        ins += rest(["in%d" % layer])
        outs += rest(["out%d" % layer])
        pre_hidden, hidden, hidden_low, slope, active, part = run(
            functools.partial(feed_kernel, (2 * layer, 2 * layers + 2 * layer)),
            [
                (tile, F32),
                (tile, F32),
                (tile, BF16),
                ((rows, hidden_units), F32),
                ((rows, hidden_units), BF16),
                (tile, BF16),
            ],
            [stream, *pieces, vecs, ins[layer], outs[layer]],
            name="feed",
        )
        pieces = tp_pieces(part)
        if layer + 1 < layers:
            qkvs += rest(["qkv%d" % (layer + 1)])
            attns += rest(["attn%d" % (layer + 1)])
        kept.append(
            dict(
                stream_low=stream_low,
                q=q,
                kv=kv,
                pk=pk,
                pq=pq,
                p=p,
                mixture=mixture,
                pre_hidden=pre_hidden,
                hidden_low=hidden_low,
                slope=slope,
                active=active,
            )
        )
    last = layers - 1
    pre_out, out_local = run(
        functools.partial(end_kernel, (2 * last + 1, 2 * layers + 2 * last + 1)),
        [(tile, F32), (tile, BF16)],
        [hidden, *pieces, vecs],
        name="end",
    )
    kept[-1]["pre_out"] = pre_out

    grad_parts = [cotangent[0]]
    x_count = lax.axis_size("x")

    def scatter_other(names, ins, cols, label):
        (other,) = run(
            functools.partial(scatter_kernel, False, names, False),
            [((model // 2, cols), BF16)],
            [place, *ins],
            smem=(0,),
            limit=30,
            name=label + "_other",
        )
        return shifted(other, "core", 1)

    def scatter_own(names, ins, arrived, label, x_first=False, after=()):
        half, cols = arrived.shape
        pieces = run(
            functools.partial(scatter_kernel, True, names, x_first),
            [((half // z_count, cols), BF16)] * z_count,
            [place, *ins, arrived],
            smem=(0,),
            scratch=[pltpu.VMEM((half, cols), BF16)],
            after=after,
            limit=16,
            name=label + "_own",
        )
        return moved_on(pieces, "x" if x_first else ZED)

    def scatter_middle(pieces, label, x_first=False):
        rows_here, cols = pieces[0].shape
        pieces = run(
            functools.partial(middle_kernel, len(pieces), x_first),
            [((rows_here // x_count, cols), BF16)] * x_count,
            [place, *pieces],
            smem=(0,),
            scratch=[pltpu.VMEM((rows_here, cols), BF16)],
            name=label + "_middle",
        )
        return moved_on(pieces, ZED if x_first else "x")

    def scatter_total(pieces, label):
        return list(run(total_kernel, [(pieces[0].shape, F32)], pieces, name=label + "_total"))

    early_names, early_cols = ("in", "out"), 2 * hidden_units
    middle_names, middle_cols = ("attn", "norm", "pos"), 2 * width + LANES
    early_ins, middle_ins, late_ins, pos_lows = [], [], [], []
    for layer in reversed(range(layers)):
        k = kept[layer]
        d_pre_out, d_out_low, d_inner, part, norm_out = run(
            functools.partial(feed_back_kernel, 2 * layer + 1, len(grad_parts) > 1),
            [
                (tile, F32),
                (tile, BF16),
                ((rows, hidden_units), BF16),
                (tile, BF16),
                ((8, model), F32),
            ],
            [*grad_parts, k["pre_out"], vecs, k["slope"], ins[layer], outs[layer]],
            name="feed_back",
        )
        pieces = tp_pieces(part)
        early_in = [k["hidden_low"], d_inner, d_out_low, k["active"]]
        early_ins += early_in
        backs = run(
            functools.partial(attention_back_kernel, 2 * layer, 0, scale),
            [
                (tile, F32),
                (tile, BF16),
                ((rows, width), BF16),
                ((win, width), BF16),
                ((win, width), BF16),
                ((8, model), F32),
            ]
            + [((length // x_count, 2 * width), BF16)] * x_count,
            [place, *pieces, d_pre_out, k["pre_hidden"], vecs, attns[layer]]
            + [k["q"], k["kv"], k["pk"], k["pq"], k["p"]],
            smem=(0,),
            scratch=[
                pltpu.VMEM((heads * rows, length), BF16),
                pltpu.VMEM((heads * rows, win), BF16),
                pltpu.VMEM((length, width), F32),
                pltpu.VMEM((heads * rows, width), BF16),
                pltpu.VMEM((heads * rows, width), BF16),
                pltpu.VMEM((heads * rows, width), BF16),
                pltpu.VMEM((win, width), F32),
                pltpu.VMEM((length, 2 * width), BF16),
            ],
            limit=20,
            name="attention_back",
        )
        d_pre_hidden, d_attended, dq, dpk, dpq, norm_hidden = backs[:6]
        dkv = moved_on(backs[6:], "x")
        pos_low, pos_rows = run(
            position_back_kernel,
            [((buckets, 2 * width), BF16), ((owners, 2 * rel_own, width), BF16)],
            [tables, dpk, dpq],
            name="position_back",
        )
        pos_lows.append(pos_low)
        norm_rel = jnp.zeros((8, model), F32)
        if not layer:
            pairs = [item for pair in zip(pos_lows, qkvs[::-1]) for item in pair]
            (norm_rel,) = run(
                relative_sums_kernel,
                [((8, model), F32)],
                [rel_unit, *pairs],
                limit=16,
                name="relative_sums",
            )
        middle_ins += [d_attended, k["mixture"], norm_hidden, norm_out, norm_rel, pos_rows]
        if not layer:
            arrived = scatter_other(
                middle_names * layers, middle_ins, middle_cols * layers, "middle"
            )
        if not layer:
            middle = scatter_own(middle_names * layers, middle_ins, arrived, "middle")
        mine, other = run(
            functools.partial(halves_kernel, x_count),
            [((rows, 2 * width), F32), ((rows, 2 * width), BF16)],
            dkv,
            name="halves",
        )
        other = shifted(other, "zl", 1)
        if not layer:
            middle = scatter_middle(middle, "middle")
        dqkv, part = run(
            functools.partial(stream_back_kernel, 0),
            [((rows, wide), BF16), (tile, BF16)],
            [dq, mine, other, qkvs[layer]],
            name="stream_back",
        )
        grad_parts = [d_pre_hidden] + tp_pieces(part)
        late_ins += [k["stream_low"], dqkv, rel_low, pos_low]
    late_names, late_cols = ("qkv",) * layers, wide * layers
    late_names, late_cols = late_names + early_names * layers, late_cols + early_cols * layers
    late_ins += early_ins
    arrived = scatter_other(late_names, late_ins, late_cols, "late")
    middle_at = [(layers - 1 - layer) * middle_cols for layer in range(layers)]
    late_at = [(layers - 1 - layer) * wide for layer in range(layers)]

    counts = [len(middle)] * layers
    (term,) = run(
        functools.partial(
            relative_term_kernel,
            counts,
            [at + width + LANES for at in middle_at],
            [0] * layers,
            width,
        ),
        [((rel_own + 8, model), F32)],
        middle * layers + qkvs,
        name="relative_term",
    )
    terms = tp_pieces(term)
    half, lot_cols = model // 2, late_cols // len(ways)
    parts = run(
        functools.partial(last_own_kernel, dims, late_names, ways),
        [((half // 2, lot_cols), BF16)] * (2 * len(ways)),
        [place, *late_ins, arrived],
        smem=(0,),
        scratch=[pltpu.VMEM((half, late_cols), BF16)],
        limit=30,
        name="late_own",
    )

    def sent(parts, step):
        moved = []
        for lot, (x_first, pairing) in enumerate(ways):
            axes = "x" if x_first == (step < 2) else ZED
            pairs = odd if pairing ^ (step % 2) else even
            moved += [parts[2 * lot], lax.ppermute(parts[2 * lot + 1], axes, pairs)]
        return moved

    def halved(parts):
        rows_here = parts[0].shape[0] // 2
        return run(
            functools.partial(halve_kernel, len(ways)),
            [((rows_here, lot_cols), BF16)] * (2 * len(ways)),
            parts,
            name="halve",
        )

    parts = halved(sent(parts, 3))
    parts = sent(parts, 2)
    (grad_tokens,) = run(token_end_kernel, [(tile, BF16)], grad_parts, name="token_end")
    parts = halved(parts)
    parts = sent(parts, 1)
    grad_rel, ends = run(
        functools.partial(relative_end_kernel, 4 * layers),
        [((rel_own, model), F32), ((8, LANES), F32)],
        [*terms, rel_emb, vecs],
        name="relative_end",
    )
    grad_attn, grad_gain, grad_bias = run(
        functools.partial(middle_end_kernel, counts, middle_at),
        [((layers, own, width), F32), ((layers, 2, own), F32), ((layers, 2, own), F32)],
        middle * layers,
        name="middle_end",
    )
    parts = sent(halved(parts), 0)
    grad_qkv, grad_in, grad_out = run(
        functools.partial(
            late_end_kernel,
            late_at,
            [wide * layers + (layers - 1 - layer) * early_cols for layer in range(layers)],
        ),
        [
            ((layers, 3, own, width), F32),
            ((layers, own, hidden_units), F32),
            ((layers, own, hidden_units), F32),
        ],
        parts,
        name="late_end",
    )
    grad_attn, grad_out = jnp.swapaxes(grad_attn, 1, 2), jnp.swapaxes(grad_out, 1, 2)
    return (
        out_local[None],
        grad_tokens[None],
        grad_qkv,
        grad_attn,
        grad_in,
        grad_out,
        grad_gain,
        grad_bias,
        grad_rel,
        ends[4, :own],
        ends[5, :own],
    )


def solution(mesh):
    sizes = mesh.shape
    zh, zl = 2, 2
    finer = Mesh(
        mesh.devices.reshape(zh, sizes["fsdp"] // zh, sizes["ctx"] // zl, zl, sizes["tp"]),
        ("zh", "core", "x", "zl", "tp"),
    )
    own = OWNERS
    fsdp = ("zh", "core")
    return jax.shard_map(
        local,
        mesh=finer,
        in_specs=(
            P(fsdp, CTX, None),
            P(fsdp, CTX, None),
            P(None, None, own, "tp"),
            P(None, "tp", own),
            P(None, own, "tp"),
            P(None, "tp", own),
            P(None, None, own),
            P(None, None, own),
            P(own, None),
            P(own),
            P(own),
            P(fsdp, CTX),
            P(),
        ),
        out_specs=(
            P(fsdp, CTX, None),
            P(fsdp, CTX, None),
            P(None, None, own, "tp"),
            P(None, "tp", own),
            P(None, own, "tp"),
            P(None, "tp", own),
            P(None, None, own),
            P(None, None, own),
            P(own, None),
            P(own),
            P(own),
        ),
        check_vma=False,
    )
```

```python
import functools
import math

import jax
import jax.numpy as jnp
from jax import lax
from jax.experimental import pallas as pl
from jax.experimental.pallas import tpu as pltpu
from jax.sharding import Mesh
from jax.sharding import PartitionSpec as P

HEAD_DIM = 64
EPS = 1e-07
NEG = -1e30
BLOCK = 128
LANES = 128
START_WAY = (True, 0)
F32 = jnp.float32
BF16 = jnp.bfloat16
CTX = ("x", "zl")
ZED = ("zh", "zl")
PLANE = ("zh", "x", "zl")
OWNERS = ("zh", "core", "x", "zl")


def dot(a, b, ca, cb):
    return lax.dot_general(a, b, (((ca,), (cb,)), ((), ())), preferred_element_type=F32)


def call(body, outs, ins, *, anys=(), hbm=(), smem=(), scratch=(), after=(), limit=8, name=None):
    specs = []
    for i in range(len(ins)):
        space = pltpu.VMEM
        if i in anys:
            space = pl.ANY
        if i in hbm:
            space = pltpu.HBM
        if i in smem:
            space = pltpu.SMEM
        specs.append(pl.BlockSpec(memory_space=space))
    count, late = len(ins), len(after)
    specs += [pl.BlockSpec(memory_space=pl.ANY)] * late
    ins = [
        pltpu.with_memory_space_constraint(value, pltpu.HBM) if i in hbm else value
        for i, value in enumerate(ins)
    ]

    def without(*refs):
        body(*refs[:count], *refs[count + late :])

    return pl.pallas_call(
        without,
        in_specs=specs,
        out_specs=tuple(pl.BlockSpec(memory_space=pltpu.VMEM) for _ in outs),
        out_shape=tuple(jax.ShapeDtypeStruct(shape, dtype) for shape, dtype in outs),
        scratch_shapes=list(scratch),
        compiler_params=pltpu.CompilerParams(vmem_limit_bytes=limit << 20),
        name=name,
    )(*ins, *after)


def ctx_shifts(x_count, zl_count):
    pairs = [(dx, dz) for dx in range(x_count) for dz in range(zl_count)]
    return sorted(pairs, key=lambda p: (min(p[0], x_count - p[0]) + p[1], p[1], p[0]))


def ctx_owner(place_ref, shift, sign, x_count, zl_count):
    x = lax.rem(place_ref[1] + (sign * shift[0]) % x_count, x_count)
    zl = lax.rem(place_ref[2] + (sign * shift[1]) % zl_count, zl_count)
    return x * zl_count + zl


def head_mask(shape, head, axis=1):
    index = lax.broadcasted_iota(jnp.int32, shape, axis)
    return (index >= head * HEAD_DIM) & (index < (head + 1) * HEAD_DIM)


def only_head(values, head, axis=1):
    mask = head_mask(values.shape, head, axis)
    return jnp.where(mask, values.astype(F32), 0.0).astype(BF16)


def unit_of(values):
    average = jnp.mean(values, axis=-1, keepdims=True)
    centered = values - average
    spread = jnp.mean(centered * centered, axis=-1, keepdims=True)
    inverse = lax.rsqrt(spread + EPS)
    return centered * inverse, inverse


def normalize_back(values, gain_vec, grad):
    unit, inverse = unit_of(values)
    scaled = grad * gain_vec
    back = (
        scaled
        - jnp.mean(scaled, axis=-1, keepdims=True)
        - unit * jnp.mean(scaled * unit, axis=-1, keepdims=True)
    ) * inverse
    return back, grad * unit


def sum_pieces(pieces):
    parts = [piece[...].astype(F32) for piece in pieces]
    return (parts[0] + parts[2]) + (parts[1] + parts[3])


def run_copies(pairs, sems):
    copies = [
        pltpu.make_async_copy(source, target, sems.at[i])
        for i, (source, target) in enumerate(pairs)
    ]
    for copy in copies:
        copy.start()
    for copy in copies:
        copy.wait()


def pack_start_kernel(rel_ref, gain_ref, bias_ref, rgain_ref, rbias_ref, doc_ref, *refs):
    out_ref, scr, gain, bias, rgain, rbias, doc, sems = refs[-8:]
    index, others, parts = refs[0], refs[1], refs[2:-8]
    parts, other_refs = parts[: -len(others)], parts[-len(others) :]
    layers, _, own = gain_ref.shape
    half = rel_ref.shape[1] // 2
    part = rel_ref.shape[0]
    pairs = [(gain_ref, gain), (bias_ref, bias), (rgain_ref, rgain), (rbias_ref, rbias)]
    pairs += [(doc_ref, doc)]
    at = 0
    for i in range(2):
        pairs.append(
            (
                rel_ref.at[:, pl.ds(i * half, half)],
                out_ref.at[pl.ds(i * part, part), pl.ds(LANES, half)],
            )
        )
    taken = 0
    for leads, target, at in [(index, out_ref, LANES + half)] + [
        (leads, target, 0) for leads, target in zip(others, other_refs)
    ]:
        for lead, ref in zip(leads, parts[taken:]):
            cols = ref.shape[-1]
            pairs.append((ref.at[lead], target.at[:, pl.ds(at, cols)]))
            at += cols
        taken += len(leads)
    run_copies(pairs, sems)
    scr[...] = jnp.zeros_like(scr)
    for layer in range(layers):
        scr[2 * layer : 2 * layer + 2, :own] = gain[layer].astype(F32)
        base = 2 * layers + 2 * layer
        scr[base : base + 2, :own] = bias[layer].astype(F32)
    scr[4 * layers : 4 * layers + 1, :own] = rgain[...].astype(F32)
    scr[4 * layers + 1 : 4 * layers + 2, :own] = rbias[...].astype(F32)
    small = scr[...].T[:own, :]
    row = lax.broadcasted_iota(jnp.int32, small.shape, 0)
    upper = lax.broadcasted_iota(jnp.int32, small.shape, 1) >= LANES // 2
    doc_row = doc[...].astype(F32)
    turned = pltpu.roll(doc_row, LANES // 2, 1)
    small = jnp.where(upper & (row == 0), turned, small)
    small = jnp.where(upper & (row == 1), doc_row, small)
    out_ref[:, :LANES] = small.astype(BF16)


def ring_order(place, pairing):
    even = place + 1 - 2 * lax.rem(place, 2)
    odd = 3 - place
    if pairing:
        return [place, odd, even, 3 - even]
    return [place, even, odd, odd + 1 - 2 * lax.rem(odd, 2)]


def assemble(dims, way, place_ref, pieces, moves, sems, more=()):
    core_count, x_count, zh_count, zl_count, own = dims
    x_first, pairing = way
    core = place_ref[3]
    xs, zs = ring_order(place_ref[1], pairing), ring_order(place_ref[4], pairing)
    pairs = list(more)
    for c_shift, piece in enumerate(pieces):
        from_c = lax.rem(core + c_shift, core_count)
        for i, z in enumerate(zs):
            zh, zl = lax.div(z, zl_count), lax.rem(z, zl_count)
            for j, x in enumerate(xs):
                owner = ((zh * core_count + from_c) * x_count + x) * zl_count + zl
                place = (i * x_count + j if x_first else j * len(zs) + i) * own
                for row, rows, col, cols, target, step, to_col in moves:
                    start = pl.multiple_of(owner * step, step)
                    pairs.append(
                        (
                            piece.at[pl.ds(place + row, rows), pl.ds(col, cols)],
                            target.at[pl.ds(start, rows), pl.ds(to_col, cols)],
                        )
                    )
    run_copies(pairs, sems)


def stack_kernel(*refs):
    count = len(refs) // 3
    for i in range(count):
        one_ref, two_ref, out_ref = refs[2 * i], refs[2 * i + 1], refs[2 * count + i]
        rows = one_ref.shape[0]
        out_ref[:rows, :] = one_ref[...]
        out_ref[rows:, :] = two_ref[...]


def rest_kernel(dims, way, columns, place_ref, one_ref, two_ref, *refs):
    targets, sems = refs[:-1], refs[-1]
    own = dims[-1]
    moves = [
        (0, own, first, target.shape[1], target, own, 0)
        for first, target in zip(columns, targets)
    ]
    assemble(dims, way, place_ref, (one_ref, two_ref), moves, sems)


def start_kernel(dims, scale, columns, place_ref, tokens_ref, *refs):
    pieces, (qkv_ref, attn_ref, small_ref, q_ref, kv_ref, low_ref, sems) = refs[:-7], refs[-7:]
    own = dims[-1]
    width = q_ref.shape[1]
    moves = [
        (0, own, first, target.shape[1], target, own, 0)
        for first, target in zip(columns, (qkv_ref, attn_ref, small_ref))
    ]
    assemble(dims, START_WAY, place_ref, pieces, moves, sems, [(tokens_ref, low_ref)])
    low = low_ref[...]
    kv_ref[...] = dot(low, qkv_ref[:, width:], 1, 0).astype(BF16)
    q_ref[...] = (scale * dot(low, qkv_ref[:, :width], 1, 0)).astype(BF16)


def relative_kernel(dims, layers, place_ref, small_ref, *refs):
    pieces, (low_ref, unit_ref, vec_ref, doc_ref, rel, sems) = refs[:-6], refs[-6:]
    own = dims[-1]
    half = rel.shape[1] // 2
    part = own // 2
    moves = [(i * part, part, LANES, half, rel, part, i * half) for i in range(2)]
    assemble(dims, START_WAY, place_ref, pieces, moves, sems)
    turned = small_ref[...].astype(F32).T[: vec_ref.shape[0], :]
    vec_ref[...] = turned
    unit, _ = unit_of(rel[...].astype(F32))
    unit_ref[...] = unit
    gain, bias = turned[4 * layers : 4 * layers + 1], turned[4 * layers + 1 : 4 * layers + 2]
    low_ref[...] = (unit * gain + bias).astype(BF16)
    blocks = doc_ref.shape[1] // LANES
    span = blocks * own
    start = pl.multiple_of(place_ref[0] * span, span)
    mine = small_ref[pl.ds(start, span), :].astype(F32)
    upper = lax.broadcasted_iota(jnp.int32, (1, LANES), 1) >= LANES // 2
    for block in range(blocks):
        first = pltpu.roll(mine[block * own : block * own + 1, :], LANES // 2, 1)
        second = mine[block * own + 1 : block * own + 2, :]
        doc_ref[:, block * LANES : (block + 1) * LANES] = jnp.where(upper, second, first)


def table_kernel(index_ref, table_ref):
    count, buckets, win = table_ref.shape
    bucket = lax.broadcasted_iota(jnp.int32, (buckets, win), 0)
    for i in range(count):
        same = bucket == index_ref[i : i + 1, :]
        table_ref[i] = jnp.where(same, 1.0, 0.0).astype(BF16)


def position_kernel(scale, skip, rel_ref, qkv_ref, table_ref, pk_ref, pq_rev_ref, pq_ref):
    width = pk_ref.shape[0]
    pos_q = (scale * dot(rel_ref[...], qkv_ref[:, skip : skip + width], 1, 0)).astype(BF16)
    pos_k = dot(rel_ref[...], qkv_ref[:, skip + width : skip + 2 * width], 1, 0).astype(BF16)
    pk_ref[...] = dot(pos_k, table_ref[0], 0, 0).astype(BF16)
    pq_rev_ref[...] = dot(pos_q, table_ref[1], 0, 0).astype(BF16)
    pq_ref[...] = dot(pos_q, table_ref[2], 0, 0).astype(BF16)


def project_kernel(scale, rows_of, skip, hidden_ref, *refs):
    pieces, rest = refs[:4], refs[4:]
    vec_ref, qkv_ref, pre_ref, stream_ref, low_ref, q_ref, kv_ref = rest
    width = q_ref.shape[1]
    gain, bias = rows_of
    pre = hidden_ref[...] + sum_pieces(pieces)
    pre_ref[...] = pre
    unit, _ = unit_of(pre)
    stream = unit * vec_ref[gain : gain + 1, :] + vec_ref[bias : bias + 1, :]
    stream_ref[...] = stream
    low = stream.astype(BF16)
    low_ref[...] = low
    kv_ref[...] = dot(low, qkv_ref[:, skip + width : skip + 3 * width], 1, 0).astype(BF16)
    q_ref[...] = (scale * dot(low, qkv_ref[:, skip : skip + width], 1, 0)).astype(BF16)


def gather_kernel(shape, place_ref, *refs):
    blocks, kv_ref, sems = refs[:-2], refs[-2], refs[-1]
    rows = blocks[0].shape[0]
    pairs = []
    for block, shift in zip(blocks, ctx_shifts(*shape)):
        owner = ctx_owner(place_ref, shift, -1, *shape)
        start = pl.multiple_of(owner * rows, rows)
        pairs.append((block, kv_ref.at[pl.ds(start, rows), :]))
    run_copies(pairs, sems)


def attention_kernel(q_ref, kv_ref, *refs):
    pk_ref, pq_ref, doc_i_ref, doc_j_ref = refs[:4]
    mix_ref, p_ref, to_ref, q_all = refs[4:]
    rows, width = q_ref.shape
    keys = kv_ref.shape[0]
    win = pk_ref.shape[1]
    heads = width // HEAD_DIM
    for head in range(heads):
        q = only_head(q_ref[...], head)
        q_all[head] = q
        to = dot(q, pk_ref[...], 1, 0)
        to = pltpu.roll(to, win + 1 - rows, 1, stride=1, stride_axis=0)
        to_ref[head] = to[:, :keys]
    doc_i = jnp.broadcast_to(doc_i_ref[...].astype(F32), (rows, rows)).T
    mix = jnp.zeros((rows, width), F32)
    for head in range(heads):
        q = q_all[head]
        parts = []
        for start in range(0, keys, BLOCK):
            key_block = kv_ref[start : start + BLOCK, :width]
            first = win - 2 * BLOCK - start
            pq = only_head(pq_ref[:, first : first + 2 * BLOCK], head, 0)
            off = dot(key_block, pq, 1, 0)
            off = pltpu.roll(off, BLOCK, 1, stride=1, stride_axis=0)
            s = dot(q, key_block, 1, 1) + to_ref[head, :, start : start + BLOCK]
            s = s + off[:, :BLOCK].T
            same = doc_i == doc_j_ref[:, start : start + BLOCK]
            parts.append(jnp.where(same, s, NEG))
        s = jnp.concatenate(parts, axis=1)
        e = jnp.exp(s - jnp.max(s, axis=1, keepdims=True))
        p = (e / jnp.sum(e, axis=1, keepdims=True)).astype(BF16)
        p_ref[head] = p
        mix = jnp.where(head_mask(mix.shape, head), dot(p, kv_ref[:, width:], 1, 0), mix)
    mix_ref[...] = mix.astype(BF16)


def attended_kernel(skip, mix_ref, full_ref, part_ref):
    attn = full_ref[:, skip : skip + mix_ref.shape[1]]
    part_ref[...] = dot(mix_ref[...], attn, 1, 1).astype(BF16)


def feed_kernel(rows_of, stream_ref, *refs):
    pieces, rest = refs[:4], refs[4:]
    vec_ref, in_ref, out_ref = rest[:3]
    pre_ref, hidden_ref, low_ref, slope_ref, active_ref, part_ref = rest[3:]
    gain, bias = rows_of
    pre = stream_ref[...].astype(F32) + sum_pieces(pieces)
    pre_ref[...] = pre
    unit, _ = unit_of(pre)
    hidden = unit * vec_ref[gain : gain + 1, :] + vec_ref[bias : bias + 1, :]
    hidden_ref[...] = hidden
    low = hidden.astype(BF16)
    low_ref[...] = low
    inner = dot(low, in_ref[...], 1, 0)
    below = 0.5 * (1.0 + lax.erf(inner * math.sqrt(0.5)))
    bell = jnp.exp(-0.5 * inner * inner) * (1.0 / math.sqrt(2.0 * math.pi))
    slope_ref[...] = below + inner * bell
    active = (inner * below).astype(BF16)
    active_ref[...] = active
    part_ref[...] = dot(active, out_ref[...], 1, 1).astype(BF16)


def turn_kernel(rows_of, hidden_ref, *refs):
    pieces, (vec_ref, slope_ref, in_ref, out_w_ref, grad_ref) = refs[:4], refs[4:9]
    out_ref, d_pre_ref, d_low_ref, d_inner_ref, part_ref, norm_ref, arrived, sem = refs[9:]
    copy = pltpu.make_async_copy(grad_ref, arrived, sem)
    copy.start()
    gain, bias = rows_of
    pre = hidden_ref[...] + sum_pieces(pieces)
    unit, inverse = unit_of(pre)
    gain_vec = vec_ref[gain : gain + 1, :]
    out_ref[...] = (unit * gain_vec + vec_ref[bias : bias + 1, :]).astype(BF16)
    copy.wait()
    grad = arrived[...].astype(F32)
    scaled = grad * gain_vec
    back = (
        scaled
        - jnp.mean(scaled, axis=-1, keepdims=True)
        - unit * jnp.mean(scaled * unit, axis=-1, keepdims=True)
    ) * inverse
    column_sums(norm_ref, grad * unit, grad)
    d_pre_ref[...] = back
    low = back.astype(BF16)
    d_low_ref[...] = low
    inner = (dot(low, out_w_ref[...], 1, 0) * slope_ref[...]).astype(BF16)
    d_inner_ref[...] = inner
    part_ref[...] = dot(inner, in_ref[...], 1, 1).astype(BF16)


def column_sums(ref, first, second):
    ref[...] = jnp.zeros_like(ref)
    ref[0:1, :] = jnp.sum(first, axis=0, keepdims=True)
    ref[1:2, :] = jnp.sum(second, axis=0, keepdims=True)


def feed_back_kernel(gain, grad_ref, *refs):
    pieces, rest = refs[:4], refs[4:]
    pre_ref, vec_ref, slope_ref, in_ref, out_ref = rest[:5]
    d_pre_ref, d_low_ref, d_inner_ref, part_ref, norm_ref = rest[5:]
    grad = grad_ref[...] + sum_pieces(pieces)
    back, gain_terms = normalize_back(pre_ref[...], vec_ref[gain : gain + 1, :], grad)
    column_sums(norm_ref, gain_terms, grad)
    d_pre_ref[...] = back
    low = back.astype(BF16)
    d_low_ref[...] = low
    inner = (dot(low, out_ref[...], 1, 0) * slope_ref[...]).astype(BF16)
    d_inner_ref[...] = inner
    part_ref[...] = dot(inner, in_ref[...], 1, 1).astype(BF16)


def attention_back_kernel(gain, skip, scale, place_ref, *refs):
    pieces, rest = refs[:4], refs[4:]
    d_out_ref, pre_ref, vec_ref, full_ref, q_ref, kv_ref, pk_ref, pq_ref, p_ref = rest[:9]
    d_pre_ref, d_low_ref, dq_ref, dpk_ref, dpq_ref, norm_ref = rest[9:15]
    ds_all, to_all, dk_pos, dm_all, q_all, qr_all, dpq_sum, dkv = rest[-8:]
    dkv_refs = rest[15:-8]
    rows, width = q_ref.shape
    keys = kv_ref.shape[0]
    heads = width // HEAD_DIM
    win = pk_ref.shape[1]

    grad = d_out_ref[...] + sum_pieces(pieces)
    back, gain_terms = normalize_back(pre_ref[...], vec_ref[gain : gain + 1, :], grad)
    column_sums(norm_ref, gain_terms, grad)
    d_pre_ref[...] = back
    d_low = back.astype(BF16)
    d_low_ref[...] = d_low
    d_mixture = dot(d_low, full_ref[:, skip : skip + width], 1, 0)

    row = lax.broadcasted_iota(jnp.int32, (rows, rows), 0)
    col = lax.broadcasted_iota(jnp.int32, (rows, rows), 1)
    flip = jnp.where(row + col == rows - 1, 1.0, 0.0).astype(BF16)
    q_back = dot(flip, q_ref[...], 1, 0)
    content = jnp.zeros((rows, width), F32)
    position = jnp.zeros((rows, width), F32)
    dpq_sum[...] = jnp.zeros_like(dpq_sum)
    for head in range(heads):
        here = slice(head * rows, (head + 1) * rows)
        mask = head_mask((rows, width), head)
        dm = only_head(d_mixture, head)
        dm_all[here, :] = dm
        q_all[here, :] = only_head(q_ref[...], head)
        qr_all[here, :] = only_head(q_back, head)
        p = p_ref[head].astype(F32)
        da = dot(dm, kv_ref[:, width:], 1, 1)
        ds = (p * (da - jnp.sum(p * da, axis=1, keepdims=True))).astype(BF16)
        ds_all[here, :] = ds
        content = jnp.where(mask, dot(ds, kv_ref[:, :width], 1, 0), content)
        ds_back = dot(flip, ds, 1, 0)
        to = jnp.concatenate([ds_back, jnp.zeros((rows, win - keys), F32)], axis=1)
        to = pltpu.roll(to, 0, 1, stride=1, stride_axis=0).astype(BF16)
        to_all[here, :] = to
        position = jnp.where(mask, dot(to, pk_ref[...], 1, 1), position)
        for start in range(0, keys, BLOCK):
            off = ds_back[:, start : start + BLOCK].T
            off = jnp.concatenate([off, jnp.zeros((BLOCK, BLOCK), F32)], axis=1)
            off = pltpu.roll(off, 0, 1, stride=1, stride_axis=0).astype(BF16)
            key_block = only_head(kv_ref[start : start + BLOCK, :width], head)
            dpq_sum[start : start + 2 * BLOCK, :] += dot(off, key_block, 0, 0)
            more = dot(off, pq_ref[:, start : start + 2 * BLOCK], 1, 1)
            if head:
                more = jnp.where(
                    head_mask(more.shape, head), more, dk_pos[start : start + BLOCK, :]
                )
            dk_pos[start : start + BLOCK, :] = more
    high = position.astype(BF16)
    low = (position - high.astype(F32)).astype(BF16)
    dq = content + dot(flip, high, 1, 0) + dot(flip, low, 1, 0)
    dq_ref[...] = (scale * dq).astype(BF16)
    dkv[:, :width] = (dot(ds_all[...], q_all[...], 0, 0) + dk_pos[...]).astype(BF16)
    p_all = p_ref[...].reshape(heads * rows, keys)
    dkv[:, width:] = dot(p_all, dm_all[...], 0, 0).astype(BF16)
    x_count = len(dkv_refs)
    zl_count = keys // (rows * x_count)
    for shift, target in enumerate(dkv_refs):
        x = lax.rem(place_ref[1] + shift, x_count)
        for side in range(zl_count):
            zl = lax.rem(place_ref[2] + side, zl_count)
            start = pl.multiple_of((x * zl_count + zl) * rows, rows)
            target[side * rows : (side + 1) * rows, :] = dkv[pl.ds(start, rows), :]
    dpk_ref[...] = dot(to_all[...], qr_all[...], 0, 0).astype(BF16)
    dpq_ref[...] = (scale * dpq_sum[...]).astype(BF16)


def position_back_kernel(table_ref, dpk_ref, dpq_ref, low_ref, rows_ref):
    width = dpk_ref.shape[1]
    d_k = dot(table_ref[0], dpk_ref[...], 1, 0).astype(BF16)
    d_q = dot(table_ref[2], dpq_ref[...], 1, 0).astype(BF16)
    low_ref[:, :width] = d_q
    low_ref[:, width:] = d_k
    owners, step = rows_ref.shape[0], rows_ref.shape[1] // 2
    for owner in range(owners):
        rows_ref[owner, :step, :] = d_q[owner * step : (owner + 1) * step, :]
        rows_ref[owner, step:, :] = d_k[owner * step : (owner + 1) * step, :]


def relative_sums_kernel(unit_ref, *refs):
    out_ref = refs[-1]
    width = refs[0].shape[1] // 2
    total = None
    for pos_ref, qkv_ref in zip(refs[:-1:2], refs[1:-1:2]):
        term = dot(pos_ref[...], qkv_ref[:, : 2 * width], 1, 1)
        total = term if total is None else total + term
    column_sums(out_ref, total * unit_ref[...], total)


def picked_columns(ref, core, parts=2):
    run = ref.shape[1] // (2 * parts)
    picked = [ref[:, pl.ds(pl.multiple_of((2 * i + core) * run, run), run)] for i in range(parts)]
    return jnp.concatenate(picked, axis=1)


def scatter_kernel(own_core, names, x_first, place_ref, *refs):
    refs = list(refs)
    core = place_ref[3] if own_core else 1 - place_ref[3]
    parts = []
    for name in names:
        if name == "qkv":
            low_ref, all_ref, rel_ref, pos_ref = refs[:4]
            del refs[:4]
            value = dot(picked_columns(low_ref, core), all_ref[...], 0, 0)
            terms = dot(picked_columns(rel_ref, core), pos_ref[...], 0, 0)
            wide = pos_ref.shape[1]
            parts += [value[:, :wide] + terms, value[:, wide:]]
        elif name == "norm":
            hid = picked_columns(refs.pop(0), core)
            out = picked_columns(refs.pop(0), core)
            rel = picked_columns(refs.pop(0), core)
            rows = [hid[0:1], out[0:1], hid[1:2], out[1:2], rel[0:2]]
            rows.append(jnp.zeros((LANES - 6, hid.shape[1]), F32))
            rows = jnp.concatenate(rows, axis=0)
            parts.append(rows.T)
        elif name == "pos":
            rows_ref = refs.pop(0)
            run = rows_ref.shape[0] // 4
            picked = [rows_ref[pl.ds((2 * i + core) * run, run)] for i in range(2)]
            picked = jnp.concatenate(picked, axis=0).astype(F32)
            parts.append(picked.reshape(-1, rows_ref.shape[2]))
        else:
            left, right = refs[:2]
            del refs[:2]
            parts.append(dot(picked_columns(left, core), right[...], 0, 0))
    if not own_core:
        out_ref = refs[0]
        at = 0
        for part in parts:
            out_ref[:, at : at + part.shape[1]] = part.astype(BF16)
            at += part.shape[1]
        return
    arrived, outs, scr = refs[0], refs[1:-1], refs[-1]
    if x_first is None:
        outs = ()
    at = 0
    for part in parts:
        cols = part.shape[1]
        scr[:, at : at + cols] = (part + arrived[:, at : at + cols].astype(F32)).astype(BF16)
        at += cols
    if not outs:
        return
    count = len(outs)
    own = outs[0].shape[0] // count
    zl_count = scr.shape[0] // (own * count * 2)
    for shift, out_ref in enumerate(outs):
        near = lax.rem(place_ref[1 if x_first else 4] + shift, count)
        for far in range(count):
            x, z = (near, far) if x_first else (far, near)
            zh, zl = lax.div(z, zl_count), lax.rem(z, zl_count)
            start = pl.multiple_of(((zh * count + x) * zl_count + zl) * own, own)
            out_ref[far * own : (far + 1) * own, :] = scr[pl.ds(start, own), :]


def last_own_kernel(dims, names, ways, place_ref, *refs):
    count = 2 * len(ways)
    ins, outs, scr = refs[: -count - 1], refs[-count - 1 : -1], refs[-1]
    scatter_kernel(True, names, None, place_ref, *ins, scr)
    _, x_count, zh_count, zl_count, own = dims
    for lot, (x_first, pairing) in enumerate(ways):
        keep_ref, send_ref = outs[2 * lot : 2 * lot + 2]
        half, cols = keep_ref.shape
        xs, zs = ring_order(place_ref[1], pairing), ring_order(place_ref[4], pairing)
        for i, z in enumerate(zs):
            zh, zl = lax.div(z, zl_count), lax.rem(z, zl_count)
            for j, x in enumerate(xs):
                place = (i * x_count + j if x_first else j * len(zs) + i) * own
                target = keep_ref if place < half else send_ref
                start = pl.multiple_of(((zh * x_count + x) * zl_count + zl) * own, own)
                rows = scr[pl.ds(start, own), lot * cols : (lot + 1) * cols]
                target[place % half : place % half + own, :] = rows


def halve_kernel(count, *refs):
    for lot in range(count):
        total = refs[2 * lot][...].astype(F32) + refs[2 * lot + 1][...].astype(F32)
        keep_ref, send_ref = refs[2 * (count + lot) : 2 * (count + lot) + 2]
        half = keep_ref.shape[0]
        keep_ref[...] = total[:half].astype(BF16)
        send_ref[...] = total[half:].astype(BF16)


def middle_kernel(count, x_first, place_ref, *refs):
    pieces, outs, scr = refs[:count], refs[count:-1], refs[-1]
    total = pieces[0][...].astype(F32)
    for piece in pieces[1:]:
        total = total + piece[...].astype(F32)
    scr[...] = total.astype(BF16)
    own = outs[0].shape[0]
    for shift, out_ref in enumerate(outs):
        far = lax.rem(place_ref[4 if x_first else 1] + shift, len(outs))
        out_ref[...] = scr[pl.ds(pl.multiple_of(far * own, own), own), :]


def halves_kernel(count, *refs):
    pieces, (mine_ref, other_ref) = refs[:count], refs[count:]
    total = pieces[0][...].astype(F32)
    for piece in pieces[1:]:
        total = total + piece[...].astype(F32)
    rows = mine_ref.shape[0]
    mine_ref[...] = total[:rows, :]
    other_ref[...] = total[rows:, :].astype(BF16)


def stream_back_kernel(skip, dq_ref, mine_ref, other_ref, qkv_ref, all_ref, part_ref):
    total = mine_ref[...] + other_ref[...].astype(F32)
    both = jnp.concatenate([dq_ref[...], total.astype(BF16)], axis=1)
    all_ref[...] = both
    qkv = qkv_ref[:, skip : skip + both.shape[1]]
    part_ref[...] = dot(both, qkv, 1, 1).astype(BF16)


def total_of(refs, first, cols):
    total = refs[0][:, first : first + cols].astype(F32)
    for ref in refs[1:]:
        total = total + ref[:, first : first + cols].astype(F32)
    return total


def total_kernel(*refs):
    refs[-1][...] = total_of(refs[:-1], 0, refs[-1].shape[1])


def groups_of(counts, refs):
    return [refs[sum(counts[:i]) : sum(counts[: i + 1])] for i in range(len(counts))]


def early_end_kernel(counts, firsts, *refs):
    in_ref, out_ref = refs[-2:]
    hidden = in_ref.shape[2]
    for layer, pieces in enumerate(groups_of(counts, refs)):
        in_ref[layer] = total_of(pieces, firsts[layer], hidden)
        out_ref[layer] = total_of(pieces, firsts[layer] + hidden, hidden)


def middle_end_kernel(counts, firsts, *refs):
    attn_ref, gain_ref, bias_ref = refs[-3:]
    width = attn_ref.shape[2]
    for layer, pieces in enumerate(groups_of(counts, refs)):
        attn_ref[layer] = total_of(pieces, firsts[layer], width)
        norms = total_of(pieces, firsts[layer] + width, LANES).T
        gain_ref[layer] = norms[0:2, :]
        bias_ref[layer] = norms[2:4, :]


def late_end_kernel(qkv_at, early_at, *refs):
    lots, (qkv_ref, in_ref, out_ref) = refs[:-3], refs[-3:]
    width, hidden = qkv_ref.shape[3], in_ref.shape[2]
    totals = [
        lots[i][...].astype(F32) + lots[i + 1][...].astype(F32) for i in range(0, len(lots), 2)
    ]
    total = jnp.concatenate(totals, axis=1)
    for layer, (first, second) in enumerate(zip(qkv_at, early_at)):
        for i in range(3):
            at = first + i * width
            qkv_ref[layer, i] = total[:, at : at + width]
        in_ref[layer] = total[:, second : second + hidden]
        out_ref[layer] = total[:, second + hidden : second + 2 * hidden]


def relative_term_kernel(counts, firsts, skips, width, *refs):
    out_ref = refs[-1]
    layers = len(counts)
    total = None
    for layer, pieces in enumerate(groups_of(counts, refs)):
        qkv_ref, skip = refs[sum(counts) + layer], skips[layer]
        moved = total_of(pieces, firsts[layer], width).astype(BF16)
        step = moved.shape[0] // 2
        term = dot(moved[:step], qkv_ref[:, skip : skip + width], 1, 1)
        term = term + dot(moved[step:], qkv_ref[:, skip + width : skip + 2 * width], 1, 1)
        total = term if total is None else total + term
    out_ref[: total.shape[0], :] = total
    sums = total_of(groups_of(counts, refs)[0], firsts[0] - LANES, LANES).T
    rest = jnp.zeros((8, total.shape[1] - sums.shape[1]), F32)
    out_ref[total.shape[0] :, :] = jnp.concatenate([sums[:8], rest], axis=1)


def token_end_kernel(grad_ref, *refs):
    refs[-1][...] = (grad_ref[...] + sum_pieces(refs[:-1])).astype(BF16)


def relative_end_kernel(gain, *refs):
    pieces, (rel_ref, vec_ref, grad_ref, ends_ref) = refs[:4], refs[4:]
    total = sum_pieces(pieces)
    rows = rel_ref.shape[0]
    back, _ = normalize_back(
        rel_ref[...].astype(F32), vec_ref[gain : gain + 1, :], total[:rows]
    )
    grad_ref[...] = back
    ends_ref[...] = total[rows : rows + 8, :LANES]


def shifted(values, axes, shift):
    count = lax.axis_size(axes)
    return lax.ppermute(values, axes, [(i, (i + shift) % count) for i in range(count)])


def ctx_shifted(values):
    x_count, zl_count = lax.axis_size("x"), lax.axis_size("zl")
    shifts = ctx_shifts(x_count, zl_count)
    moved = [values[0]]
    for i in reversed(range(1, len(shifts))):
        dx, dz = shifts[i]
        pairs = []
        for x in range(x_count):
            for z in range(zl_count):
                target = (x + dx) % x_count * zl_count + (z + dz) % zl_count
                pairs.append((x * zl_count + z, target))
        moved.insert(1, lax.ppermute(values[i], CTX, pairs))
    return moved


def tp_pieces(low):
    count = lax.axis_size("tp")
    order = sorted(range(1, count), key=lambda s: -min(s, count - s))
    moved = {s: shifted(low, "tp", s) for s in order}
    return [low] + [moved[s] for s in range(1, count)]


def moved_on(pieces, axes):
    count = len(pieces)
    order = sorted(range(1, count), key=lambda s: -min(s, count - s))
    moved = {s: shifted(pieces[s], axes, s) for s in order}
    return [pieces[0]] + [moved[s] for s in range(1, count)]


def local(
    tokens,
    cotangent,
    w_qkv,
    w_attn,
    w_in,
    w_out,
    ln_gain,
    ln_bias,
    rel_emb,
    rel_gain,
    rel_bias,
    doc_ids,
    rel_bucket,
):
    _, rows, model = tokens.shape
    layers, _, own, width = w_qkv.shape
    hidden_units = w_in.shape[2]
    heads = width // HEAD_DIM
    ctx_count = lax.axis_size(CTX)
    owners = lax.axis_size(OWNERS)
    length = rows * ctx_count
    row_start = lax.axis_index(CTX) * rows
    scale = 1.0 / math.sqrt(3.0 * HEAD_DIM)
    win = length + rows
    rel_own = rel_emb.shape[0]
    buckets = rel_own * owners
    wide = 3 * width

    shape = (lax.axis_size("x"), lax.axis_size("zl"))
    x_count, z_count = lax.axis_size("x"), lax.axis_size(ZED)
    dims = (lax.axis_size("core"), x_count, lax.axis_size("zh"), lax.axis_size("zl"), own)
    plane = lax.axis_size(PLANE)
    place = [("zh", "core"), "x", "zl", "core", ZED]
    place = jnp.stack([lax.axis_index(axes) for axes in place]).astype(jnp.int32)
    dma = pltpu.SemaphoreType.DMA

    previous = []

    def run(*args, after=(), **kwargs):
        outs = call(*args, after=(*previous, *after), **kwargs)
        previous[:] = [outs[-1]]
        return outs

    attn_rows, out_rows = jnp.swapaxes(w_attn, 1, 2), jnp.swapaxes(w_out, 1, 2)
    table = [{"qkv0": wide, "attn0": width}, {"in0": hidden_units}, {"out0": hidden_units}, {}]
    for layer in range(1, layers):
        table[1]["qkv%d" % layer] = wide
        table[2]["in%d" % layer] = hidden_units
        table[3].update({"out%d" % layer: hidden_units, "attn%d" % layer: width})
    ways = [START_WAY, (True, 1), (False, 0), (False, 1)]
    sources = {"attn": attn_rows, "in": w_in, "out": out_rows}

    def listed(table, at):
        arrays, index, columns = [], [], {}
        for name, cols in table.items():
            kind, layer = name[:-1], int(name[-1])
            columns[name] = at
            at += cols
            if kind == "qkv":
                arrays += [w_qkv] * 3
                index += [(layer, i) for i in range(3)]
            else:
                arrays.append(sources[kind])
                index.append(layer)
        return arrays, index, columns, at

    one_arrays, one_index, one_at, one_cols = listed(table[0], LANES + model // 2)
    vectors = [rel_emb, ln_gain, ln_bias, rel_gain[None], rel_bias[None], doc_ids]

    found = {name: (0, at) for name, at in one_at.items()}
    arrays, other_index, sizes = list(one_arrays), [], []
    for lot in range(1, len(table)):
        more, index, columns, cols = listed(table[lot], 0)
        found.update({name: (lot, at) for name, at in columns.items()})
        arrays += more
        other_index.append(index)
        sizes.append(cols)

    def pack_start(*refs):
        pack_start_kernel(*refs[:6], one_index, other_index, *refs[6:])

    lots = run(
        pack_start,
        [((own, cols), BF16) for cols in sizes + [one_cols]],
        vectors + arrays,
        hbm=range(len(vectors) + len(arrays)),
        scratch=[
            pltpu.VMEM((LANES, LANES), F32),
            pltpu.VMEM(ln_gain.shape, BF16),
            pltpu.VMEM(ln_bias.shape, BF16),
            pltpu.VMEM((1, own), BF16),
            pltpu.VMEM((1, own), BF16),
            pltpu.VMEM((1, rows), jnp.int32),
            dma((7 + len(arrays),)),
        ],
        name="pack_start",
    )
    lots = [lots[-1], *lots[:-1]]

    padded = jnp.pad(rel_bucket, (1, 1), mode="edge")
    to_index = lax.dynamic_slice_in_dim(padded, row_start, win, 0)
    from_index = lax.dynamic_slice_in_dim(padded, length - rows - row_start + 1, win, 0)
    index = jnp.stack([to_index[::-1], from_index[::-1], from_index])
    (tables,) = run(table_kernel, [((3, buckets, win), BF16)], [index], limit=8, name="tables")

    even, odd = [(0, 1), (1, 0), (2, 3), (3, 2)], [(1, 2), (2, 1), (3, 0), (0, 3)]
    for step in range(4):
        moved = []
        for lot, (x_first, pairing) in zip(lots, ways):
            axes = "x" if x_first == (step < 2) else ZED
            moved.append(lax.ppermute(lot, axes, odd if pairing ^ (step % 2) else even))
        both = [piece for pair in zip(lots, moved) for piece in pair]
        shapes = [((2 * lot.shape[0], lot.shape[1]), BF16) for lot in lots]
        lots = list(run(stack_kernel, shapes, both, limit=16, name="stack"))
    for i in range(4):
        lots[i] = [lots[i], shifted(lots[i], "core", 1)]
    one_pieces = lots[0]
    qkv, attn, small, q, key_value = run(
        functools.partial(start_kernel, dims, scale, [one_at["qkv0"], one_at["attn0"], 0]),
        [
            ((model, wide), BF16),
            ((model, width), BF16),
            ((model, LANES), BF16),
            ((rows, width), BF16),
            ((rows, 2 * width), BF16),
        ],
        [place, tokens[0], *one_pieces],
        smem=(0,),
        anys=range(2, 2 + len(one_pieces)),
        hbm=(1,),
        scratch=[pltpu.VMEM((rows, model), BF16), dma((3 * owners + 1,))],
        name="start",
    )
    rel_low, rel_unit, vecs, doc_j = run(
        functools.partial(relative_kernel, dims, layers),
        [
            ((buckets, model), BF16),
            ((buckets, model), F32),
            ((16, model), F32),
            ((1, length), F32),
        ],
        [place, small, *one_pieces],
        smem=(0,),
        anys=range(2, 2 + len(one_pieces)),
        limit=16,
        scratch=[pltpu.VMEM((buckets, model), BF16), dma((2 * owners,))],
        name="relative",
    )

    def rest(names):
        lot = found[names[0]][0]
        return run(
            functools.partial(rest_kernel, dims, ways[lot], [found[name][1] for name in names]),
            [((model, table[lot][name]), BF16) for name in names],
            [place, *lots[lot]],
            smem=(0,),
            anys=(1, 2),
            scratch=[dma((len(names) * owners,))],
            name="rest",
        )

    qkvs, attns, ins, outs = [qkv], [attn], [], []

    token_low = tokens[0]
    stream = token_low
    kept = []
    hidden, pieces = None, None
    tile = (rows, model)
    for layer in range(layers):
        if layer:
            pre_out, stream, stream_low, q, key_value = run(
                functools.partial(
                    project_kernel,
                    scale,
                    (2 * layer - 1, 2 * layers + 2 * layer - 1),
                    0,
                ),
                [
                    (tile, F32),
                    (tile, F32),
                    (tile, BF16),
                    ((rows, width), BF16),
                    ((rows, 2 * width), BF16),
                ],
                [hidden, *pieces, vecs, qkvs[layer]],
                name="project",
            )
            kept[-1]["pre_out"] = pre_out
        else:
            stream_low = token_low
        blocks = ctx_shifted([key_value] * ctx_count)
        pk, pq_rev, pq = run(
            functools.partial(position_kernel, scale, 0),
            [((width, win), BF16)] * 3,
            [rel_low, qkvs[layer], tables],
            name="position",
        )
        (kv,) = run(
            functools.partial(gather_kernel, shape),
            [((length, 2 * width), BF16)],
            [place, *blocks],
            smem=(0,),
            anys=range(1, 1 + ctx_count),
            scratch=[dma((ctx_count,))],
            name="gather",
        )
        mixture, p = run(
            attention_kernel,
            [((rows, width), BF16), ((heads, rows, length), BF16)],
            [q, kv, pk, pq_rev, doc_ids, doc_j],
            scratch=[
                pltpu.VMEM((heads, rows, length), F32),
                pltpu.VMEM((heads, rows, width), BF16),
            ],
            limit=16,
            name="attention",
        )
        (part,) = run(
            functools.partial(attended_kernel, 0),
            [(tile, BF16)],
            [mixture, attns[layer]],
            name="attended",
        )
        pieces = tp_pieces(part)
        ins += rest(["in%d" % layer])
        outs += rest(["out%d" % layer])
        pre_hidden, hidden, hidden_low, slope, active, part = run(
            functools.partial(feed_kernel, (2 * layer, 2 * layers + 2 * layer)),
            [
                (tile, F32),
                (tile, F32),
                (tile, BF16),
                ((rows, hidden_units), F32),
                ((rows, hidden_units), BF16),
                (tile, BF16),
            ],
            [stream, *pieces, vecs, ins[layer], outs[layer]],
            name="feed",
        )
        pieces = tp_pieces(part)
        if layer + 1 < layers:
            qkvs += rest(["qkv%d" % (layer + 1)])
            attns += rest(["attn%d" % (layer + 1)])
        kept.append(
            dict(
                stream_low=stream_low,
                q=q,
                kv=kv,
                pk=pk,
                pq=pq,
                p=p,
                mixture=mixture,
                pre_hidden=pre_hidden,
                hidden_low=hidden_low,
                slope=slope,
                active=active,
            )
        )
    last = layers - 1
    turned = run(
        functools.partial(turn_kernel, (2 * last + 1, 2 * layers + 2 * last + 1)),
        [
            (tile, BF16),
            (tile, F32),
            (tile, BF16),
            ((rows, hidden_units), BF16),
            (tile, BF16),
            ((8, model), F32),
        ],
        [hidden, *pieces, vecs, kept[-1]["slope"], ins[-1], outs[-1], cotangent[0]],
        hbm=(9,),
        scratch=[pltpu.VMEM((rows, model), BF16), dma],
        name="turn",
    )
    out_local = turned[0]

    grad_parts = None
    x_count = lax.axis_size("x")

    def scatter_other(names, ins, cols, label):
        (other,) = run(
            functools.partial(scatter_kernel, False, names, False),
            [((model // 2, cols), BF16)],
            [place, *ins],
            smem=(0,),
            limit=30,
            name=label + "_other",
        )
        return shifted(other, "core", 1)

    def scatter_own(names, ins, arrived, label, x_first=False, after=()):
        half, cols = arrived.shape
        pieces = run(
            functools.partial(scatter_kernel, True, names, x_first),
            [((half // z_count, cols), BF16)] * z_count,
            [place, *ins, arrived],
            smem=(0,),
            scratch=[pltpu.VMEM((half, cols), BF16)],
            after=after,
            limit=16,
            name=label + "_own",
        )
        return moved_on(pieces, "x" if x_first else ZED)

    def scatter_middle(pieces, label, x_first=False):
        rows_here, cols = pieces[0].shape
        pieces = run(
            functools.partial(middle_kernel, len(pieces), x_first),
            [((rows_here // x_count, cols), BF16)] * x_count,
            [place, *pieces],
            smem=(0,),
            scratch=[pltpu.VMEM((rows_here, cols), BF16)],
            name=label + "_middle",
        )
        return moved_on(pieces, ZED if x_first else "x")

    def scatter_total(pieces, label):
        return list(run(total_kernel, [(pieces[0].shape, F32)], pieces, name=label + "_total"))

    early_names, early_cols = ("in", "out"), 2 * hidden_units
    middle_names, middle_cols = ("attn", "norm", "pos"), 2 * width + LANES
    early_ins, middle_ins, late_ins, pos_lows = [], [], [], []
    for layer in reversed(range(layers)):
        k = kept[layer]
        if grad_parts is None:
            d_pre_out, d_out_low, d_inner, part, norm_out = turned[1:]
        else:
            d_pre_out, d_out_low, d_inner, part, norm_out = run(
                functools.partial(feed_back_kernel, 2 * layer + 1),
                [
                    (tile, F32),
                    (tile, BF16),
                    ((rows, hidden_units), BF16),
                    (tile, BF16),
                    ((8, model), F32),
                ],
                [*grad_parts, k["pre_out"], vecs, k["slope"], ins[layer], outs[layer]],
                name="feed_back",
            )
        pieces = tp_pieces(part)
        early_in = [k["hidden_low"], d_inner, d_out_low, k["active"]]
        early_ins += early_in
        backs = run(
            functools.partial(attention_back_kernel, 2 * layer, 0, scale),
            [
                (tile, F32),
                (tile, BF16),
                ((rows, width), BF16),
                ((win, width), BF16),
                ((win, width), BF16),
                ((8, model), F32),
            ]
            + [((length // x_count, 2 * width), BF16)] * x_count,
            [place, *pieces, d_pre_out, k["pre_hidden"], vecs, attns[layer]]
            + [k["q"], k["kv"], k["pk"], k["pq"], k["p"]],
            smem=(0,),
            scratch=[
                pltpu.VMEM((heads * rows, length), BF16),
                pltpu.VMEM((heads * rows, win), BF16),
                pltpu.VMEM((length, width), F32),
                pltpu.VMEM((heads * rows, width), BF16),
                pltpu.VMEM((heads * rows, width), BF16),
                pltpu.VMEM((heads * rows, width), BF16),
                pltpu.VMEM((win, width), F32),
                pltpu.VMEM((length, 2 * width), BF16),
            ],
            limit=20,
            name="attention_back",
        )
        d_pre_hidden, d_attended, dq, dpk, dpq, norm_hidden = backs[:6]
        dkv = moved_on(backs[6:], "x")
        pos_low, pos_rows = run(
            position_back_kernel,
            [((buckets, 2 * width), BF16), ((owners, 2 * rel_own, width), BF16)],
            [tables, dpk, dpq],
            name="position_back",
        )
        pos_lows.append(pos_low)
        norm_rel = jnp.zeros((8, model), F32)
        if not layer:
            pairs = [item for pair in zip(pos_lows, qkvs[::-1]) for item in pair]
            (norm_rel,) = run(
                relative_sums_kernel,
                [((8, model), F32)],
                [rel_unit, *pairs],
                limit=16,
                name="relative_sums",
            )
        middle_ins += [d_attended, k["mixture"], norm_hidden, norm_out, norm_rel, pos_rows]
        if not layer:
            arrived = scatter_other(
                middle_names * layers, middle_ins, middle_cols * layers, "middle"
            )
        if not layer:
            middle = scatter_own(middle_names * layers, middle_ins, arrived, "middle")
        mine, other = run(
            functools.partial(halves_kernel, x_count),
            [((rows, 2 * width), F32), ((rows, 2 * width), BF16)],
            dkv,
            name="halves",
        )
        other = shifted(other, "zl", 1)
        if not layer:
            middle = scatter_middle(middle, "middle")
        dqkv, part = run(
            functools.partial(stream_back_kernel, 0),
            [((rows, wide), BF16), (tile, BF16)],
            [dq, mine, other, qkvs[layer]],
            name="stream_back",
        )
        grad_parts = [d_pre_hidden] + tp_pieces(part)
        late_ins += [k["stream_low"], dqkv, rel_low, pos_low]
    late_names, late_cols = ("qkv",) * layers, wide * layers
    late_names, late_cols = late_names + early_names * layers, late_cols + early_cols * layers
    late_ins += early_ins
    arrived = scatter_other(late_names, late_ins, late_cols, "late")
    middle_at = [(layers - 1 - layer) * middle_cols for layer in range(layers)]
    late_at = [(layers - 1 - layer) * wide for layer in range(layers)]

    counts = [len(middle)] * layers
    (term,) = run(
        functools.partial(
            relative_term_kernel,
            counts,
            [at + width + LANES for at in middle_at],
            [0] * layers,
            width,
        ),
        [((rel_own + 8, model), F32)],
        middle * layers + qkvs,
        name="relative_term",
    )
    terms = tp_pieces(term)
    half, lot_cols = model // 2, late_cols // len(ways)
    parts = run(
        functools.partial(last_own_kernel, dims, late_names, ways),
        [((half // 2, lot_cols), BF16)] * (2 * len(ways)),
        [place, *late_ins, arrived],
        smem=(0,),
        scratch=[pltpu.VMEM((half, late_cols), BF16)],
        limit=30,
        name="late_own",
    )

    def sent(parts, step):
        moved = []
        for lot, (x_first, pairing) in enumerate(ways):
            axes = "x" if x_first == (step < 2) else ZED
            pairs = odd if pairing ^ (step % 2) else even
            moved += [parts[2 * lot], lax.ppermute(parts[2 * lot + 1], axes, pairs)]
        return moved

    def halved(parts):
        rows_here = parts[0].shape[0] // 2
        return run(
            functools.partial(halve_kernel, len(ways)),
            [((rows_here, lot_cols), BF16)] * (2 * len(ways)),
            parts,
            name="halve",
        )

    parts = halved(sent(parts, 3))
    parts = sent(parts, 2)
    (grad_tokens,) = run(token_end_kernel, [(tile, BF16)], grad_parts, name="token_end")
    parts = halved(parts)
    parts = sent(parts, 1)
    grad_rel, ends = run(
        functools.partial(relative_end_kernel, 4 * layers),
        [((rel_own, model), F32), ((8, LANES), F32)],
        [*terms, rel_emb, vecs],
        name="relative_end",
    )
    grad_attn, grad_gain, grad_bias = run(
        functools.partial(middle_end_kernel, counts, middle_at),
        [((layers, own, width), F32), ((layers, 2, own), F32), ((layers, 2, own), F32)],
        middle * layers,
        name="middle_end",
    )
    parts = sent(halved(parts), 0)
    grad_qkv, grad_in, grad_out = run(
        functools.partial(
            late_end_kernel,
            late_at,
            [wide * layers + (layers - 1 - layer) * early_cols for layer in range(layers)],
        ),
        [
            ((layers, 3, own, width), F32),
            ((layers, own, hidden_units), F32),
            ((layers, own, hidden_units), F32),
        ],
        parts,
        name="late_end",
    )
    grad_attn, grad_out = jnp.swapaxes(grad_attn, 1, 2), jnp.swapaxes(grad_out, 1, 2)
    return (
        out_local[None],
        grad_tokens[None],
        grad_qkv,
        grad_attn,
        grad_in,
        grad_out,
        grad_gain,
        grad_bias,
        grad_rel,
        ends[4, :own],
        ends[5, :own],
    )


def solution(mesh):
    sizes = mesh.shape
    zh, zl = 2, 2
    finer = Mesh(
        mesh.devices.reshape(zh, sizes["fsdp"] // zh, sizes["ctx"] // zl, zl, sizes["tp"]),
        ("zh", "core", "x", "zl", "tp"),
    )
    own = OWNERS
    fsdp = ("zh", "core")
    return jax.shard_map(
        local,
        mesh=finer,
        in_specs=(
            P(fsdp, CTX, None),
            P(fsdp, CTX, None),
            P(None, None, own, "tp"),
            P(None, "tp", own),
            P(None, own, "tp"),
            P(None, "tp", own),
            P(None, None, own),
            P(None, None, own),
            P(own, None),
            P(own),
            P(own),
            P(fsdp, CTX),
            P(),
        ),
        out_specs=(
            P(fsdp, CTX, None),
            P(fsdp, CTX, None),
            P(None, None, own, "tp"),
            P(None, "tp", own),
            P(None, own, "tp"),
            P(None, "tp", own),
            P(None, None, own),
            P(None, None, own),
            P(own, None),
            P(own),
            P(own),
        ),
        check_vma=False,
    )
```

```python
import functools
import math

import jax
import jax.numpy as jnp
from jax import lax
from jax.experimental import pallas as pl
from jax.experimental.pallas import tpu as pltpu
from jax.sharding import Mesh
from jax.sharding import PartitionSpec as P

HEAD_DIM = 64
EPS = 1e-07
NEG = -1e30
BLOCK = 128
LANES = 128
START_WAY = (True, 0)
F32 = jnp.float32
BF16 = jnp.bfloat16
CTX = ("x", "zl")
ZED = ("zh", "zl")
PLANE = ("zh", "x", "zl")
OWNERS = ("zh", "core", "x", "zl")


def dot(a, b, ca, cb):
    return lax.dot_general(a, b, (((ca,), (cb,)), ((), ())), preferred_element_type=F32)


def call(body, outs, ins, *, anys=(), hbm=(), smem=(), scratch=(), after=(), limit=8, name=None):
    specs = []
    for i in range(len(ins)):
        space = pltpu.VMEM
        if i in anys:
            space = pl.ANY
        if i in hbm:
            space = pltpu.HBM
        if i in smem:
            space = pltpu.SMEM
        specs.append(pl.BlockSpec(memory_space=space))
    count, late = len(ins), len(after)
    specs += [pl.BlockSpec(memory_space=pl.ANY)] * late
    ins = [
        pltpu.with_memory_space_constraint(value, pltpu.HBM) if i in hbm else value
        for i, value in enumerate(ins)
    ]

    def without(*refs):
        body(*refs[:count], *refs[count + late :])

    return pl.pallas_call(
        without,
        in_specs=specs,
        out_specs=tuple(pl.BlockSpec(memory_space=pltpu.VMEM) for _ in outs),
        out_shape=tuple(jax.ShapeDtypeStruct(shape, dtype) for shape, dtype in outs),
        scratch_shapes=list(scratch),
        compiler_params=pltpu.CompilerParams(vmem_limit_bytes=limit << 20),
        name=name,
    )(*ins, *after)


def ctx_shifts(x_count, zl_count):
    pairs = [(dx, dz) for dx in range(x_count) for dz in range(zl_count)]
    return sorted(pairs, key=lambda p: (min(p[0], x_count - p[0]) + p[1], p[1], p[0]))


def ctx_owner(place_ref, shift, sign, x_count, zl_count):
    x = lax.rem(place_ref[1] + (sign * shift[0]) % x_count, x_count)
    zl = lax.rem(place_ref[2] + (sign * shift[1]) % zl_count, zl_count)
    return x * zl_count + zl


def head_mask(shape, head, axis=1):
    index = lax.broadcasted_iota(jnp.int32, shape, axis)
    return (index >= head * HEAD_DIM) & (index < (head + 1) * HEAD_DIM)


def only_head(values, head, axis=1):
    mask = head_mask(values.shape, head, axis)
    return jnp.where(mask, values.astype(F32), 0.0).astype(BF16)


def unit_of(values):
    average = jnp.mean(values, axis=-1, keepdims=True)
    centered = values - average
    spread = jnp.mean(centered * centered, axis=-1, keepdims=True)
    inverse = lax.rsqrt(spread + EPS)
    return centered * inverse, inverse


def normalize_back(values, gain_vec, grad):
    unit, inverse = unit_of(values)
    scaled = grad * gain_vec
    back = (
        scaled
        - jnp.mean(scaled, axis=-1, keepdims=True)
        - unit * jnp.mean(scaled * unit, axis=-1, keepdims=True)
    ) * inverse
    return back, grad * unit


def sum_pieces(pieces):
    parts = [piece[...].astype(F32) for piece in pieces]
    return (parts[0] + parts[2]) + (parts[1] + parts[3])


def run_copies(pairs, sems):
    copies = [
        pltpu.make_async_copy(source, target, sems.at[i])
        for i, (source, target) in enumerate(pairs)
    ]
    for copy in copies:
        copy.start()
    for copy in copies:
        copy.wait()


def pack_start_kernel(rel_ref, gain_ref, bias_ref, rgain_ref, rbias_ref, doc_ref, *refs):
    out_ref, scr, gain, bias, rgain, rbias, doc, sems = refs[-8:]
    index, others, parts = refs[0], refs[1], refs[2:-8]
    parts, other_refs = parts[: -len(others)], parts[-len(others) :]
    layers, _, own = gain_ref.shape
    half = rel_ref.shape[1] // 2
    part = rel_ref.shape[0]
    pairs = [(gain_ref, gain), (bias_ref, bias), (rgain_ref, rgain), (rbias_ref, rbias)]
    pairs += [(doc_ref, doc)]
    at = 0
    for i in range(2):
        pairs.append(
            (
                rel_ref.at[:, pl.ds(i * half, half)],
                out_ref.at[pl.ds(i * part, part), pl.ds(LANES, half)],
            )
        )
    taken = 0
    for leads, target, at in [(index, out_ref, LANES + half)] + [
        (leads, target, 0) for leads, target in zip(others, other_refs)
    ]:
        for lead, ref in zip(leads, parts[taken:]):
            cols = ref.shape[-1]
            pairs.append((ref.at[lead], target.at[:, pl.ds(at, cols)]))
            at += cols
        taken += len(leads)
    run_copies(pairs, sems)
    scr[...] = jnp.zeros_like(scr)
    for layer in range(layers):
        scr[2 * layer : 2 * layer + 2, :own] = gain[layer].astype(F32)
        base = 2 * layers + 2 * layer
        scr[base : base + 2, :own] = bias[layer].astype(F32)
    scr[4 * layers : 4 * layers + 1, :own] = rgain[...].astype(F32)
    scr[4 * layers + 1 : 4 * layers + 2, :own] = rbias[...].astype(F32)
    small = scr[...].T[:own, :]
    row = lax.broadcasted_iota(jnp.int32, small.shape, 0)
    upper = lax.broadcasted_iota(jnp.int32, small.shape, 1) >= LANES // 2
    doc_row = doc[...].astype(F32)
    turned = pltpu.roll(doc_row, LANES // 2, 1)
    small = jnp.where(upper & (row == 0), turned, small)
    small = jnp.where(upper & (row == 1), doc_row, small)
    out_ref[:, :LANES] = small.astype(BF16)


def ring_order(place, pairing):
    even = place + 1 - 2 * lax.rem(place, 2)
    odd = 3 - place
    if pairing:
        return [place, odd, even, 3 - even]
    return [place, even, odd, odd + 1 - 2 * lax.rem(odd, 2)]


def assemble(dims, way, place_ref, pieces, moves, sems, more=()):
    core_count, x_count, zh_count, zl_count, own = dims
    x_first, pairing = way
    core = place_ref[3]
    xs, zs = ring_order(place_ref[1], pairing), ring_order(place_ref[4], pairing)
    pairs = list(more)
    for c_shift, piece in enumerate(pieces):
        from_c = lax.rem(core + c_shift, core_count)
        for i, z in enumerate(zs):
            zh, zl = lax.div(z, zl_count), lax.rem(z, zl_count)
            for j, x in enumerate(xs):
                owner = ((zh * core_count + from_c) * x_count + x) * zl_count + zl
                place = (i * x_count + j if x_first else j * len(zs) + i) * own
                for row, rows, col, cols, target, step, to_col in moves:
                    start = pl.multiple_of(owner * step, step)
                    pairs.append(
                        (
                            piece.at[pl.ds(place + row, rows), pl.ds(col, cols)],
                            target.at[pl.ds(start, rows), pl.ds(to_col, cols)],
                        )
                    )
    run_copies(pairs, sems)


def stack_kernel(*refs):
    count = len(refs) // 3
    for i in range(count):
        one_ref, two_ref, out_ref = refs[2 * i], refs[2 * i + 1], refs[2 * count + i]
        rows = one_ref.shape[0]
        out_ref[:rows, :] = one_ref[...]
        out_ref[rows:, :] = two_ref[...]


def rest_kernel(dims, way, columns, place_ref, one_ref, two_ref, *refs):
    targets, sems = refs[:-1], refs[-1]
    own = dims[-1]
    moves = [
        (0, own, first, target.shape[1], target, own, 0)
        for first, target in zip(columns, targets)
    ]
    assemble(dims, way, place_ref, (one_ref, two_ref), moves, sems)


def start_kernel(dims, scale, columns, place_ref, tokens_ref, *refs):
    pieces, (qkv_ref, attn_ref, small_ref, q_ref, kv_ref, low_ref, sems) = refs[:-7], refs[-7:]
    own = dims[-1]
    width = q_ref.shape[1]
    moves = [
        (0, own, first, target.shape[1], target, own, 0)
        for first, target in zip(columns, (qkv_ref, attn_ref, small_ref))
    ]
    assemble(dims, START_WAY, place_ref, pieces, moves, sems, [(tokens_ref, low_ref)])
    low = low_ref[...]
    kv_ref[...] = dot(low, qkv_ref[:, width:], 1, 0).astype(BF16)
    q_ref[...] = (scale * dot(low, qkv_ref[:, :width], 1, 0)).astype(BF16)


def relative_kernel(dims, layers, place_ref, small_ref, *refs):
    pieces, (low_ref, unit_ref, vec_ref, doc_ref, rel, sems) = refs[:-6], refs[-6:]
    own = dims[-1]
    half = rel.shape[1] // 2
    part = own // 2
    moves = [(i * part, part, LANES, half, rel, part, i * half) for i in range(2)]
    assemble(dims, START_WAY, place_ref, pieces, moves, sems)
    turned = small_ref[...].astype(F32).T[: vec_ref.shape[0], :]
    vec_ref[...] = turned
    unit, _ = unit_of(rel[...].astype(F32))
    unit_ref[...] = unit
    gain, bias = turned[4 * layers : 4 * layers + 1], turned[4 * layers + 1 : 4 * layers + 2]
    low_ref[...] = (unit * gain + bias).astype(BF16)
    blocks = doc_ref.shape[1] // LANES
    span = blocks * own
    start = pl.multiple_of(place_ref[0] * span, span)
    mine = small_ref[pl.ds(start, span), :].astype(F32)
    upper = lax.broadcasted_iota(jnp.int32, (1, LANES), 1) >= LANES // 2
    for block in range(blocks):
        first = pltpu.roll(mine[block * own : block * own + 1, :], LANES // 2, 1)
        second = mine[block * own + 1 : block * own + 2, :]
        doc_ref[:, block * LANES : (block + 1) * LANES] = jnp.where(upper, second, first)


def table_kernel(index_ref, table_ref):
    count, buckets, win = table_ref.shape
    bucket = lax.broadcasted_iota(jnp.int32, (buckets, win), 0)
    for i in range(count):
        same = bucket == index_ref[i : i + 1, :]
        table_ref[i] = jnp.where(same, 1.0, 0.0).astype(BF16)


def position_kernel(scale, skip, rel_ref, qkv_ref, table_ref, pk_ref, pq_rev_ref, pq_ref):
    width = pk_ref.shape[0]
    pos_q = (scale * dot(rel_ref[...], qkv_ref[:, skip : skip + width], 1, 0)).astype(BF16)
    pos_k = dot(rel_ref[...], qkv_ref[:, skip + width : skip + 2 * width], 1, 0).astype(BF16)
    pk_ref[...] = dot(pos_k, table_ref[0], 0, 0).astype(BF16)
    pq_rev_ref[...] = dot(pos_q, table_ref[1], 0, 0).astype(BF16)
    pq_ref[...] = dot(pos_q, table_ref[2], 0, 0).astype(BF16)


def project_kernel(scale, rows_of, skip, hidden_ref, *refs):
    pieces, rest = refs[:4], refs[4:]
    vec_ref, qkv_ref, pre_ref, stream_ref, low_ref, q_ref, kv_ref = rest
    width = q_ref.shape[1]
    gain, bias = rows_of
    pre = hidden_ref[...] + sum_pieces(pieces)
    pre_ref[...] = pre
    unit, _ = unit_of(pre)
    stream = unit * vec_ref[gain : gain + 1, :] + vec_ref[bias : bias + 1, :]
    stream_ref[...] = stream
    low = stream.astype(BF16)
    low_ref[...] = low
    kv_ref[...] = dot(low, qkv_ref[:, skip + width : skip + 3 * width], 1, 0).astype(BF16)
    q_ref[...] = (scale * dot(low, qkv_ref[:, skip : skip + width], 1, 0)).astype(BF16)


def gather_kernel(shape, place_ref, *refs):
    blocks, kv_ref, sems = refs[:-2], refs[-2], refs[-1]
    rows = blocks[0].shape[0]
    pairs = []
    for block, shift in zip(blocks, ctx_shifts(*shape)):
        owner = ctx_owner(place_ref, shift, -1, *shape)
        start = pl.multiple_of(owner * rows, rows)
        pairs.append((block, kv_ref.at[pl.ds(start, rows), :]))
    run_copies(pairs, sems)


def attention_kernel(q_ref, kv_ref, *refs):
    pk_ref, pq_ref, doc_i_ref, doc_j_ref = refs[:4]
    mix_ref, p_ref, to_ref, q_all = refs[4:]
    rows, width = q_ref.shape
    keys = kv_ref.shape[0]
    win = pk_ref.shape[1]
    heads = width // HEAD_DIM
    for head in range(heads):
        q = only_head(q_ref[...], head)
        q_all[head] = q
        to = dot(q, pk_ref[...], 1, 0)
        to = pltpu.roll(to, win + 1 - rows, 1, stride=1, stride_axis=0)
        to_ref[head] = to[:, :keys]
    doc_i = jnp.broadcast_to(doc_i_ref[...].astype(F32), (rows, rows)).T
    mix = jnp.zeros((rows, width), F32)
    for head in range(heads):
        q = q_all[head]
        parts = []
        for start in range(0, keys, BLOCK):
            key_block = kv_ref[start : start + BLOCK, :width]
            first = win - 2 * BLOCK - start
            pq = only_head(pq_ref[:, first : first + 2 * BLOCK], head, 0)
            off = dot(key_block, pq, 1, 0)
            off = pltpu.roll(off, BLOCK, 1, stride=1, stride_axis=0)
            s = dot(q, key_block, 1, 1) + to_ref[head, :, start : start + BLOCK]
            s = s + off[:, :BLOCK].T
            same = doc_i == doc_j_ref[:, start : start + BLOCK]
            parts.append(jnp.where(same, s, NEG))
        s = jnp.concatenate(parts, axis=1)
        e = jnp.exp(s - jnp.max(s, axis=1, keepdims=True))
        p = (e / jnp.sum(e, axis=1, keepdims=True)).astype(BF16)
        p_ref[head] = p
        mix = jnp.where(head_mask(mix.shape, head), dot(p, kv_ref[:, width:], 1, 0), mix)
    mix_ref[...] = mix.astype(BF16)


def attended_kernel(skip, mix_ref, full_ref, part_ref):
    attn = full_ref[:, skip : skip + mix_ref.shape[1]]
    part_ref[...] = dot(mix_ref[...], attn, 1, 1).astype(BF16)


def feed_kernel(rows_of, stream_ref, *refs):
    pieces, rest = refs[:4], refs[4:]
    vec_ref, in_ref, out_ref = rest[:3]
    pre_ref, hidden_ref, low_ref, slope_ref, active_ref, part_ref = rest[3:]
    gain, bias = rows_of
    pre = stream_ref[...].astype(F32) + sum_pieces(pieces)
    pre_ref[...] = pre
    unit, _ = unit_of(pre)
    hidden = unit * vec_ref[gain : gain + 1, :] + vec_ref[bias : bias + 1, :]
    hidden_ref[...] = hidden
    low = hidden.astype(BF16)
    low_ref[...] = low
    inner = dot(low, in_ref[...], 1, 0)
    below = 0.5 * (1.0 + lax.erf(inner * math.sqrt(0.5)))
    bell = jnp.exp(-0.5 * inner * inner) * (1.0 / math.sqrt(2.0 * math.pi))
    slope_ref[...] = below + inner * bell
    active = (inner * below).astype(BF16)
    active_ref[...] = active
    part_ref[...] = dot(active, out_ref[...], 1, 1).astype(BF16)


def turn_kernel(rows_of, hidden_ref, *refs):
    pieces, (vec_ref, slope_ref, in_ref, out_w_ref, grad_ref) = refs[:4], refs[4:9]
    out_ref, d_pre_ref, d_low_ref, d_inner_ref, part_ref, norm_ref, arrived, sem = refs[9:]
    copy = pltpu.make_async_copy(grad_ref, arrived, sem)
    copy.start()
    gain, bias = rows_of
    pre = hidden_ref[...] + sum_pieces(pieces)
    unit, inverse = unit_of(pre)
    gain_vec = vec_ref[gain : gain + 1, :]
    out_ref[...] = (unit * gain_vec + vec_ref[bias : bias + 1, :]).astype(BF16)
    copy.wait()
    grad = arrived[...].astype(F32)
    scaled = grad * gain_vec
    back = (
        scaled
        - jnp.mean(scaled, axis=-1, keepdims=True)
        - unit * jnp.mean(scaled * unit, axis=-1, keepdims=True)
    ) * inverse
    column_sums(norm_ref, grad * unit, grad)
    d_pre_ref[...] = back
    low = back.astype(BF16)
    d_low_ref[...] = low
    inner = (dot(low, out_w_ref[...], 1, 0) * slope_ref[...]).astype(BF16)
    d_inner_ref[...] = inner
    part_ref[...] = dot(inner, in_ref[...], 1, 1).astype(BF16)


def column_sums(ref, first, second):
    ref[...] = jnp.zeros_like(ref)
    ref[0:1, :] = jnp.sum(first, axis=0, keepdims=True)
    ref[1:2, :] = jnp.sum(second, axis=0, keepdims=True)


def feed_back_kernel(gain, grad_ref, *refs):
    pieces, rest = refs[:4], refs[4:]
    pre_ref, vec_ref, slope_ref, in_ref, out_ref = rest[:5]
    d_pre_ref, d_low_ref, d_inner_ref, part_ref, norm_ref = rest[5:]
    grad = grad_ref[...] + sum_pieces(pieces)
    back, gain_terms = normalize_back(pre_ref[...], vec_ref[gain : gain + 1, :], grad)
    column_sums(norm_ref, gain_terms, grad)
    d_pre_ref[...] = back
    low = back.astype(BF16)
    d_low_ref[...] = low
    inner = (dot(low, out_ref[...], 1, 0) * slope_ref[...]).astype(BF16)
    d_inner_ref[...] = inner
    part_ref[...] = dot(inner, in_ref[...], 1, 1).astype(BF16)


def attention_back_kernel(gain, skip, scale, place_ref, *refs):
    pieces, rest = refs[:4], refs[4:]
    d_out_ref, pre_ref, vec_ref, full_ref, q_ref, kv_ref, pk_ref, pq_ref, p_ref = rest[:9]
    d_pre_ref, d_low_ref, dq_ref, dpk_ref, dpq_ref, norm_ref = rest[9:15]
    ds_all, to_all, dk_pos, dm_all, q_all, qr_all, dpq_sum, dkv = rest[-8:]
    dkv_refs = rest[15:-8]
    rows, width = q_ref.shape
    keys = kv_ref.shape[0]
    heads = width // HEAD_DIM
    win = pk_ref.shape[1]

    grad = d_out_ref[...] + sum_pieces(pieces)
    back, gain_terms = normalize_back(pre_ref[...], vec_ref[gain : gain + 1, :], grad)
    column_sums(norm_ref, gain_terms, grad)
    d_pre_ref[...] = back
    d_low = back.astype(BF16)
    d_low_ref[...] = d_low
    d_mixture = dot(d_low, full_ref[:, skip : skip + width], 1, 0)

    row = lax.broadcasted_iota(jnp.int32, (rows, rows), 0)
    col = lax.broadcasted_iota(jnp.int32, (rows, rows), 1)
    flip = jnp.where(row + col == rows - 1, 1.0, 0.0).astype(BF16)
    q_back = dot(flip, q_ref[...], 1, 0)
    content = jnp.zeros((rows, width), F32)
    position = jnp.zeros((rows, width), F32)
    dpq_sum[...] = jnp.zeros_like(dpq_sum)
    for head in range(heads):
        here = slice(head * rows, (head + 1) * rows)
        mask = head_mask((rows, width), head)
        dm = only_head(d_mixture, head)
        dm_all[here, :] = dm
        q_all[here, :] = only_head(q_ref[...], head)
        qr_all[here, :] = only_head(q_back, head)
        p = p_ref[head].astype(F32)
        da = dot(dm, kv_ref[:, width:], 1, 1)
        ds = (p * (da - jnp.sum(p * da, axis=1, keepdims=True))).astype(BF16)
        ds_all[here, :] = ds
        content = jnp.where(mask, dot(ds, kv_ref[:, :width], 1, 0), content)
        ds_back = dot(flip, ds, 1, 0)
        to = jnp.concatenate([ds_back, jnp.zeros((rows, win - keys), F32)], axis=1)
        to = pltpu.roll(to, 0, 1, stride=1, stride_axis=0).astype(BF16)
        to_all[here, :] = to
        position = jnp.where(mask, dot(to, pk_ref[...], 1, 1), position)
        for start in range(0, keys, BLOCK):
            off = ds_back[:, start : start + BLOCK].T
            off = jnp.concatenate([off, jnp.zeros((BLOCK, BLOCK), F32)], axis=1)
            off = pltpu.roll(off, 0, 1, stride=1, stride_axis=0).astype(BF16)
            key_block = only_head(kv_ref[start : start + BLOCK, :width], head)
            dpq_sum[start : start + 2 * BLOCK, :] += dot(off, key_block, 0, 0)
            more = dot(off, pq_ref[:, start : start + 2 * BLOCK], 1, 1)
            if head:
                more = jnp.where(
                    head_mask(more.shape, head), more, dk_pos[start : start + BLOCK, :]
                )
            dk_pos[start : start + BLOCK, :] = more
    high = position.astype(BF16)
    low = (position - high.astype(F32)).astype(BF16)
    dq = content + dot(flip, high, 1, 0) + dot(flip, low, 1, 0)
    dq_ref[...] = (scale * dq).astype(BF16)
    dkv[:, :width] = (dot(ds_all[...], q_all[...], 0, 0) + dk_pos[...]).astype(BF16)
    p_all = p_ref[...].reshape(heads * rows, keys)
    dkv[:, width:] = dot(p_all, dm_all[...], 0, 0).astype(BF16)
    x_count = len(dkv_refs)
    zl_count = keys // (rows * x_count)
    for shift, target in enumerate(dkv_refs):
        x = lax.rem(place_ref[1] + shift, x_count)
        for side in range(zl_count):
            zl = lax.rem(place_ref[2] + side, zl_count)
            start = pl.multiple_of((x * zl_count + zl) * rows, rows)
            target[side * rows : (side + 1) * rows, :] = dkv[pl.ds(start, rows), :]
    dpk_ref[...] = dot(to_all[...], qr_all[...], 0, 0).astype(BF16)
    dpq_ref[...] = (scale * dpq_sum[...]).astype(BF16)


def position_back_kernel(table_ref, dpk_ref, dpq_ref, low_ref, rows_ref):
    width = dpk_ref.shape[1]
    d_k = dot(table_ref[0], dpk_ref[...], 1, 0).astype(BF16)
    d_q = dot(table_ref[2], dpq_ref[...], 1, 0).astype(BF16)
    low_ref[:, :width] = d_q
    low_ref[:, width:] = d_k
    owners, step = rows_ref.shape[0], rows_ref.shape[1] // 2
    for owner in range(owners):
        rows_ref[owner, :step, :] = d_q[owner * step : (owner + 1) * step, :]
        rows_ref[owner, step:, :] = d_k[owner * step : (owner + 1) * step, :]


def relative_sums_kernel(unit_ref, *refs):
    out_ref = refs[-1]
    width = refs[0].shape[1] // 2
    total = None
    for pos_ref, qkv_ref in zip(refs[:-1:2], refs[1:-1:2]):
        term = dot(pos_ref[...], qkv_ref[:, : 2 * width], 1, 1)
        total = term if total is None else total + term
    column_sums(out_ref, total * unit_ref[...], total)


def picked_columns(ref, core, parts=2):
    run = ref.shape[1] // (2 * parts)
    picked = [ref[:, pl.ds(pl.multiple_of((2 * i + core) * run, run), run)] for i in range(parts)]
    return jnp.concatenate(picked, axis=1)


def scatter_kernel(own_core, names, x_first, place_ref, *refs):
    refs = list(refs)
    core = place_ref[3] if own_core else 1 - place_ref[3]
    parts = []
    for name in names:
        if name == "qkv":
            low_ref, all_ref, rel_ref, pos_ref = refs[:4]
            del refs[:4]
            value = dot(picked_columns(low_ref, core), all_ref[...], 0, 0)
            terms = dot(picked_columns(rel_ref, core), pos_ref[...], 0, 0)
            wide = pos_ref.shape[1]
            parts += [value[:, :wide] + terms, value[:, wide:]]
        elif name == "norm":
            hid = picked_columns(refs.pop(0), core)
            out = picked_columns(refs.pop(0), core)
            rel = picked_columns(refs.pop(0), core)
            rows = [hid[0:1], out[0:1], hid[1:2], out[1:2], rel[0:2]]
            rows.append(jnp.zeros((LANES - 6, hid.shape[1]), F32))
            rows = jnp.concatenate(rows, axis=0)
            parts.append(rows.T)
        elif name == "pos":
            rows_ref = refs.pop(0)
            run = rows_ref.shape[0] // 4
            picked = [rows_ref[pl.ds((2 * i + core) * run, run)] for i in range(2)]
            picked = jnp.concatenate(picked, axis=0).astype(F32)
            parts.append(picked.reshape(-1, rows_ref.shape[2]))
        else:
            left, right = refs[:2]
            del refs[:2]
            parts.append(dot(picked_columns(left, core), right[...], 0, 0))
    if not own_core:
        out_ref = refs[0]
        at = 0
        for part in parts:
            out_ref[:, at : at + part.shape[1]] = part.astype(BF16)
            at += part.shape[1]
        return
    arrived, outs, scr = refs[0], refs[1:-1], refs[-1]
    if x_first is None:
        outs = ()
    at = 0
    for part in parts:
        cols = part.shape[1]
        scr[:, at : at + cols] = (part + arrived[:, at : at + cols].astype(F32)).astype(BF16)
        at += cols
    if not outs:
        return
    count = len(outs)
    own = outs[0].shape[0] // count
    zl_count = scr.shape[0] // (own * count * 2)
    for shift, out_ref in enumerate(outs):
        near = lax.rem(place_ref[1 if x_first else 4] + shift, count)
        for far in range(count):
            x, z = (near, far) if x_first else (far, near)
            zh, zl = lax.div(z, zl_count), lax.rem(z, zl_count)
            start = pl.multiple_of(((zh * count + x) * zl_count + zl) * own, own)
            out_ref[far * own : (far + 1) * own, :] = scr[pl.ds(start, own), :]


def last_own_kernel(dims, names, ways, place_ref, *refs):
    count = 2 * len(ways)
    ins, outs, scr = refs[: -count - 1], refs[-count - 1 : -1], refs[-1]
    scatter_kernel(True, names, None, place_ref, *ins, scr)
    _, x_count, zh_count, zl_count, own = dims
    for lot, (x_first, pairing) in enumerate(ways):
        keep_ref, send_ref = outs[2 * lot : 2 * lot + 2]
        half, cols = keep_ref.shape
        xs, zs = ring_order(place_ref[1], pairing), ring_order(place_ref[4], pairing)
        for i, z in enumerate(zs):
            zh, zl = lax.div(z, zl_count), lax.rem(z, zl_count)
            for j, x in enumerate(xs):
                place = (i * x_count + j if x_first else j * len(zs) + i) * own
                target = keep_ref if place < half else send_ref
                start = pl.multiple_of(((zh * x_count + x) * zl_count + zl) * own, own)
                rows = scr[pl.ds(start, own), lot * cols : (lot + 1) * cols]
                target[place % half : place % half + own, :] = rows


def halve_kernel(count, *refs):
    for lot in range(count):
        total = refs[2 * lot][...].astype(F32) + refs[2 * lot + 1][...].astype(F32)
        keep_ref, send_ref = refs[2 * (count + lot) : 2 * (count + lot) + 2]
        half = keep_ref.shape[0]
        keep_ref[...] = total[:half].astype(BF16)
        send_ref[...] = total[half:].astype(BF16)


def middle_kernel(count, x_first, place_ref, *refs):
    pieces, outs, scr = refs[:count], refs[count:-1], refs[-1]
    total = pieces[0][...].astype(F32)
    for piece in pieces[1:]:
        total = total + piece[...].astype(F32)
    scr[...] = total.astype(BF16)
    own = outs[0].shape[0]
    for shift, out_ref in enumerate(outs):
        far = lax.rem(place_ref[4 if x_first else 1] + shift, len(outs))
        out_ref[...] = scr[pl.ds(pl.multiple_of(far * own, own), own), :]


def halves_kernel(count, *refs):
    pieces, (mine_ref, other_ref) = refs[:count], refs[count:]
    total = pieces[0][...].astype(F32)
    for piece in pieces[1:]:
        total = total + piece[...].astype(F32)
    rows = mine_ref.shape[0]
    mine_ref[...] = total[:rows, :]
    other_ref[...] = total[rows:, :].astype(BF16)


def stream_back_kernel(skip, dq_ref, mine_ref, other_ref, qkv_ref, all_ref, part_ref):
    total = mine_ref[...] + other_ref[...].astype(F32)
    both = jnp.concatenate([dq_ref[...], total.astype(BF16)], axis=1)
    all_ref[...] = both
    qkv = qkv_ref[:, skip : skip + both.shape[1]]
    part_ref[...] = dot(both, qkv, 1, 1).astype(BF16)


def total_of(refs, first, cols):
    total = refs[0][:, first : first + cols].astype(F32)
    for ref in refs[1:]:
        total = total + ref[:, first : first + cols].astype(F32)
    return total


def total_kernel(*refs):
    refs[-1][...] = total_of(refs[:-1], 0, refs[-1].shape[1])


def groups_of(counts, refs):
    return [refs[sum(counts[:i]) : sum(counts[: i + 1])] for i in range(len(counts))]


def early_end_kernel(counts, firsts, *refs):
    in_ref, out_ref = refs[-2:]
    hidden = in_ref.shape[2]
    for layer, pieces in enumerate(groups_of(counts, refs)):
        in_ref[layer] = total_of(pieces, firsts[layer], hidden)
        out_ref[layer] = total_of(pieces, firsts[layer] + hidden, hidden)


def middle_end_kernel(counts, firsts, *refs):
    attn_ref, gain_ref, bias_ref = refs[-3:]
    width = attn_ref.shape[2]
    for layer, pieces in enumerate(groups_of(counts, refs)):
        attn_ref[layer] = total_of(pieces, firsts[layer], width)
        norms = total_of(pieces, firsts[layer] + width, LANES).T
        gain_ref[layer] = norms[0:2, :]
        bias_ref[layer] = norms[2:4, :]


def late_end_kernel(qkv_at, early_at, *refs):
    lots, (qkv_ref, in_ref, out_ref) = refs[:-3], refs[-3:]
    width, hidden = qkv_ref.shape[3], in_ref.shape[2]
    totals = [
        lots[i][...].astype(F32) + lots[i + 1][...].astype(F32) for i in range(0, len(lots), 2)
    ]
    total = jnp.concatenate(totals, axis=1)
    for layer, (first, second) in enumerate(zip(qkv_at, early_at)):
        for i in range(3):
            at = first + i * width
            qkv_ref[layer, i] = total[:, at : at + width]
        in_ref[layer] = total[:, second : second + hidden]
        out_ref[layer] = total[:, second + hidden : second + 2 * hidden]


def relative_term_kernel(counts, firsts, skips, width, *refs):
    out_ref = refs[-1]
    layers = len(counts)
    total = None
    for layer, pieces in enumerate(groups_of(counts, refs)):
        qkv_ref, skip = refs[sum(counts) + layer], skips[layer]
        moved = total_of(pieces, firsts[layer], width).astype(BF16)
        step = moved.shape[0] // 2
        term = dot(moved[:step], qkv_ref[:, skip : skip + width], 1, 1)
        term = term + dot(moved[step:], qkv_ref[:, skip + width : skip + 2 * width], 1, 1)
        total = term if total is None else total + term
    out_ref[: total.shape[0], :] = total
    sums = total_of(groups_of(counts, refs)[0], firsts[0] - LANES, LANES).T
    rest = jnp.zeros((8, total.shape[1] - sums.shape[1]), F32)
    out_ref[total.shape[0] :, :] = jnp.concatenate([sums[:8], rest], axis=1)


def token_end_kernel(grad_ref, *refs):
    refs[-1][...] = (grad_ref[...] + sum_pieces(refs[:-1])).astype(BF16)


def relative_end_kernel(gain, *refs):
    pieces, (rel_ref, vec_ref, grad_ref, ends_ref) = refs[:4], refs[4:]
    total = sum_pieces(pieces)
    rows = rel_ref.shape[0]
    back, _ = normalize_back(
        rel_ref[...].astype(F32), vec_ref[gain : gain + 1, :], total[:rows]
    )
    grad_ref[...] = back
    ends_ref[...] = total[rows : rows + 8, :LANES]


def shifted(values, axes, shift):
    count = lax.axis_size(axes)
    return lax.ppermute(values, axes, [(i, (i + shift) % count) for i in range(count)])


def ctx_shifted(values):
    x_count, zl_count = lax.axis_size("x"), lax.axis_size("zl")
    shifts = ctx_shifts(x_count, zl_count)
    moved = [values[0]]
    for i in reversed(range(1, len(shifts))):
        dx, dz = shifts[i]
        pairs = []
        for x in range(x_count):
            for z in range(zl_count):
                target = (x + dx) % x_count * zl_count + (z + dz) % zl_count
                pairs.append((x * zl_count + z, target))
        moved.insert(1, lax.ppermute(values[i], CTX, pairs))
    return moved


def tp_pieces(low):
    count = lax.axis_size("tp")
    order = sorted(range(1, count), key=lambda s: -min(s, count - s))
    moved = {s: shifted(low, "tp", s) for s in order}
    return [low] + [moved[s] for s in range(1, count)]


def moved_on(pieces, axes):
    count = len(pieces)
    order = sorted(range(1, count), key=lambda s: -min(s, count - s))
    moved = {s: shifted(pieces[s], axes, s) for s in order}
    return [pieces[0]] + [moved[s] for s in range(1, count)]


def local(
    tokens,
    cotangent,
    w_qkv,
    w_attn,
    w_in,
    w_out,
    ln_gain,
    ln_bias,
    rel_emb,
    rel_gain,
    rel_bias,
    doc_ids,
    rel_bucket,
):
    _, rows, model = tokens.shape
    layers, _, own, width = w_qkv.shape
    hidden_units = w_in.shape[2]
    heads = width // HEAD_DIM
    ctx_count = lax.axis_size(CTX)
    owners = lax.axis_size(OWNERS)
    length = rows * ctx_count
    row_start = lax.axis_index(CTX) * rows
    scale = 1.0 / math.sqrt(3.0 * HEAD_DIM)
    win = length + rows
    rel_own = rel_emb.shape[0]
    buckets = rel_own * owners
    wide = 3 * width

    shape = (lax.axis_size("x"), lax.axis_size("zl"))
    x_count, z_count = lax.axis_size("x"), lax.axis_size(ZED)
    dims = (lax.axis_size("core"), x_count, lax.axis_size("zh"), lax.axis_size("zl"), own)
    plane = lax.axis_size(PLANE)
    place = [("zh", "core"), "x", "zl", "core", ZED]
    place = jnp.stack([lax.axis_index(axes) for axes in place]).astype(jnp.int32)
    dma = pltpu.SemaphoreType.DMA

    previous = []

    def run(*args, after=(), **kwargs):
        outs = call(*args, after=(*previous, *after), **kwargs)
        previous[:] = [outs[-1]]
        return outs

    attn_rows, out_rows = jnp.swapaxes(w_attn, 1, 2), jnp.swapaxes(w_out, 1, 2)
    table = [{"qkv0": wide, "attn0": width}, {"in0": hidden_units}, {"out0": hidden_units}, {}]
    for layer in range(1, layers):
        table[1]["qkv%d" % layer] = wide
        table[2]["in%d" % layer] = hidden_units
        table[3].update({"out%d" % layer: hidden_units, "attn%d" % layer: width})
    ways = [START_WAY, (True, 1), (False, 0), (False, 1)]
    sources = {"attn": attn_rows, "in": w_in, "out": out_rows}

    def listed(table, at):
        arrays, index, columns = [], [], {}
        for name, cols in table.items():
            kind, layer = name[:-1], int(name[-1])
            columns[name] = at
            at += cols
            if kind == "qkv":
                arrays += [w_qkv] * 3
                index += [(layer, i) for i in range(3)]
            else:
                arrays.append(sources[kind])
                index.append(layer)
        return arrays, index, columns, at

    one_arrays, one_index, one_at, one_cols = listed(table[0], LANES + model // 2)
    vectors = [rel_emb, ln_gain, ln_bias, rel_gain[None], rel_bias[None], doc_ids]

    found = {name: (0, at) for name, at in one_at.items()}
    arrays, other_index, sizes = list(one_arrays), [], []
    for lot in range(1, len(table)):
        more, index, columns, cols = listed(table[lot], 0)
        found.update({name: (lot, at) for name, at in columns.items()})
        arrays += more
        other_index.append(index)
        sizes.append(cols)

    def pack_start(*refs):
        pack_start_kernel(*refs[:6], one_index, other_index, *refs[6:])

    lots = run(
        pack_start,
        [((own, cols), BF16) for cols in sizes + [one_cols]],
        vectors + arrays,
        hbm=range(len(vectors) + len(arrays)),
        scratch=[
            pltpu.VMEM((LANES, LANES), F32),
            pltpu.VMEM(ln_gain.shape, BF16),
            pltpu.VMEM(ln_bias.shape, BF16),
            pltpu.VMEM((1, own), BF16),
            pltpu.VMEM((1, own), BF16),
            pltpu.VMEM((1, rows), jnp.int32),
            dma((7 + len(arrays),)),
        ],
        name="pack_start",
    )
    lots = [lots[-1], *lots[:-1]]

    padded = jnp.pad(rel_bucket, (1, 1), mode="edge")
    to_index = lax.dynamic_slice_in_dim(padded, row_start, win, 0)
    from_index = lax.dynamic_slice_in_dim(padded, length - rows - row_start + 1, win, 0)
    index = jnp.stack([to_index[::-1], from_index[::-1], from_index])
    (tables,) = run(table_kernel, [((3, buckets, win), BF16)], [index], limit=8, name="tables")

    even, odd = [(0, 1), (1, 0), (2, 3), (3, 2)], [(1, 2), (2, 1), (3, 0), (0, 3)]
    for step in range(4):
        moved = []
        for lot, (x_first, pairing) in zip(lots, ways):
            axes = "x" if x_first == (step < 2) else ZED
            moved.append(lax.ppermute(lot, axes, odd if pairing ^ (step % 2) else even))
        both = [piece for pair in zip(lots, moved) for piece in pair]
        shapes = [((2 * lot.shape[0], lot.shape[1]), BF16) for lot in lots]
        lots = list(run(stack_kernel, shapes, both, limit=16, name="stack"))
    for i in range(4):
        lots[i] = [lots[i], shifted(lots[i], "core", 1)]
    one_pieces = lots[0]
    qkv, attn, small, q, key_value = run(
        functools.partial(start_kernel, dims, scale, [one_at["qkv0"], one_at["attn0"], 0]),
        [
            ((model, wide), BF16),
            ((model, width), BF16),
            ((model, LANES), BF16),
            ((rows, width), BF16),
            ((rows, 2 * width), BF16),
        ],
        [place, tokens[0], *one_pieces],
        smem=(0,),
        anys=range(2, 2 + len(one_pieces)),
        hbm=(1,),
        scratch=[pltpu.VMEM((rows, model), BF16), dma((3 * owners + 1,))],
        name="start",
    )
    rel_low, rel_unit, vecs, doc_j = run(
        functools.partial(relative_kernel, dims, layers),
        [
            ((buckets, model), BF16),
            ((buckets, model), F32),
            ((16, model), F32),
            ((1, length), F32),
        ],
        [place, small, *one_pieces],
        smem=(0,),
        anys=range(2, 2 + len(one_pieces)),
        limit=16,
        scratch=[pltpu.VMEM((buckets, model), BF16), dma((2 * owners,))],
        name="relative",
    )

    def rest(names):
        lot = found[names[0]][0]
        return run(
            functools.partial(rest_kernel, dims, ways[lot], [found[name][1] for name in names]),
            [((model, table[lot][name]), BF16) for name in names],
            [place, *lots[lot]],
            smem=(0,),
            anys=(1, 2),
            scratch=[dma((len(names) * owners,))],
            name="rest",
        )

    qkvs, attns, ins, outs = [qkv], [attn], [], []

    token_low = tokens[0]
    stream = token_low
    kept = []
    hidden, pieces = None, None
    tile = (rows, model)
    for layer in range(layers):
        if layer:
            pre_out, stream, stream_low, q, key_value = run(
                functools.partial(
                    project_kernel,
                    scale,
                    (2 * layer - 1, 2 * layers + 2 * layer - 1),
                    0,
                ),
                [
                    (tile, F32),
                    (tile, F32),
                    (tile, BF16),
                    ((rows, width), BF16),
                    ((rows, 2 * width), BF16),
                ],
                [hidden, *pieces, vecs, qkvs[layer]],
                name="project",
            )
            kept[-1]["pre_out"] = pre_out
        else:
            stream_low = token_low
        blocks = ctx_shifted([key_value] * ctx_count)
        pk, pq_rev, pq = run(
            functools.partial(position_kernel, scale, 0),
            [((width, win), BF16)] * 3,
            [rel_low, qkvs[layer], tables],
            name="position",
        )
        (kv,) = run(
            functools.partial(gather_kernel, shape),
            [((length, 2 * width), BF16)],
            [place, *blocks],
            smem=(0,),
            anys=range(1, 1 + ctx_count),
            scratch=[dma((ctx_count,))],
            name="gather",
        )
        mixture, p = run(
            attention_kernel,
            [((rows, width), BF16), ((heads, rows, length), BF16)],
            [q, kv, pk, pq_rev, doc_ids, doc_j],
            scratch=[
                pltpu.VMEM((heads, rows, length), F32),
                pltpu.VMEM((heads, rows, width), BF16),
            ],
            limit=16,
            name="attention",
        )
        (part,) = run(
            functools.partial(attended_kernel, 0),
            [(tile, BF16)],
            [mixture, attns[layer]],
            name="attended",
        )
        pieces = tp_pieces(part)
        ins += rest(["in%d" % layer])
        outs += rest(["out%d" % layer])
        pre_hidden, hidden, hidden_low, slope, active, part = run(
            functools.partial(feed_kernel, (2 * layer, 2 * layers + 2 * layer)),
            [
                (tile, F32),
                (tile, F32),
                (tile, BF16),
                ((rows, hidden_units), F32),
                ((rows, hidden_units), BF16),
                (tile, BF16),
            ],
            [stream, *pieces, vecs, ins[layer], outs[layer]],
            name="feed",
        )
        pieces = tp_pieces(part)
        if layer + 1 < layers:
            qkvs += rest(["qkv%d" % (layer + 1)])
            attns += rest(["attn%d" % (layer + 1)])
        kept.append(
            dict(
                stream_low=stream_low,
                q=q,
                kv=kv,
                pk=pk,
                pq=pq,
                p=p,
                mixture=mixture,
                pre_hidden=pre_hidden,
                hidden_low=hidden_low,
                slope=slope,
                active=active,
            )
        )
    last = layers - 1
    turned = run(
        functools.partial(turn_kernel, (2 * last + 1, 2 * layers + 2 * last + 1)),
        [
            (tile, BF16),
            (tile, F32),
            (tile, BF16),
            ((rows, hidden_units), BF16),
            (tile, BF16),
            ((8, model), F32),
        ],
        [hidden, *pieces, vecs, kept[-1]["slope"], ins[-1], outs[-1], cotangent[0]],
        hbm=(9,),
        scratch=[pltpu.VMEM((rows, model), BF16), dma],
        name="turn",
    )
    out_local = turned[0]

    grad_parts = None
    x_count = lax.axis_size("x")

    def scatter_other(names, ins, cols, label):
        (other,) = run(
            functools.partial(scatter_kernel, False, names, False),
            [((model // 2, cols), BF16)],
            [place, *ins],
            smem=(0,),
            limit=30,
            name=label + "_other",
        )
        return shifted(other, "core", 1)

    def scatter_own(names, ins, arrived, label, x_first=False, after=()):
        half, cols = arrived.shape
        pieces = run(
            functools.partial(scatter_kernel, True, names, x_first),
            [((half // z_count, cols), BF16)] * z_count,
            [place, *ins, arrived],
            smem=(0,),
            scratch=[pltpu.VMEM((half, cols), BF16)],
            after=after,
            limit=16,
            name=label + "_own",
        )
        return moved_on(pieces, "x" if x_first else ZED)

    def scatter_middle(pieces, label, x_first=False):
        rows_here, cols = pieces[0].shape
        pieces = run(
            functools.partial(middle_kernel, len(pieces), x_first),
            [((rows_here // x_count, cols), BF16)] * x_count,
            [place, *pieces],
            smem=(0,),
            scratch=[pltpu.VMEM((rows_here, cols), BF16)],
            name=label + "_middle",
        )
        return moved_on(pieces, ZED if x_first else "x")

    def scatter_total(pieces, label):
        return list(run(total_kernel, [(pieces[0].shape, F32)], pieces, name=label + "_total"))

    early_names, early_cols = ("in", "out"), 2 * hidden_units
    middle_names, middle_cols = ("attn", "norm", "pos"), 2 * width + LANES
    early_ins, middle_ins, late_ins, pos_lows = [], [], [], []
    for layer in reversed(range(layers)):
        k = kept[layer]
        if grad_parts is None:
            d_pre_out, d_out_low, d_inner, part, norm_out = turned[1:]
        else:
            d_pre_out, d_out_low, d_inner, part, norm_out = run(
                functools.partial(feed_back_kernel, 2 * layer + 1),
                [
                    (tile, F32),
                    (tile, BF16),
                    ((rows, hidden_units), BF16),
                    (tile, BF16),
                    ((8, model), F32),
                ],
                [*grad_parts, k["pre_out"], vecs, k["slope"], ins[layer], outs[layer]],
                name="feed_back",
            )
        pieces = tp_pieces(part)
        early_in = [k["hidden_low"], d_inner, d_out_low, k["active"]]
        early_ins += early_in
        backs = run(
            functools.partial(attention_back_kernel, 2 * layer, 0, scale),
            [
                (tile, F32),
                (tile, BF16),
                ((rows, width), BF16),
                ((win, width), BF16),
                ((win, width), BF16),
                ((8, model), F32),
            ]
            + [((length // x_count, 2 * width), BF16)] * x_count,
            [place, *pieces, d_pre_out, k["pre_hidden"], vecs, attns[layer]]
            + [k["q"], k["kv"], k["pk"], k["pq"], k["p"]],
            smem=(0,),
            scratch=[
                pltpu.VMEM((heads * rows, length), BF16),
                pltpu.VMEM((heads * rows, win), BF16),
                pltpu.VMEM((length, width), F32),
                pltpu.VMEM((heads * rows, width), BF16),
                pltpu.VMEM((heads * rows, width), BF16),
                pltpu.VMEM((heads * rows, width), BF16),
                pltpu.VMEM((win, width), F32),
                pltpu.VMEM((length, 2 * width), BF16),
            ],
            limit=20,
            name="attention_back",
        )
        d_pre_hidden, d_attended, dq, dpk, dpq, norm_hidden = backs[:6]
        dkv = moved_on(backs[6:], "x")
        pos_low, pos_rows = run(
            position_back_kernel,
            [((buckets, 2 * width), BF16), ((owners, 2 * rel_own, width), BF16)],
            [tables, dpk, dpq],
            name="position_back",
        )
        pos_lows.append(pos_low)
        norm_rel = jnp.zeros((8, model), F32)
        if not layer:
            pairs = [item for pair in zip(pos_lows, qkvs[::-1]) for item in pair]
            (norm_rel,) = run(
                relative_sums_kernel,
                [((8, model), F32)],
                [rel_unit, *pairs],
                limit=16,
                name="relative_sums",
            )
        middle_ins += [d_attended, k["mixture"], norm_hidden, norm_out, norm_rel, pos_rows]
        if not layer:
            arrived = scatter_other(
                middle_names * layers, middle_ins, middle_cols * layers, "middle"
            )
        if not layer:
            middle = scatter_own(middle_names * layers, middle_ins, arrived, "middle")
        mine, other = run(
            functools.partial(halves_kernel, x_count),
            [((rows, 2 * width), F32), ((rows, 2 * width), BF16)],
            dkv,
            name="halves",
        )
        other = shifted(other, "zl", 1)
        if not layer:
            middle = scatter_middle(middle, "middle")
        dqkv, part = run(
            functools.partial(stream_back_kernel, 0),
            [((rows, wide), BF16), (tile, BF16)],
            [dq, mine, other, qkvs[layer]],
            name="stream_back",
        )
        grad_parts = [d_pre_hidden] + tp_pieces(part)
        late_ins += [k["stream_low"], dqkv, rel_low, pos_low]
    late_names, late_cols = ("qkv",) * layers, wide * layers
    late_names, late_cols = late_names + early_names * layers, late_cols + early_cols * layers
    late_ins += early_ins
    arrived = scatter_other(late_names, late_ins, late_cols, "late")
    middle_at = [(layers - 1 - layer) * middle_cols for layer in range(layers)]
    late_at = [(layers - 1 - layer) * wide for layer in range(layers)]

    counts = [len(middle)] * layers
    (term,) = run(
        functools.partial(
            relative_term_kernel,
            counts,
            [at + width + LANES for at in middle_at],
            [0] * layers,
            width,
        ),
        [((rel_own + 8, model), F32)],
        middle * layers + qkvs,
        name="relative_term",
    )
    terms = tp_pieces(term)
    half, lot_cols = model // 2, late_cols // len(ways)
    parts = run(
        functools.partial(last_own_kernel, dims, late_names, ways),
        [((half // 2, lot_cols), BF16)] * (2 * len(ways)),
        [place, *late_ins, arrived],
        smem=(0,),
        scratch=[pltpu.VMEM((half, late_cols), BF16)],
        limit=30,
        name="late_own",
    )

    def sent(parts, step):
        moved = []
        for lot, (x_first, pairing) in enumerate(ways):
            axes = "x" if x_first == (step < 2) else ZED
            pairs = odd if pairing ^ (step % 2) else even
            moved += [parts[2 * lot], lax.ppermute(parts[2 * lot + 1], axes, pairs)]
        return moved

    def halved(parts):
        rows_here = parts[0].shape[0] // 2
        return run(
            functools.partial(halve_kernel, len(ways)),
            [((rows_here, lot_cols), BF16)] * (2 * len(ways)),
            parts,
            name="halve",
        )

    parts = halved(sent(parts, 3))
    parts = sent(parts, 2)
    (grad_tokens,) = run(token_end_kernel, [(tile, BF16)], grad_parts, name="token_end")
    parts = halved(parts)
    parts = sent(parts, 1)
    parts = sent(halved(parts), 0)
    grad_rel, ends = run(
        functools.partial(relative_end_kernel, 4 * layers),
        [((rel_own, model), F32), ((8, LANES), F32)],
        [*terms, rel_emb, vecs],
        name="relative_end",
    )
    grad_attn, grad_gain, grad_bias = run(
        functools.partial(middle_end_kernel, counts, middle_at),
        [((layers, own, width), F32), ((layers, 2, own), F32), ((layers, 2, own), F32)],
        middle * layers,
        name="middle_end",
    )
    grad_qkv, grad_in, grad_out = run(
        functools.partial(
            late_end_kernel,
            late_at,
            [wide * layers + (layers - 1 - layer) * early_cols for layer in range(layers)],
        ),
        [
            ((layers, 3, own, width), F32),
            ((layers, own, hidden_units), F32),
            ((layers, own, hidden_units), F32),
        ],
        parts,
        name="late_end",
    )
    grad_attn, grad_out = jnp.swapaxes(grad_attn, 1, 2), jnp.swapaxes(grad_out, 1, 2)
    return (
        out_local[None],
        grad_tokens[None],
        grad_qkv,
        grad_attn,
        grad_in,
        grad_out,
        grad_gain,
        grad_bias,
        grad_rel,
        ends[4, :own],
        ends[5, :own],
    )


def solution(mesh):
    sizes = mesh.shape
    zh, zl = 2, 2
    finer = Mesh(
        mesh.devices.reshape(zh, sizes["fsdp"] // zh, sizes["ctx"] // zl, zl, sizes["tp"]),
        ("zh", "core", "x", "zl", "tp"),
    )
    own = OWNERS
    fsdp = ("zh", "core")
    return jax.shard_map(
        local,
        mesh=finer,
        in_specs=(
            P(fsdp, CTX, None),
            P(fsdp, CTX, None),
            P(None, None, own, "tp"),
            P(None, "tp", own),
            P(None, own, "tp"),
            P(None, "tp", own),
            P(None, None, own),
            P(None, None, own),
            P(own, None),
            P(own),
            P(own),
            P(fsdp, CTX),
            P(),
        ),
        out_specs=(
            P(fsdp, CTX, None),
            P(fsdp, CTX, None),
            P(None, None, own, "tp"),
            P(None, "tp", own),
            P(None, own, "tp"),
            P(None, "tp", own),
            P(None, None, own),
            P(None, None, own),
            P(own, None),
            P(own),
            P(own),
        ),
        check_vma=False,
    )
```
